128 devices in a mesh: loop: 4 (over y_lo, core), wide: 32 (over y_hi, x, z).
Axes of the slice: x: 4, y: 4 (y_hi: 2, y_lo: 2; y = y_hi * 2 + y_lo), z: 4, core: 2. Of those that a mesh axis runs over, the one named last changes fastest.
Arguments:
- features: float32 [128, 65536], P(None, 'wide'), may hold values from -6 to 6
- weight: float32 [128, 128], replicated, may hold values from -0.5 to 0.5
- cotangent: float32 [128, 65536], P(None, 'wide'), may hold values from -6 to 6
- tiles: float32 [4, 32, 256, 128, 128], P('loop', 'wide'), may hold values from 0 to 0.001953125
- tile_rows: int32 [4, 32, 256], P('loop', 'wide'), may hold values from 0 to 15
- tile_cols: int32 [4, 32, 256], P('loop', 'wide'), may hold values from 0 to 127
- counts: int32 [4, 32], P('loop', 'wide'), may hold values from 64 to 256, as said below
Outputs:
- activated: float32 [128, 65536], P(None, 'wide')
- input_grad: float32 [128, 65536], P(None, 'wide')
- weight_grad: float32 [128, 128], replicated
The draws below stay inside these ranges and needn't reach their ends.
Inputs may be any that keep to these rules, and one draw needn't show every extreme that they name: `counts`: each count is 256 / 4 times a power of two; one panel holds exactly 256 live tiles; slots at or past a panel's count are ignored.
All inputs are finite; a program needn't handle non-finite values.
Results may differ from the reference program's by a relative error of at most 0.0003.
Values sent between devices are 32-bit elements; how exact they have to be, the bound alone decides.
No kernel may reach another device: no remote copies, remote signals or barrier semaphores. Data moves between devices by JAX's collectives and lax.ppermute only.
A program may use at most 192 MiB of HBM per device.

```python
import jax
import jax.numpy as jnp
from jax import lax

F = 128
TILE = 128
NW = 2048
MAXT = 256
RB = 16
CG = 128
NODES = 65536
N_LOOP = 4
N_WIDE = 32


def draw_counts(key, part):
    key = jax.random.fold_in(key, 7)
    first, second = jax.random.split(key)
    powers = jax.random.randint(first, (N_LOOP * N_WIDE,), 0, 3)
    values = MAXT // 4 * jnp.left_shift(jnp.ones_like(powers), powers)
    chosen = jax.random.randint(second, (), 0, N_LOOP * N_WIDE)
    flat = jnp.where(jnp.arange(N_LOOP * N_WIDE) == chosen, MAXT, values)
    return flat.reshape(N_LOOP, N_WIDE).astype(jnp.int32)


def plant(values, rng, least, top_value):
    longest = values.shape.index(max(values.shape))
    spots = []
    for shift in (0, 1):
        where = [jax.random.randint(jax.random.fold_in(rng, axis), (), 0, length) for axis, length in enumerate(values.shape)]
        where[longest] = (where[longest] + shift) % values.shape[longest]
        spots.append(tuple(where))
    return values.at[spots[0]].set(least).at[spots[1]].set(top_value)


def block_scale(own_key, shape, cuts, smallest, largest):
    def one(position, parts):
        heights = jax.random.uniform(jax.random.fold_in(jax.random.fold_in(own_key, 6), position), (parts,), jnp.float32, smallest / len(cuts), largest / len(cuts))
        return jnp.repeat(jnp.exp(heights), shape[position] // parts).reshape((-1,) + (1,) * (len(shape) - position - 1))

    level = one(*cuts[0])
    for cut in cuts[1:]:
        level = level * one(*cut)
    return level


def bell_draw(own_key, dims, width, limit, cuts=(), kind=jnp.bfloat16):
    factor_of = block_scale(own_key, dims, cuts, -0.22, 0.18) if cuts else 1.0
    array = jax.random.normal(own_key, dims, jnp.float32) * width * factor_of
    return jnp.minimum(jnp.maximum(array, -limit), limit).astype(kind)


def setup_inputs(seed: int = 0) -> dict:
    key_of = jax.random.split(jax.random.key(seed), 8)
    return {
        "features": bell_draw(key_of[0], (F, NODES), 1.0, 6.0, ((1, 32),), jnp.float32),
        "weight": bell_draw(key_of[1], (F, F), F ** -0.5, 0.5, (), jnp.float32),
        "cotangent": bell_draw(key_of[2], (F, NODES), 1.0, 6.0, ((1, 32),), jnp.float32),
        "tiles": jnp.clip(0.001953125 * jax.random.uniform(key_of[3], (N_LOOP, N_WIDE, MAXT, TILE, TILE), jnp.float32) ** block_scale(key_of[3], (N_LOOP, N_WIDE, MAXT, TILE, TILE), ((0, 4), (1, 32)), -0.2, 0.2), 0.0, 0.001953125),
        "tile_rows": plant(jax.random.randint(key_of[4], (N_LOOP, N_WIDE, MAXT), 0, RB), jax.random.fold_in(key_of[4], 1), 0, RB - 1).astype(jnp.int32),
        "tile_cols": plant(jax.random.randint(key_of[5], (N_LOOP, N_WIDE, MAXT), 0, CG), jax.random.fold_in(key_of[5], 1), 0, CG - 1).astype(jnp.int32),
        "counts": draw_counts(jax.random.fold_in(key_of[7], 71), 0),
    }


HI = lax.Precision.HIGHEST

def panel_forward(group3, tile_collection, rows, cols, entry_count):
    taken = jnp.take(group3, cols, axis=1)
    part = jnp.einsum('fbc,brc->bfr', taken, tile_collection, precision=HI)
    live = jnp.arange(MAXT, dtype=jnp.int32) < entry_count
    onehot = ((rows[:, None] == jnp.arange(RB, dtype=jnp.int32)[None, :]) & live[:, None]).astype(jnp.float32)
    return jnp.einsum('bn,bfr->fnr', onehot, part, precision=HI)

def panel_backward(slope3, tile_collection, rows, cols, entry_count):
    taken = jnp.take(slope3, rows, axis=1)
    part = jnp.einsum('fbr,brc->bfc', taken, tile_collection, precision=HI)
    live = jnp.arange(MAXT, dtype=jnp.int32) < entry_count
    onehot = ((cols[:, None] == jnp.arange(CG, dtype=jnp.int32)[None, :]) & live[:, None]).astype(jnp.float32)
    return jnp.einsum('bn,bfc->fnc', onehot, part, precision=HI)

def reference(features, weight, cotangent, tiles, tile_rows, tile_cols, counts):
    quarter = NW // N_LOOP
    projected = jnp.dot(weight.T, features, precision=HI, preferred_element_type=jnp.float32)
    groups = projected.reshape(F, N_WIDE, N_LOOP, quarter)

    def forward_block(block_entry):
        block_tiles = lax.dynamic_index_in_dim(tiles, block_entry, 1, keepdims=False)
        block_rows = lax.dynamic_index_in_dim(tile_rows, block_entry, 1, keepdims=False)
        block_cols = lax.dynamic_index_in_dim(tile_cols, block_entry, 1, keepdims=False)
        block_counts = lax.dynamic_index_in_dim(counts, block_entry, 1, keepdims=False)
        total = jnp.zeros((F, RB, TILE), jnp.float32)
        for group in range(N_LOOP):
            group3 = groups[:, :, group, :].reshape(F, CG, TILE)
            total = total + panel_forward(group3, block_tiles[group], block_rows[group], block_cols[group], block_counts[group])
        return total
    blocks = lax.map(forward_block, jnp.arange(N_WIDE, dtype=jnp.int32))
    aggregated = jnp.transpose(blocks, (1, 0, 2, 3)).reshape(F, NODES)
    activated, pull = jax.vjp(jax.nn.gelu, aggregated)
    slope = pull(cotangent)[0]
    slope4 = slope.reshape(F, N_WIDE, RB, TILE)

    def backward_block(carry, block_entry):
        block_tiles = lax.dynamic_index_in_dim(tiles, block_entry, 1, keepdims=False)
        block_rows = lax.dynamic_index_in_dim(tile_rows, block_entry, 1, keepdims=False)
        block_cols = lax.dynamic_index_in_dim(tile_cols, block_entry, 1, keepdims=False)
        block_counts = lax.dynamic_index_in_dim(counts, block_entry, 1, keepdims=False)
        slope3 = lax.dynamic_index_in_dim(slope4, block_entry, 1, keepdims=False)
        terms = []
        for group in range(N_LOOP):
            terms.append(panel_backward(slope3, block_tiles[group], block_rows[group], block_cols[group], block_counts[group]))
        return (carry + jnp.stack(terms), None)
    start = jnp.zeros((N_LOOP, F, CG, TILE), jnp.float32)
    summed, unused = lax.scan(backward_block, start, jnp.arange(N_WIDE, dtype=jnp.int32))
    grad_proj = jnp.transpose(summed.reshape(N_LOOP, F, N_WIDE, quarter), (1, 2, 0, 3)).reshape(F, NODES)
    weight_grad = jnp.dot(features, grad_proj.T, precision=HI, preferred_element_type=jnp.float32)
    input_grad = jnp.dot(weight, grad_proj, precision=HI, preferred_element_type=jnp.float32)
    return (activated, input_grad, weight_grad)
```

```python
import jax
import jax.numpy as jnp
from jax import lax
from jax.experimental import pallas as pl
from jax.experimental.pallas import tpu as pltpu
from jax.sharding import PartitionSpec as P

HI = lax.Precision.HIGHEST
AXES = ("loop", "wide")
SIDE = 4
TILE = 128
SLOTS = 256
CHUNK = 32
BUFFERS = 16
PER = 8
VMEM_BYTES = 56 * 1024 * 1024


def device_index(y, core, x, z):
    y, x, z = y % SIDE, x % SIDE, z % SIDE
    return (((y & 1) * 2 + core) * 2 + (y >> 1)) * 16 + x * SIDE + z


def permute(value, move):
    pairs = []
    for y in range(SIDE):
        for core in range(2):
            for x in range(SIDE):
                for z in range(SIDE):
                    pairs.append((device_index(y, core, x, z), device_index(*move(y, core, x, z))))
    return lax.ppermute(value, AXES, pairs)


def x_up(y, core, x, z):
    return (y, core, x + 1, z)


def x_down(y, core, x, z):
    return (y, core, x - 1, z)


def z_up(y, core, x, z):
    return (y, core, x, z + 1)


def z_down(y, core, x, z):
    return (y, core, x, z - 1)


def y_partner(y, core, x, z):
    return (3 - y, core, x, z)


def y_pair(y, core, x, z):
    return (y ^ 1, core, x, z)


def y_far(y, core, x, z):
    return (y + 2, core, x, z)


def core_swap(y, core, x, z):
    return (y, 1 - core, x, z)


def flip(y, core, x, z, axis, step):
    return (y, core, x ^ step, z) if axis == "x" else (y, core, x, z ^ step)


def ring_gather_near(value, up, down):
    one = permute(value, down)
    three = permute(value, up)
    two = permute(one, down)
    return [value, one, two, three]


def ring_gather_far(value, up, down):
    one = permute(value, down)
    three = permute(value, up)
    two = permute(three, up)
    return [value, one, two, three]


def ring_reduce_near(parts, up, down):
    moved = permute(parts[2], up)
    three = permute(parts[3], down)
    one = permute(parts[1] + moved, up)
    return parts[0] + one + three


def ring_reduce_far(parts, up, down):
    moved = permute(parts[2], down)
    one = permute(parts[1], up)
    three = permute(parts[3] + moved, down)
    return parts[0] + one + three


def split_high_low(value):
    high = value.astype(jnp.bfloat16)
    low = (value - high.astype(jnp.float32)).astype(jnp.bfloat16)
    return high, low


def tile_copy(tiles_ref, held, sems, chunk):
    part = pl.ds(chunk * CHUNK, CHUNK)
    return pltpu.make_async_copy(tiles_ref.at[part], held.at[part], sems.at[chunk])


def forward_kernel(count_ref, rows_ref, slots_ref, tiles_ref, *rest):
    buffers = rest[:BUFFERS]
    out_ref, held, group, pairs, tile_sems, group_sems = rest[BUFFERS:]
    count = count_ref[0]
    copies = []
    for index in range(BUFFERS):
        copy = pltpu.make_async_copy(
            buffers[index], group.at[pl.ds(index * PER, PER)], group_sems.at[index]
        )
        copy.start()
        copies.append(copy)
    for chunk in range(SLOTS // CHUNK):

        @pl.when(chunk * CHUNK < count)
        def _():
            tile_copy(tiles_ref, held, tile_sems, chunk).start()

    out_ref[...] = jnp.zeros_like(out_ref)
    for index in range(BUFFERS):
        copies[index].wait()

        @pl.loop(index * PER, (index + 1) * PER)
        def _(slot):
            high, low = split_high_low(group[slot])
            pairs[slot, :, :TILE] = high
            pairs[slot, :, TILE:] = low

    for chunk in range(SLOTS // CHUNK):

        @pl.when(chunk * CHUNK < count)
        def _():
            tile_copy(tiles_ref, held, tile_sems, chunk).wait()

            @pl.loop(chunk * CHUNK, (chunk + 1) * CHUNK, unroll=4)
            def _(t):
                high, low = split_high_low(held[t])
                right = pairs[slots_ref[t]]
                product = jnp.dot(
                    jnp.concatenate([high, low], axis=1),
                    jnp.concatenate([right, right], axis=0),
                    preferred_element_type=jnp.float32,
                )
                out_ref[rows_ref[t]] += product[:, :TILE] + product[:, TILE:]


def backward_kernel(count_ref, rows_ref, slots_ref, tiles_ref, slope_ref, *rest):
    buffers = rest[:BUFFERS]
    held, total, pairs, tile_sems, out_sems = rest[BUFFERS:]
    count = count_ref[0]
    for chunk in range(SLOTS // CHUNK):

        @pl.when(chunk * CHUNK < count)
        def _():
            tile_copy(tiles_ref, held, tile_sems, chunk).start()

    for row in range(pairs.shape[0]):
        high, low = split_high_low(slope_ref[:, row * TILE : (row + 1) * TILE])
        pairs[row, :, :TILE] = high
        pairs[row, :, TILE:] = low

    @pl.loop(0, BUFFERS * PER)
    def _(slot):
        total[slot] = jnp.zeros((TILE, TILE), jnp.float32)

    for chunk in range(SLOTS // CHUNK):

        @pl.when(chunk * CHUNK < count)
        def _():
            tile_copy(tiles_ref, held, tile_sems, chunk).wait()

            @pl.loop(chunk * CHUNK, (chunk + 1) * CHUNK, unroll=4)
            def _(t):
                high, low = split_high_low(held[t])
                right = jnp.concatenate([high, low], axis=1)
                product = jnp.dot(
                    pairs[rows_ref[t]],
                    jnp.concatenate([right, right], axis=0),
                    preferred_element_type=jnp.float32,
                )
                total[slots_ref[t]] += product[:, :TILE] + product[:, TILE:]

    copies = []
    for index in range(BUFFERS):
        copy = pltpu.make_async_copy(
            total.at[pl.ds(index * PER, PER)], buffers[index], out_sems.at[index]
        )
        copy.start()
        copies.append(copy)
    for copy in copies:
        copy.wait()


def smem():
    return pl.BlockSpec(memory_space=pltpu.SMEM)


def vmem():
    return pl.BlockSpec(memory_space=pltpu.VMEM)


def anywhere():
    return pl.BlockSpec(memory_space=pl.ANY)


def forward_part(count, rows, slots, tiles, buffers, nrow):
    return pl.pallas_call(
        forward_kernel,
        name="forward_tiles",
        out_shape=jax.ShapeDtypeStruct((nrow, TILE, TILE), jnp.float32),
        in_specs=[smem(), smem(), smem(), anywhere()] + [anywhere()] * BUFFERS,
        out_specs=vmem(),
        scratch_shapes=[
            pltpu.VMEM((SLOTS, TILE, TILE), jnp.float32),
            pltpu.VMEM((BUFFERS * PER, TILE, TILE), jnp.float32),
            pltpu.VMEM((BUFFERS * PER, TILE, 2 * TILE), jnp.bfloat16),
            pltpu.SemaphoreType.DMA((SLOTS // CHUNK,)),
            pltpu.SemaphoreType.DMA((BUFFERS,)),
        ],
        compiler_params=pltpu.CompilerParams(vmem_limit_bytes=VMEM_BYTES),
    )(count, rows, slots, tiles, *buffers)


def backward_part(count, rows, slots, tiles, slope):
    return pl.pallas_call(
        backward_kernel,
        name="backward_tiles",
        out_shape=[jax.ShapeDtypeStruct((PER, TILE, TILE), jnp.float32)] * BUFFERS,
        in_specs=[smem(), smem(), smem(), anywhere(), vmem()],
        out_specs=[anywhere()] * BUFFERS,
        scratch_shapes=[
            pltpu.VMEM((SLOTS, TILE, TILE), jnp.float32),
            pltpu.VMEM((BUFFERS * PER, TILE, TILE), jnp.float32),
            pltpu.VMEM((slope.shape[1] // TILE, TILE, 2 * TILE), jnp.bfloat16),
            pltpu.SemaphoreType.DMA((SLOTS // CHUNK,)),
            pltpu.SemaphoreType.DMA((BUFFERS,)),
        ],
        compiler_params=pltpu.CompilerParams(vmem_limit_bytes=VMEM_BYTES),
    )(count, rows, slots, tiles, slope)


def relative_slots(cols, wide):
    node_block = cols // 4
    part = cols % 4
    across = (node_block // 16) ^ (wide // 16)
    dx = (node_block // 4 - wide // 4) % 4
    dz = (node_block - wide) % 4
    first = (across * 4 + dz) * PER + dx * 2 + part
    second = (8 + across * 4 + dx) * PER + dz * 2 + part - 2
    return jnp.where(part < 2, first, second)


def gather_features(features, loop):
    feats, shard_nodes = features.shape
    split = features.reshape(feats, 4, 4, TILE)

    def quarter(index):
        piece = lax.dynamic_index_in_dim(split, index, 1, keepdims=False)
        return jnp.transpose(piece, (1, 2, 0))

    partner = permute(quarter(loop ^ 2), y_partner)
    own = quarter(loop)
    buffers = []
    halves = []
    for piece, gather in ((own, ring_gather_near), (partner, ring_gather_far)):
        row = gather(piece[:2], x_up, x_down)
        column = gather(piece[2:], z_up, z_down)
        halves.append((row, column, gather))
    for which in range(2):
        for row, column, gather in halves:
            if which == 0:
                buffers += gather(jnp.concatenate(row, axis=0), z_up, z_down)
            else:
                buffers += gather(jnp.concatenate(column, axis=0), x_up, x_down)
    return buffers


def scatter_terms(buffers):
    sums = []
    for across, reduce in ((0, ring_reduce_near), (1, ring_reduce_far)):
        row = reduce(buffers[across * 4 : across * 4 + 4], z_up, z_down)
        column = reduce(buffers[8 + across * 4 : 12 + across * 4], x_up, x_down)
        first = reduce([row[2 * i : 2 * i + 2] for i in range(4)], x_up, x_down)
        second = reduce([column[2 * i : 2 * i + 2] for i in range(4)], z_up, z_down)
        sums.append(jnp.concatenate([first, second], axis=0))
    return sums[0] + permute(sums[1], y_far)


def sum_over_loop(partial, loop):
    core = loop % 2
    half = partial.shape[0] // 2
    kept = lax.dynamic_slice_in_dim(partial, core * half, half, 0)
    given = lax.dynamic_slice_in_dim(partial, (1 - core) * half, half, 0)
    kept = kept + permute(given, core_swap)
    kept = kept + permute(kept, y_pair)
    other = permute(kept, core_swap)
    return jnp.where(
        core == 0,
        jnp.concatenate([kept, other], axis=0),
        jnp.concatenate([other, kept], axis=0),
    )


def sum_over_wide(value):
    for axis in ("x", "z"):
        for step in (1, 2):
            value = value + permute(value, lambda y, c, x, z: flip(y, c, x, z, axis, step))
    return value + permute(value, y_far)


def gather_loop(own, loop):
    low, core = loop // 2, loop % 2
    across = permute(own, y_pair)
    own_other = permute(own, core_swap)
    across_other = permute(across, core_swap)
    same = jnp.where(
        core == 0, jnp.stack([own, own_other]), jnp.stack([own_other, own])
    )
    far = jnp.where(
        core == 0, jnp.stack([across, across_other]), jnp.stack([across_other, across])
    )
    whole = jnp.where(low == 0, jnp.stack([same, far]), jnp.stack([far, same]))
    feats = own.shape[1]
    return jnp.transpose(whole.reshape(-1, feats, TILE), (1, 0, 2)).reshape(feats, -1)


def per_device(features, weight, cotangent, tiles, tile_rows, tile_cols, counts):
    feats, shard_nodes = features.shape
    loop = lax.axis_index("loop")
    wide = lax.axis_index("wide")
    nrow = shard_nodes // TILE
    tile_collection = tiles.reshape(SLOTS, TILE, TILE)
    rows = tile_rows.reshape(SLOTS)
    slots = relative_slots(tile_cols.reshape(SLOTS), wide)
    count = counts.reshape(1)

    buffers = gather_features(features, loop)
    partial = forward_part(count, rows, slots, tile_collection, buffers, nrow)
    gathered = sum_over_loop(partial, loop).reshape(shard_nodes, feats)
    aggregated = lax.dot_general(
        weight, gathered, (((0,), (1,)), ((), ())), precision=HI, preferred_element_type=jnp.float32
    )
    activated, pull = jax.vjp(jax.nn.gelu, aggregated)
    slope = pull(cotangent)[0]
    weight_term = lax.dot_general(
        gathered, slope, (((0,), (1,)), ((), ())), precision=HI, preferred_element_type=jnp.float32
    )
    weight_grad = sum_over_wide(weight_term)
    spread = jnp.dot(weight, slope, precision=HI, preferred_element_type=jnp.float32)
    terms = backward_part(count, rows, slots, tile_collection, spread)
    input_cols = scatter_terms(terms)
    input_grad = gather_loop(input_cols, loop)
    return (activated, input_grad, weight_grad)


def solution(mesh):
    return jax.shard_map(
        per_device,
        mesh=mesh,
        in_specs=(
            P(None, "wide"),
            P(),
            P(None, "wide"),
            P("loop", "wide", None, None, None),
            P("loop", "wide", None),
            P("loop", "wide", None),
            P("loop", "wide"),
        ),
        out_specs=(P(None, "wide"), P(None, "wide"), P()),
        check_vma=False,
    )
```

```python
import functools

import jax
import jax.numpy as jnp
from jax import lax
from jax.experimental import pallas as pl
from jax.experimental.pallas import tpu as pltpu
from jax.sharding import PartitionSpec as P

HI = lax.Precision.HIGHEST
AXES = ("loop", "wide")
SIDE = 4
TILE = 128
SLOTS = 256
GROUP = 16
PER = 8
CLASS_BUFFERS = (8, 6, 2)
VMEM_BYTES = 28 * 1024 * 1024


def device_index(y, core, x, z):
    y, x, z = y % SIDE, x % SIDE, z % SIDE
    return (((y & 1) * 2 + core) * 2 + (y >> 1)) * 16 + x * SIDE + z


def permute(value, move):
    pairs = []
    for y in range(SIDE):
        for core in range(2):
            for x in range(SIDE):
                for z in range(SIDE):
                    pairs.append((device_index(y, core, x, z), device_index(*move(y, core, x, z))))
    return lax.ppermute(value, AXES, pairs)


def toward(core):
    return 1 - 2 * core


def x_up(y, core, x, z):
    return (y, core, x + toward(core), z)


def x_down(y, core, x, z):
    return (y, core, x - toward(core), z)


def z_up(y, core, x, z):
    return (y, core, x, z + toward(core))


def z_down(y, core, x, z):
    return (y, core, x, z - toward(core))


def y_partner(y, core, x, z):
    return (3 - y, core, x, z)


def y_pair(y, core, x, z):
    return (y ^ 1, core, x, z)


def y_far(y, core, x, z):
    return (y + 2, core, x, z)


def core_swap(y, core, x, z):
    return (y, 1 - core, x, z)


def after(value, *others):
    return lax.optimization_barrier((value,) + others)[0]


def split_high_low(value):
    high = value.astype(jnp.bfloat16)
    low = (value - high.astype(jnp.float32)).astype(jnp.bfloat16)
    return high, low


def start_groups(tiles_ref, order_ref, held, sems, begin, groups):
    @pl.loop(0, groups)
    def _(group):
        for j in range(GROUP):
            spot = group * GROUP + j
            source = order_ref[jnp.minimum(begin + spot, SLOTS - 1)]
            pltpu.make_async_copy(tiles_ref.at[source], held.at[spot], sems.at[group]).start()


def wait_group(tiles_ref, held, sems, group):
    part = pl.ds(group * GROUP, GROUP)
    pltpu.make_async_copy(tiles_ref.at[pl.ds(0, GROUP)], held.at[part], sems.at[group]).wait()


def class_range(bounds_ref, which):
    begin, end = bounds_ref[which], bounds_ref[which + 1]
    return begin, end, (end - begin + GROUP - 1) // GROUP


def forward_kernel(which, bounds_ref, order_ref, rows_ref, slots_ref, tiles_ref, *rest):
    number = CLASS_BUFFERS[which]
    base = sum(CLASS_BUFFERS[:which]) * PER
    buffers = rest[:number]
    rest = rest[number:]
    prior_ref = rest[0] if which else None
    out_ref, held, pairs, total, sems = rest[-5:]
    nrow = out_ref.shape[0]
    begin, end, groups = class_range(bounds_ref, which)
    start_groups(tiles_ref, order_ref, held, sems, begin, groups)
    if which:
        total[0:nrow] = prior_ref[...]
    else:
        total[0:nrow] = jnp.zeros_like(out_ref)
    for index in range(number):

        @pl.loop(0, PER, unroll=4)
        def _(j):
            high, low = split_high_low(buffers[index][j])
            pairs[index * PER + j, :, :TILE] = high
            pairs[index * PER + j, :, TILE:] = low

    @pl.loop(0, groups)
    def _(group):
        wait_group(tiles_ref, held, sems, group)
        for j in range(GROUP):
            spot = group * GROUP + j
            place = jnp.minimum(begin + spot, SLOTS - 1)
            live = begin + spot < end
            row = jnp.where(live, rows_ref[place], nrow)
            slot = jnp.where(live, slots_ref[place] - base, 0)
            high, low = split_high_low(held[spot])
            right = pairs[slot]
            product = jnp.dot(
                jnp.concatenate([high, low], axis=1),
                jnp.concatenate([right, right], axis=0),
                preferred_element_type=jnp.float32,
            )
            total[row] += product[:, :TILE] + product[:, TILE:]

    out_ref[...] = total[0:nrow]


def backward_kernel(which, bounds_ref, order_ref, rows_ref, slots_ref, tiles_ref, slope_ref, *rest):
    number = CLASS_BUFFERS[which]
    base = sum(CLASS_BUFFERS[:which]) * PER
    buffers = rest[:number]
    held, pairs, total, sems, out_sems = rest[number:]
    begin, end, groups = class_range(bounds_ref, which)
    start_groups(tiles_ref, order_ref, held, sems, begin, groups)
    for row in range(pairs.shape[0]):
        high, low = split_high_low(slope_ref[:, row * TILE : (row + 1) * TILE])
        pairs[row, :, :TILE] = high
        pairs[row, :, TILE:] = low

    @pl.loop(0, number * PER, unroll=4)
    def _(slot):
        total[slot] = jnp.zeros((TILE, TILE), jnp.float32)

    @pl.loop(0, groups)
    def _(group):
        wait_group(tiles_ref, held, sems, group)
        for j in range(GROUP):
            spot = group * GROUP + j
            place = jnp.minimum(begin + spot, SLOTS - 1)
            live = begin + spot < end
            slot = jnp.where(live, slots_ref[place] - base, number * PER)
            high, low = split_high_low(held[spot])
            right = jnp.concatenate([high, low], axis=1)
            product = jnp.dot(
                pairs[rows_ref[place]],
                jnp.concatenate([right, right], axis=0),
                preferred_element_type=jnp.float32,
            )
            total[slot] += product[:, :TILE] + product[:, TILE:]

    copies = []
    for index in range(number):
        copy = pltpu.make_async_copy(
            total.at[pl.ds(index * PER, PER)], buffers[index], out_sems.at[index]
        )
        copy.start()
        copies.append(copy)
    for copy in copies:
        copy.wait()


def smem():
    return pl.BlockSpec(memory_space=pltpu.SMEM)


def vmem():
    return pl.BlockSpec(memory_space=pltpu.VMEM)


def anywhere():
    return pl.BlockSpec(memory_space=pl.ANY)


def cost(which):
    live = (96, 72, 24)[which]
    return pl.CostEstimate(
        flops=live * 8 * TILE**3, bytes_accessed=live * 4 * TILE**2, transcendentals=0
    )


def forward_part(which, plan, tiles, buffers, prior, nrow):
    extra = [prior] if which else []
    number = CLASS_BUFFERS[which]
    return pl.pallas_call(
        functools.partial(forward_kernel, which),
        name="forward_tiles_%d" % which,
        out_shape=jax.ShapeDtypeStruct((nrow, TILE, TILE), jnp.float32),
        in_specs=[smem()] * 4 + [anywhere()] + [vmem()] * (number + len(extra)),
        out_specs=vmem(),
        scratch_shapes=[
            pltpu.VMEM((SLOTS, TILE, TILE), jnp.float32),
            pltpu.VMEM((number * PER, TILE, 2 * TILE), jnp.bfloat16),
            pltpu.VMEM((nrow + 1, TILE, TILE), jnp.float32),
            pltpu.SemaphoreType.DMA((SLOTS // GROUP,)),
        ],
        cost_estimate=cost(which),
        compiler_params=pltpu.CompilerParams(vmem_limit_bytes=VMEM_BYTES),
    )(*plan, tiles, *buffers, *extra)


def backward_part(which, plan, tiles, slope):
    number = CLASS_BUFFERS[which]
    return pl.pallas_call(
        functools.partial(backward_kernel, which),
        name="backward_tiles_%d" % which,
        out_shape=[jax.ShapeDtypeStruct((PER, TILE, TILE), jnp.float32)] * number,
        in_specs=[smem()] * 4 + [anywhere(), vmem()],
        out_specs=[anywhere()] * number,
        scratch_shapes=[
            pltpu.VMEM((SLOTS, TILE, TILE), jnp.float32),
            pltpu.VMEM((slope.shape[1] // TILE, TILE, 2 * TILE), jnp.bfloat16),
            pltpu.VMEM((number * PER + 1, TILE, TILE), jnp.float32),
            pltpu.SemaphoreType.DMA((SLOTS // GROUP,)),
            pltpu.SemaphoreType.DMA((number,)),
        ],
        cost_estimate=cost(which),
        compiler_params=pltpu.CompilerParams(vmem_limit_bytes=VMEM_BYTES),
    )(*plan, tiles, slope)


def make_plan(rows, cols, count, loop, wide):
    sign = 1 - 2 * (loop % 2)
    node_block = cols // 4
    part = cols % 4
    across = (node_block // 16) ^ (wide // 16)
    dx = ((node_block // 4 - wide // 4) * sign) % 4
    dz = ((node_block - wide) * sign) % 4
    is_first = part < 2
    ring = jnp.where(is_first, dz, dx)
    inner = jnp.where(is_first, dx * 2 + part, dz * 2 + part - 2)
    near = jnp.where(is_first, 0, 4) + ring
    apart = jnp.where(is_first, 8, 11) + jnp.where(ring == 3, 2, ring)
    apart = jnp.where(ring == 2, jnp.where(is_first, 14, 15), apart)
    buffer = jnp.where(across == 0, near, apart)
    slots = buffer * PER + inner
    spots = jnp.arange(SLOTS, dtype=jnp.int32)
    kind = jnp.where(buffer < 8, 0, jnp.where(buffer < 14, 1, 2))
    kind = jnp.where(spots < count[0], kind, 3)
    ahead = (kind[None, :] < kind[:, None]) | (
        (kind[None, :] == kind[:, None]) & (spots[None, :] < spots[:, None])
    )
    rank = jnp.sum(ahead.astype(jnp.int32), axis=1)
    here = rank[None, :] == spots[:, None]

    def sort(values):
        return jnp.sum(jnp.where(here, values[None, :], 0), axis=1)

    steps = jnp.arange(4, dtype=jnp.int32)
    bounds = jnp.sum((kind[None, :] < steps[:, None]).astype(jnp.int32), axis=1)
    return bounds, sort(spots), sort(rows), sort(slots)


def gather_ring(value, up, down, near):
    one = permute(value, down)
    three = permute(value, up)
    two = permute(one, down) if near else permute(three, up)
    return [value, one, two, three]


def reduce_ring(parts, up, down, near):
    if near:
        one = parts[1] + permute(parts[2], up)
        three = parts[3]
    else:
        one = parts[1]
        three = parts[3] + permute(parts[2], down)
    return parts[0] + permute(one, up) + permute(three, down)


def quarter_tiles(features, index):
    feats = features.shape[0]
    split = features.reshape(feats, 4, 4, TILE)
    piece = lax.dynamic_index_in_dim(split, index, 1, keepdims=False)
    return jnp.transpose(piece, (1, 2, 0))


def gather_features(features, loop):
    partner = permute(quarter_tiles(features, loop ^ 2), y_partner)
    own = quarter_tiles(features, loop)
    sets = []
    for piece, near in ((own, True), (partner, False)):
        row = jnp.concatenate(gather_ring(piece[:2], x_up, x_down, near), axis=0)
        column = jnp.concatenate(gather_ring(piece[2:], z_up, z_down, near), axis=0)
        first = gather_ring(row, z_up, z_down, near)
        second = gather_ring(column, x_up, x_down, near)
        sets.append((first, second))
    first, second = sets[1]
    return (
        sets[0][0] + sets[0][1],
        [first[0], first[1], first[3], second[0], second[1], second[3]],
        [first[2], second[2]],
    )


def scatter_terms(own, apart, apart_far):
    first = [apart[0], apart[1], apart_far[0], apart[2]]
    second = [apart[3], apart[4], apart_far[1], apart[5]]
    pieces = []
    for row, column, near in ((first, second, False), (own[:4], own[4:], True)):
        row = reduce_ring(row, z_up, z_down, near)
        column = reduce_ring(column, x_up, x_down, near)
        half = reduce_ring([row[2 * i : 2 * i + 2] for i in range(4)], x_up, x_down, near)
        other = reduce_ring([column[2 * i : 2 * i + 2] for i in range(4)], z_up, z_down, near)
        pieces.append(jnp.concatenate([half, other], axis=0))
    return pieces[1] + permute(pieces[0], y_far)


def sum_over_loop(partial, loop):
    core = loop % 2
    half = partial.shape[0] // 2
    kept = lax.dynamic_slice_in_dim(partial, core * half, half, 0)
    given = lax.dynamic_slice_in_dim(partial, (1 - core) * half, half, 0)
    kept = kept + permute(given, core_swap)
    kept = kept + permute(kept, y_pair)
    other = permute(kept, core_swap)
    return jnp.where(
        core == 0,
        jnp.concatenate([kept, other], axis=0),
        jnp.concatenate([other, kept], axis=0),
    )


def sum_over_wide(value):
    for step in (1, 2):
        value = value + permute(value, lambda y, c, x, z: (y, c, x ^ step, z))
    for step in (1, 2):
        value = value + permute(value, lambda y, c, x, z: (y, c, x, z ^ step))
    return value + permute(value, y_far)


def gather_loop(own, loop):
    low, core = loop // 2, loop % 2
    across = permute(own, y_pair)
    own_other = permute(own, core_swap)
    across_other = permute(across, core_swap)
    same = jnp.where(
        core == 0, jnp.stack([own, own_other]), jnp.stack([own_other, own])
    )
    far = jnp.where(
        core == 0, jnp.stack([across, across_other]), jnp.stack([across_other, across])
    )
    whole = jnp.where(low == 0, jnp.stack([same, far]), jnp.stack([far, same]))
    feats = own.shape[1]
    return jnp.transpose(whole.reshape(-1, feats, TILE), (1, 0, 2)).reshape(feats, -1)


def per_device(features, weight, cotangent, tiles, tile_rows, tile_cols, counts):
    feats, shard_nodes = features.shape
    loop = lax.axis_index("loop")
    wide = lax.axis_index("wide")
    nrow = shard_nodes // TILE
    tile_collection = tiles.reshape(SLOTS, TILE, TILE)
    plan = make_plan(
        tile_rows.reshape(SLOTS), tile_cols.reshape(SLOTS), counts.reshape(1), loop, wide
    )

    partial = None
    for which, buffers in enumerate(gather_features(features, loop)):
        partial = forward_part(which, plan, tile_collection, buffers, partial, nrow)
    gathered = sum_over_loop(partial, loop).reshape(shard_nodes, feats)
    aggregated = lax.dot_general(
        weight, gathered, (((0,), (1,)), ((), ())), precision=HI, preferred_element_type=jnp.float32
    )
    activated, pull = jax.vjp(jax.nn.gelu, aggregated)
    slope = pull(cotangent)[0]
    weight_term = lax.dot_general(
        gathered, slope, (((0,), (1,)), ((), ())), precision=HI, preferred_element_type=jnp.float32
    )
    spread = jnp.dot(weight, slope, precision=HI, preferred_element_type=jnp.float32)
    terms = [None, None, None]
    for which in (2, 1, 0):
        terms[which] = backward_part(which, plan, tile_collection, spread)
    weight_grad = sum_over_wide(weight_term)
    input_cols = scatter_terms(*terms)
    input_cols = after(input_cols, weight_grad)
    input_grad = gather_loop(input_cols, loop)
    return (activated, input_grad, weight_grad)


def solution(mesh):
    return jax.shard_map(
        per_device,
        mesh=mesh,
        in_specs=(
            P(None, "wide"),
            P(),
            P(None, "wide"),
            P("loop", "wide", None, None, None),
            P("loop", "wide", None),
            P("loop", "wide", None),
            P("loop", "wide"),
        ),
        out_specs=(P(None, "wide"), P(None, "wide"), P()),
        check_vma=False,
    )
```

```python
import functools

import jax
import jax.numpy as jnp
from jax import lax
from jax.experimental import pallas as pl
from jax.experimental.pallas import tpu as pltpu
from jax.sharding import PartitionSpec as P

HI = lax.Precision.HIGHEST
AXES = ("loop", "wide")
SIDE = 4
TILE = 128
SLOTS = 256
GROUP = 16
CHUNK = 32
STAGES = 3
PAIR_BYTES = 40 * 1024 * 1024
PER = 8
CLASS_BUFFERS = (8, 6, 2)
VMEM_BYTES = 24 * 1024 * 1024


def device_index(y, core, x, z):
    y, x, z = y % SIDE, x % SIDE, z % SIDE
    return (((y & 1) * 2 + core) * 2 + (y >> 1)) * 16 + x * SIDE + z


def permute(value, move):
    pairs = []
    for y in range(SIDE):
        for core in range(2):
            for x in range(SIDE):
                for z in range(SIDE):
                    pairs.append((device_index(y, core, x, z), device_index(*move(y, core, x, z))))
    return lax.ppermute(value, AXES, pairs)


def toward(core):
    return 1 - 2 * core


def x_up(y, core, x, z):
    return (y, core, x + toward(core), z)


def x_down(y, core, x, z):
    return (y, core, x - toward(core), z)


def z_up(y, core, x, z):
    return (y, core, x, z + toward(core))


def z_down(y, core, x, z):
    return (y, core, x, z - toward(core))


def y_partner(y, core, x, z):
    return (3 - y, core, x, z)


def y_pair(y, core, x, z):
    return (y ^ 1, core, x, z)


def y_far(y, core, x, z):
    return (y + 2, core, x, z)


def core_swap(y, core, x, z):
    return (y, 1 - core, x, z)


def after(value, *others):
    return lax.optimization_barrier((value,) + others)[0]


def split_high_low(value):
    high = value.astype(jnp.bfloat16)
    low = (value - high.astype(jnp.float32)).astype(jnp.bfloat16)
    return high, low


def pair_kernel(count_ref, tiles_ref, out_ref, held, sems):
    count = count_ref[0]

    def copy(chunk):
        source = tiles_ref.at[pl.ds(chunk * CHUNK, CHUNK)]
        return pltpu.make_async_copy(source, held.at[chunk % STAGES], sems.at[chunk % STAGES])

    def when_live(chunk):
        return pl.when(chunk * CHUNK < count)

    for chunk in range(STAGES):
        when_live(chunk)(copy(chunk).start)
    for chunk in range(SLOTS // CHUNK):

        @when_live(chunk)
        def _():
            copy(chunk).wait()

            @pl.loop(0, CHUNK, unroll=8)
            def _(j):
                high, low = split_high_low(held[chunk % STAGES, j])
                out_ref[chunk * CHUNK + j, :, :TILE] = high
                out_ref[chunk * CHUNK + j, :, TILE:] = low

            if chunk + STAGES < SLOTS // CHUNK:
                when_live(chunk + STAGES)(copy(chunk + STAGES).start)


def pair_tiles(count, tiles):
    return pl.pallas_call(
        pair_kernel,
        name="pair_tiles",
        out_shape=pltpu.VMEM((SLOTS, TILE, 2 * TILE), jnp.bfloat16),
        in_specs=[smem(), anywhere()],
        out_specs=vmem(),
        scratch_shapes=[
            pltpu.VMEM((STAGES, CHUNK, TILE, TILE), jnp.float32),
            pltpu.SemaphoreType.DMA((STAGES,)),
        ],
        cost_estimate=cost(8),
        compiler_params=pltpu.CompilerParams(vmem_limit_bytes=PAIR_BYTES),
    )(count, tiles)


def class_range(bounds_ref, which):
    begin, end = bounds_ref[which], bounds_ref[which + 1]
    return begin, end, (end - begin + GROUP - 1) // GROUP


def forward_kernel(which, bounds_ref, order_ref, rows_ref, slots_ref, tiles_ref, *rest):
    number = CLASS_BUFFERS[which]
    base = sum(CLASS_BUFFERS[:which]) * PER
    buffers = rest[:number]
    rest = rest[number:]
    prior_ref = rest[0] if which else None
    out_ref, pairs, total = rest[-3:]
    nrow = out_ref.shape[0]
    begin, end, groups = class_range(bounds_ref, which)
    if which:
        total[0:nrow] = prior_ref[...]
    else:
        total[0:nrow] = jnp.zeros_like(out_ref)
    for index in range(number):

        @pl.loop(0, PER, unroll=4)
        def _(j):
            high, low = split_high_low(buffers[index][j])
            pairs[index * PER + j, :, :TILE] = high
            pairs[index * PER + j, :, TILE:] = low

    @pl.loop(0, groups)
    def _(group):
        for j in range(GROUP):
            spot = group * GROUP + j
            place = jnp.minimum(begin + spot, SLOTS - 1)
            live = begin + spot < end
            row = jnp.where(live, rows_ref[place], nrow)
            slot = jnp.where(live, slots_ref[place] - base, 0)
            right = pairs[slot]
            product = jnp.dot(
                tiles_ref[order_ref[place]],
                jnp.concatenate([right, right], axis=0),
                preferred_element_type=jnp.float32,
            )
            total[row] += product[:, :TILE] + product[:, TILE:]

    out_ref[...] = total[0:nrow]


def backward_kernel(which, bounds_ref, order_ref, rows_ref, slots_ref, tiles_ref, slope_ref, *rest):
    number = CLASS_BUFFERS[which]
    base = sum(CLASS_BUFFERS[:which]) * PER
    buffers = rest[:number]
    pairs, total, out_sems = rest[number:]
    begin, end, groups = class_range(bounds_ref, which)
    for row in range(pairs.shape[0]):
        high, low = split_high_low(slope_ref[:, row * TILE : (row + 1) * TILE])
        pairs[row, :, :TILE] = high
        pairs[row, :, TILE:] = low

    @pl.loop(0, number * PER, unroll=4)
    def _(slot):
        total[slot] = jnp.zeros((TILE, TILE), jnp.float32)

    @pl.loop(0, groups)
    def _(group):
        for j in range(GROUP):
            spot = group * GROUP + j
            place = jnp.minimum(begin + spot, SLOTS - 1)
            live = begin + spot < end
            slot = jnp.where(live, slots_ref[place] - base, number * PER)
            right = tiles_ref[order_ref[place]]
            product = jnp.dot(
                pairs[rows_ref[place]],
                jnp.concatenate([right, right], axis=0),
                preferred_element_type=jnp.float32,
            )
            total[slot] += product[:, :TILE] + product[:, TILE:]

    copies = []
    for index in range(number):
        copy = pltpu.make_async_copy(
            total.at[pl.ds(index * PER, PER)], buffers[index], out_sems.at[index]
        )
        copy.start()
        copies.append(copy)
    for copy in copies:
        copy.wait()


def smem():
    return pl.BlockSpec(memory_space=pltpu.SMEM)


def vmem():
    return pl.BlockSpec(memory_space=pltpu.VMEM)


def anywhere():
    return pl.BlockSpec(memory_space=pl.ANY)


def cost(microseconds):
    return pl.CostEstimate(
        flops=int(microseconds * 1.1e9), bytes_accessed=1 << 20, transcendentals=0
    )


def forward_part(which, plan, tiles, buffers, prior, nrow):
    extra = [prior] if which else []
    number = CLASS_BUFFERS[which]
    return pl.pallas_call(
        functools.partial(forward_kernel, which),
        name="forward_tiles_%d" % which,
        out_shape=jax.ShapeDtypeStruct((nrow, TILE, TILE), jnp.float32),
        in_specs=[smem()] * 4 + [vmem()] * (1 + number + len(extra)),
        out_specs=vmem(),
        scratch_shapes=[
            pltpu.VMEM((number * PER, TILE, 2 * TILE), jnp.bfloat16),
            pltpu.VMEM((nrow + 1, TILE, TILE), jnp.float32),
        ],
        cost_estimate=cost((6, 5, 2)[which]),
        compiler_params=pltpu.CompilerParams(vmem_limit_bytes=VMEM_BYTES),
    )(*plan, tiles, *buffers, *extra)


def backward_part(which, plan, tiles, slope):
    number = CLASS_BUFFERS[which]
    return pl.pallas_call(
        functools.partial(backward_kernel, which),
        name="backward_tiles_%d" % which,
        out_shape=[jax.ShapeDtypeStruct((PER, TILE, TILE), jnp.float32)] * number,
        in_specs=[smem()] * 4 + [vmem(), vmem()],
        out_specs=[anywhere()] * number,
        scratch_shapes=[
            pltpu.VMEM((slope.shape[1] // TILE, TILE, 2 * TILE), jnp.bfloat16),
            pltpu.VMEM((number * PER + 1, TILE, TILE), jnp.float32),
            pltpu.SemaphoreType.DMA((number,)),
        ],
        cost_estimate=cost((6, 5, 2)[which]),
        compiler_params=pltpu.CompilerParams(vmem_limit_bytes=VMEM_BYTES),
    )(*plan, tiles, slope)


def make_plan(rows, cols, count, loop, wide):
    sign = 1 - 2 * (loop % 2)
    node_block = cols // 4
    part = cols % 4
    across = (node_block // 16) ^ (wide // 16)
    dx = ((node_block // 4 - wide // 4) * sign) % 4
    dz = ((node_block - wide) * sign) % 4
    is_first = part < 2
    ring = jnp.where(is_first, dz, dx)
    inner = jnp.where(is_first, dx * 2 + part, dz * 2 + part - 2)
    near = jnp.where(is_first, 0, 4) + ring
    apart = jnp.where(is_first, 8, 11) + jnp.where(ring == 3, 2, ring)
    apart = jnp.where(ring == 2, jnp.where(is_first, 14, 15), apart)
    buffer = jnp.where(across == 0, near, apart)
    slots = buffer * PER + inner
    spots = jnp.arange(SLOTS, dtype=jnp.int32)
    kind = jnp.where(buffer < 8, 0, jnp.where(buffer < 14, 1, 2))
    kind = jnp.where(spots < count[0], kind, 3)
    ahead = (kind[None, :] < kind[:, None]) | (
        (kind[None, :] == kind[:, None]) & (spots[None, :] < spots[:, None])
    )
    rank = jnp.sum(ahead.astype(jnp.int32), axis=1)
    here = rank[None, :] == spots[:, None]

    def sort(values):
        return jnp.sum(jnp.where(here, values[None, :], 0), axis=1)

    steps = jnp.arange(4, dtype=jnp.int32)
    bounds = jnp.sum((kind[None, :] < steps[:, None]).astype(jnp.int32), axis=1)
    return bounds, sort(spots), sort(rows), sort(slots)


def reduce_ring(parts, up, down, near):
    if near:
        one = parts[1] + permute(parts[2], up)
        three = parts[3]
    else:
        one = parts[1]
        three = parts[3] + permute(parts[2], down)
    return parts[0] + permute(one, up) + permute(three, down)


def quarter_tiles(features, index):
    feats = features.shape[0]
    split = features.reshape(feats, 4, 4, TILE)
    piece = lax.dynamic_index_in_dim(split, index, 1, keepdims=False)
    return jnp.transpose(piece, (1, 2, 0))


def gather_features(features, loop):
    own = quarter_tiles(features, loop)
    partner = permute(quarter_tiles(features, loop ^ 2), y_partner)
    row_one, row_three = permute(own[:2], x_down), permute(own[:2], x_up)
    column_one, column_three = permute(own[2:], z_down), permute(own[2:], z_up)
    row_two, column_two = permute(row_one, x_down), permute(column_one, z_down)
    row = jnp.concatenate([own[:2], row_one, row_two, row_three], axis=0)
    column = jnp.concatenate([own[2:], column_one, column_two, column_three], axis=0)
    first_one, second_one = permute(row, z_down), permute(column, x_down)
    first_three, second_three = permute(row, z_up), permute(column, x_up)
    first_two, second_two = permute(first_one, z_down), permute(second_one, x_down)
    near = [row, first_one, first_two, first_three, column, second_one, second_two, second_three]

    partner = after(partner, row, column)
    row_one, row_three = permute(partner[:2], x_down), permute(partner[:2], x_up)
    column_one, column_three = permute(partner[2:], z_down), permute(partner[2:], z_up)
    row_two, column_two = permute(row_three, x_up), permute(column_three, z_up)
    row = jnp.concatenate([partner[:2], row_one, row_two, row_three], axis=0)
    column = jnp.concatenate([partner[2:], column_one, column_two, column_three], axis=0)
    first_one, second_one = permute(row, z_down), permute(column, x_down)
    first_three, second_three = permute(row, z_up), permute(column, x_up)
    apart = [row, first_one, first_three, column, second_one, second_three]
    return near, apart


def scatter_terms(own, apart, apart_far):
    first = [apart[0], apart[1], apart_far[0], apart[2]]
    second = [apart[3], apart[4], apart_far[1], apart[5]]
    pieces = []
    for row, column, near in ((first, second, False), (own[:4], own[4:], True)):
        row = reduce_ring(row, z_up, z_down, near)
        column = reduce_ring(column, x_up, x_down, near)
        half = reduce_ring([row[2 * i : 2 * i + 2] for i in range(4)], x_up, x_down, near)
        other = reduce_ring([column[2 * i : 2 * i + 2] for i in range(4)], z_up, z_down, near)
        pieces.append(jnp.concatenate([half, other], axis=0))
    return pieces[1] + permute(pieces[0], y_far)


def sum_over_loop(partial, loop):
    core = loop % 2
    half = partial.shape[0] // 2
    kept = lax.dynamic_slice_in_dim(partial, core * half, half, 0)
    given = lax.dynamic_slice_in_dim(partial, (1 - core) * half, half, 0)
    kept = kept + permute(given, core_swap)
    kept = kept + permute(kept, y_pair)
    other = permute(kept, core_swap)
    return jnp.where(
        core == 0,
        jnp.concatenate([kept, other], axis=0),
        jnp.concatenate([other, kept], axis=0),
    )


def sum_over_wide(value):
    for step in (1, 2):
        value = value + permute(value, lambda y, c, x, z: (y, c, x ^ step, z))
    for step in (1, 2):
        value = value + permute(value, lambda y, c, x, z: (y, c, x, z ^ step))
    return value + permute(value, y_far)


def gather_loop(own, loop):
    low, core = loop // 2, loop % 2
    across = permute(own, y_pair)
    own_other = permute(own, core_swap)
    across_other = permute(across, core_swap)
    same = jnp.where(
        core == 0, jnp.stack([own, own_other]), jnp.stack([own_other, own])
    )
    far = jnp.where(
        core == 0, jnp.stack([across, across_other]), jnp.stack([across_other, across])
    )
    whole = jnp.where(low == 0, jnp.stack([same, far]), jnp.stack([far, same]))
    feats = own.shape[1]
    return jnp.transpose(whole.reshape(-1, feats, TILE), (1, 0, 2)).reshape(feats, -1)


def per_device(features, weight, cotangent, tiles, tile_rows, tile_cols, counts):
    feats, shard_nodes = features.shape
    loop = lax.axis_index("loop")
    wide = lax.axis_index("wide")
    nrow = shard_nodes // TILE
    tile_collection = tiles.reshape(SLOTS, TILE, TILE)
    plan = make_plan(
        tile_rows.reshape(SLOTS), tile_cols.reshape(SLOTS), counts.reshape(1), loop, wide
    )

    near, apart = gather_features(features, loop)
    pairs = pair_tiles(after(counts.reshape(1), near[0], near[4]), tile_collection)
    partial = forward_part(0, plan, pairs, near, None, nrow)
    far = [permute(after(apart[2], pairs), z_up), permute(after(apart[5], pairs), x_up)]
    partial = forward_part(1, plan, pairs, apart, partial, nrow)
    partial = forward_part(2, plan, pairs, far, partial, nrow)
    gathered = sum_over_loop(partial, loop).reshape(shard_nodes, feats)
    aggregated = lax.dot_general(
        weight, gathered, (((0,), (1,)), ((), ())), precision=HI, preferred_element_type=jnp.float32
    )
    activated, pull = jax.vjp(jax.nn.gelu, aggregated)
    slope = pull(cotangent)[0]
    weight_term = lax.dot_general(
        gathered, slope, (((0,), (1,)), ((), ())), precision=HI, preferred_element_type=jnp.float32
    )
    spread = jnp.dot(weight, slope, precision=HI, preferred_element_type=jnp.float32)
    apart_far = backward_part(2, plan, pairs, spread)
    apart = backward_part(1, plan, pairs, after(spread, *apart_far))
    own = backward_part(0, plan, pairs, after(spread, *apart))
    weight_grad = sum_over_wide(weight_term)
    input_cols = scatter_terms(own, apart, apart_far)
    input_cols = after(input_cols, weight_grad)
    input_grad = gather_loop(input_cols, loop)
    return (activated, input_grad, weight_grad)


def solution(mesh):
    return jax.shard_map(
        per_device,
        mesh=mesh,
        in_specs=(
            P(None, "wide"),
            P(),
            P(None, "wide"),
            P("loop", "wide", None, None, None),
            P("loop", "wide", None),
            P("loop", "wide", None),
            P("loop", "wide"),
        ),
        out_specs=(P(None, "wide"), P(None, "wide"), P()),
        check_vma=False,
    )
```

```python
import functools

import jax
import jax.numpy as jnp
from jax import lax
from jax.experimental import pallas as pl
from jax.experimental.pallas import tpu as pltpu
from jax.sharding import PartitionSpec as P

HI = lax.Precision.HIGHEST
AXES = ("loop", "wide")
SIDE = 4
TILE = 128
SLOTS = 256
GROUP = 16
CHUNK = 32
STAGES = 3
PAIR_BYTES = 8 * 1024 * 1024
PER = 8
CLASS_BUFFERS = (8, 6, 2)
VMEM_BYTES = 8 * 1024 * 1024


def device_index(y, core, x, z):
    y, x, z = y % SIDE, x % SIDE, z % SIDE
    return (((y & 1) * 2 + core) * 2 + (y >> 1)) * 16 + x * SIDE + z


def permute(value, move):
    pairs = []
    for y in range(SIDE):
        for core in range(2):
            for x in range(SIDE):
                for z in range(SIDE):
                    pairs.append((device_index(y, core, x, z), device_index(*move(y, core, x, z))))
    return lax.ppermute(value, AXES, pairs)


def toward(core):
    return 1 - 2 * core


def x_up(y, core, x, z):
    return (y, core, x + toward(core), z)


def x_down(y, core, x, z):
    return (y, core, x - toward(core), z)


def z_up(y, core, x, z):
    return (y, core, x, z + toward(core))


def z_down(y, core, x, z):
    return (y, core, x, z - toward(core))


def y_partner(y, core, x, z):
    return (3 - y, core, x, z)


def y_pair(y, core, x, z):
    return (y ^ 1, core, x, z)


def y_far(y, core, x, z):
    return (y + 2, core, x, z)


def core_swap(y, core, x, z):
    return (y, 1 - core, x, z)


def after(value, *others):
    return lax.optimization_barrier((value,) + others)[0]


def split_high_low(value):
    high = value.astype(jnp.bfloat16)
    low = (value - high.astype(jnp.float32)).astype(jnp.bfloat16)
    return high, low


def pair_kernel(count_ref, tiles_ref, out_ref, held, sems):
    count = count_ref[0]

    def copy(chunk):
        source = tiles_ref.at[pl.ds(chunk * CHUNK, CHUNK)]
        return pltpu.make_async_copy(source, held.at[chunk % STAGES], sems.at[chunk % STAGES])

    def when_live(chunk):
        return pl.when(chunk * CHUNK < count)

    for chunk in range(STAGES):
        when_live(chunk)(copy(chunk).start)
    for chunk in range(SLOTS // CHUNK):

        @when_live(chunk)
        def _():
            copy(chunk).wait()

            @pl.loop(0, CHUNK, unroll=8)
            def _(j):
                high, low = split_high_low(held[chunk % STAGES, j])
                out_ref[chunk * CHUNK + j, :, :TILE] = high
                out_ref[chunk * CHUNK + j, :, TILE:] = low

            if chunk + STAGES < SLOTS // CHUNK:
                when_live(chunk + STAGES)(copy(chunk + STAGES).start)


def pair_tiles(count, tiles):
    return pl.pallas_call(
        pair_kernel,
        name="pair_tiles",
        out_shape=pltpu.VMEM((SLOTS, TILE, 2 * TILE), jnp.bfloat16),
        in_specs=[smem(), anywhere()],
        out_specs=vmem(),
        scratch_shapes=[
            pltpu.VMEM((STAGES, CHUNK, TILE, TILE), jnp.float32),
            pltpu.SemaphoreType.DMA((STAGES,)),
        ],
        cost_estimate=cost(8),
        compiler_params=pltpu.CompilerParams(vmem_limit_bytes=PAIR_BYTES),
    )(count, tiles)


def class_range(bounds_ref, which):
    begin, end = bounds_ref[which], bounds_ref[which + 1]
    return begin, end, (end - begin + GROUP - 1) // GROUP


def forward_kernel(which, bounds_ref, order_ref, rows_ref, slots_ref, tiles_ref, *rest):
    number = CLASS_BUFFERS[which]
    base = sum(CLASS_BUFFERS[:which]) * PER
    buffers = rest[:number]
    rest = rest[number:]
    prior_ref = rest[0] if which else None
    out_ref, pairs, total = rest[-3:]
    nrow = out_ref.shape[0]
    begin, end, groups = class_range(bounds_ref, which)
    if which:
        total[0:nrow] = prior_ref[...]
    else:
        total[0:nrow] = jnp.zeros_like(out_ref)
    for index in range(number):

        @pl.loop(0, PER, unroll=4)
        def _(j):
            high, low = split_high_low(buffers[index][j])
            pairs[index * PER + j, :, :TILE] = high
            pairs[index * PER + j, :, TILE:] = low

    @pl.loop(0, groups)
    def _(group):
        for j in range(GROUP):
            spot = group * GROUP + j
            place = jnp.minimum(begin + spot, SLOTS - 1)
            live = begin + spot < end
            row = jnp.where(live, rows_ref[place], nrow)
            slot = jnp.where(live, slots_ref[place] - base, 0)
            right = pairs[slot]
            product = jnp.dot(
                tiles_ref[order_ref[place]],
                jnp.concatenate([right, right], axis=0),
                preferred_element_type=jnp.float32,
            )
            total[row] += product[:, :TILE] + product[:, TILE:]

    out_ref[...] = total[0:nrow]


def backward_kernel(which, bounds_ref, order_ref, rows_ref, slots_ref, tiles_ref, slope_ref, *rest):
    number = CLASS_BUFFERS[which]
    base = sum(CLASS_BUFFERS[:which]) * PER
    buffers = rest[:number]
    pairs, total, out_sems = rest[number:]
    begin, end, groups = class_range(bounds_ref, which)
    for row in range(pairs.shape[0]):
        high, low = split_high_low(slope_ref[:, row * TILE : (row + 1) * TILE])
        pairs[row, :, :TILE] = high
        pairs[row, :, TILE:] = low

    @pl.loop(0, number * PER, unroll=4)
    def _(slot):
        total[slot] = jnp.zeros((TILE, TILE), jnp.float32)

    @pl.loop(0, groups)
    def _(group):
        for j in range(GROUP):
            spot = group * GROUP + j
            place = jnp.minimum(begin + spot, SLOTS - 1)
            live = begin + spot < end
            slot = jnp.where(live, slots_ref[place] - base, number * PER)
            right = tiles_ref[order_ref[place]]
            product = jnp.dot(
                pairs[rows_ref[place]],
                jnp.concatenate([right, right], axis=0),
                preferred_element_type=jnp.float32,
            )
            total[slot] += product[:, :TILE] + product[:, TILE:]

    copies = []
    for index in range(number):
        copy = pltpu.make_async_copy(
            total.at[pl.ds(index * PER, PER)], buffers[index], out_sems.at[index]
        )
        copy.start()
        copies.append(copy)
    for copy in copies:
        copy.wait()


def smem():
    return pl.BlockSpec(memory_space=pltpu.SMEM)


def vmem():
    return pl.BlockSpec(memory_space=pltpu.VMEM)


def anywhere():
    return pl.BlockSpec(memory_space=pl.ANY)


def cost(microseconds):
    return pl.CostEstimate(
        flops=int(microseconds * 1.1e9), bytes_accessed=1 << 20, transcendentals=0
    )


def forward_part(which, plan, tiles, buffers, prior, nrow):
    extra = [prior] if which else []
    number = CLASS_BUFFERS[which]
    return pl.pallas_call(
        functools.partial(forward_kernel, which),
        name="forward_tiles_%d" % which,
        out_shape=jax.ShapeDtypeStruct((nrow, TILE, TILE), jnp.float32),
        in_specs=[smem()] * 4 + [vmem()] * (1 + number + len(extra)),
        out_specs=vmem(),
        scratch_shapes=[
            pltpu.VMEM((number * PER, TILE, 2 * TILE), jnp.bfloat16),
            pltpu.VMEM((nrow + 1, TILE, TILE), jnp.float32),
        ],
        cost_estimate=cost((6, 5, 2)[which]),
        compiler_params=pltpu.CompilerParams(vmem_limit_bytes=VMEM_BYTES),
    )(*plan, tiles, *buffers, *extra)


def backward_part(which, plan, tiles, slope):
    number = CLASS_BUFFERS[which]
    return pl.pallas_call(
        functools.partial(backward_kernel, which),
        name="backward_tiles_%d" % which,
        out_shape=[jax.ShapeDtypeStruct((PER, TILE, TILE), jnp.float32)] * number,
        in_specs=[smem()] * 4 + [vmem(), vmem()],
        out_specs=[anywhere()] * number,
        scratch_shapes=[
            pltpu.VMEM((slope.shape[1] // TILE, TILE, 2 * TILE), jnp.bfloat16),
            pltpu.VMEM((number * PER + 1, TILE, TILE), jnp.float32),
            pltpu.SemaphoreType.DMA((number,)),
        ],
        cost_estimate=cost((6, 5, 2)[which]),
        compiler_params=pltpu.CompilerParams(vmem_limit_bytes=VMEM_BYTES),
    )(*plan, tiles, slope)


def make_plan(rows, cols, count, loop, wide):
    sign = 1 - 2 * (loop % 2)
    node_block = cols // 4
    part = cols % 4
    across = (node_block // 16) ^ (wide // 16)
    dx = ((node_block // 4 - wide // 4) * sign) % 4
    dz = ((node_block - wide) * sign) % 4
    is_first = part < 2
    ring = jnp.where(is_first, dz, dx)
    inner = jnp.where(is_first, dx * 2 + part, dz * 2 + part - 2)
    near = jnp.where(is_first, 0, 4) + ring
    apart = jnp.where(is_first, 8, 11) + jnp.where(ring == 3, 2, ring)
    apart = jnp.where(ring == 2, jnp.where(is_first, 14, 15), apart)
    buffer = jnp.where(across == 0, near, apart)
    slots = buffer * PER + inner
    spots = jnp.arange(SLOTS, dtype=jnp.int32)
    kind = jnp.where(buffer < 8, 0, jnp.where(buffer < 14, 1, 2))
    kind = jnp.where(spots < count[0], kind, 3)
    ahead = (kind[None, :] < kind[:, None]) | (
        (kind[None, :] == kind[:, None]) & (spots[None, :] < spots[:, None])
    )
    rank = jnp.sum(ahead.astype(jnp.int32), axis=1)
    here = rank[None, :] == spots[:, None]

    def sort(values):
        return jnp.sum(jnp.where(here, values[None, :], 0), axis=1)

    steps = jnp.arange(4, dtype=jnp.int32)
    bounds = jnp.sum((kind[None, :] < steps[:, None]).astype(jnp.int32), axis=1)
    return bounds, sort(spots), sort(rows), sort(slots)


def reduce_ring(parts, up, down, near):
    if near:
        one = parts[1] + permute(parts[2], up)
        three = parts[3]
    else:
        one = parts[1]
        three = parts[3] + permute(parts[2], down)
    return parts[0] + permute(one, up) + permute(three, down)


def quarter_tiles(features, index):
    feats = features.shape[0]
    split = features.reshape(feats, 4, 4, TILE)
    piece = lax.dynamic_index_in_dim(split, index, 1, keepdims=False)
    return jnp.transpose(piece, (1, 2, 0))


def gather_features(features, loop):
    own = quarter_tiles(features, loop)
    partner = permute(quarter_tiles(features, loop ^ 2), y_partner)
    row_one, row_three = permute(own[:2], x_down), permute(own[:2], x_up)
    column_one, column_three = permute(own[2:], z_down), permute(own[2:], z_up)
    row_two, column_two = permute(row_one, x_down), permute(column_one, z_down)
    row = jnp.concatenate([own[:2], row_one, row_two, row_three], axis=0)
    column = jnp.concatenate([own[2:], column_one, column_two, column_three], axis=0)
    first_one, second_one = permute(row, z_down), permute(column, x_down)
    first_three, second_three = permute(row, z_up), permute(column, x_up)
    first_two, second_two = permute(first_one, z_down), permute(second_one, x_down)
    near = [row, first_one, first_two, first_three, column, second_one, second_two, second_three]

    partner = after(partner, row, column)
    row_one, row_three = permute(partner[:2], x_down), permute(partner[:2], x_up)
    column_one, column_three = permute(partner[2:], z_down), permute(partner[2:], z_up)
    row_two, column_two = permute(row_three, x_up), permute(column_three, z_up)
    row = jnp.concatenate([partner[:2], row_one, row_two, row_three], axis=0)
    column = jnp.concatenate([partner[2:], column_one, column_two, column_three], axis=0)
    first_one, second_one = permute(row, z_down), permute(column, x_down)
    first_three, second_three = permute(row, z_up), permute(column, x_up)
    apart = [row, first_one, first_three, column, second_one, second_three]
    return near, apart


def scatter_terms(own, apart, apart_far, weight_term):
    row_sent = permute(apart_far[0], z_down)
    column_sent = permute(apart_far[1], x_down)
    weight_term = flip_add(after(weight_term, row_sent), "x", 1)
    row_one, column_one = permute(apart[1], z_up), permute(apart[4], x_up)
    row_three = permute(apart[2] + row_sent, z_down)
    column_three = permute(apart[5] + column_sent, x_down)
    row = apart[0] + row_one + row_three
    column = apart[3] + column_one + column_three
    weight_term = flip_add(after(weight_term, column), "x", 2)
    apart_half = reduce_ring(split_row(row), x_up, x_down, False)
    apart_other = reduce_ring(split_row(column), z_up, z_down, False)
    sent = permute(jnp.concatenate([apart_half, apart_other], axis=0), y_far)

    row = reduce_ring(own[:4], z_up, z_down, True)
    weight_term = flip_add(after(weight_term, row), "z", 1)
    column = reduce_ring(own[4:], x_up, x_down, True)
    weight_term = flip_add(after(weight_term, column), "z", 2)
    half = reduce_ring(split_row(row), x_up, x_down, True)
    other = reduce_ring(split_row(column), z_up, z_down, True)
    kept = jnp.concatenate([half, other], axis=0)
    total = after(kept, weight_term) + sent
    return total, weight_term + permute(weight_term, y_far)


def split_row(row):
    return [row[2 * i : 2 * i + 2] for i in range(4)]


def flip_add(value, axis, step):
    if axis == "x":
        return value + permute(value, lambda y, c, x, z: (y, c, x ^ step, z))
    return value + permute(value, lambda y, c, x, z: (y, c, x, z ^ step))


def sum_over_loop(partial, loop):
    core = loop % 2
    half = partial.shape[0] // 2
    kept = lax.dynamic_slice_in_dim(partial, core * half, half, 0)
    given = lax.dynamic_slice_in_dim(partial, (1 - core) * half, half, 0)
    kept = kept + permute(given, core_swap)
    kept = kept + permute(kept, y_pair)
    other = permute(kept, core_swap)
    return jnp.where(
        core == 0,
        jnp.concatenate([kept, other], axis=0),
        jnp.concatenate([other, kept], axis=0),
    )


def gather_loop(own, loop):
    low, core = loop // 2, loop % 2
    across = permute(own, y_pair)
    own_other = permute(own, core_swap)
    across_other = permute(across, core_swap)
    same = jnp.where(
        core == 0, jnp.stack([own, own_other]), jnp.stack([own_other, own])
    )
    far = jnp.where(
        core == 0, jnp.stack([across, across_other]), jnp.stack([across_other, across])
    )
    whole = jnp.where(low == 0, jnp.stack([same, far]), jnp.stack([far, same]))
    feats = own.shape[1]
    return jnp.transpose(whole.reshape(-1, feats, TILE), (1, 0, 2)).reshape(feats, -1)


def per_device(features, weight, cotangent, tiles, tile_rows, tile_cols, counts):
    feats, shard_nodes = features.shape
    loop = lax.axis_index("loop")
    wide = lax.axis_index("wide")
    nrow = shard_nodes // TILE
    tile_collection = tiles.reshape(SLOTS, TILE, TILE)
    plan = make_plan(
        tile_rows.reshape(SLOTS), tile_cols.reshape(SLOTS), counts.reshape(1), loop, wide
    )

    near, apart = gather_features(features, loop)
    pairs = pair_tiles(after(counts.reshape(1), near[0], near[4]), tile_collection)
    partial = forward_part(0, plan, pairs, near, None, nrow)
    far = [permute(after(apart[2], pairs), z_up), permute(after(apart[5], pairs), x_up)]
    partial = forward_part(1, plan, pairs, apart, partial, nrow)
    partial = forward_part(2, plan, pairs, far, partial, nrow)
    gathered = sum_over_loop(partial, loop).reshape(shard_nodes, feats)
    aggregated = lax.dot_general(
        weight, gathered, (((0,), (1,)), ((), ())), precision=HI, preferred_element_type=jnp.float32
    )
    activated, pull = jax.vjp(jax.nn.gelu, aggregated)
    slope = pull(cotangent)[0]
    weight_term = lax.dot_general(
        gathered, slope, (((0,), (1,)), ((), ())), precision=HI, preferred_element_type=jnp.float32
    )
    spread = jnp.dot(weight, slope, precision=HI, preferred_element_type=jnp.float32)
    apart_far = backward_part(2, plan, pairs, spread)
    apart = backward_part(1, plan, pairs, after(spread, *apart_far))
    own = backward_part(0, plan, pairs, after(spread, *apart))
    input_cols, weight_grad = scatter_terms(own, apart, apart_far, weight_term)
    input_grad = gather_loop(input_cols, loop)
    return (activated, input_grad, weight_grad)


def solution(mesh):
    return jax.shard_map(
        per_device,
        mesh=mesh,
        in_specs=(
            P(None, "wide"),
            P(),
            P(None, "wide"),
            P("loop", "wide", None, None, None),
            P("loop", "wide", None),
            P("loop", "wide", None),
            P("loop", "wide"),
        ),
        out_specs=(P(None, "wide"), P(None, "wide"), P()),
        check_vma=False,
    )
```

```python
import functools

import jax
import jax.numpy as jnp
from jax import lax
from jax.experimental import pallas as pl
from jax.experimental.pallas import tpu as pltpu
from jax.sharding import PartitionSpec as P

HI = lax.Precision.HIGHEST
GELU_SCALE = 0.7978845608028654
GELU_CUBE = 0.044715
AXES = ("loop", "wide")
SIDE = 4
TILE = 128
SLOTS = 256
GROUP = 16
CHUNK = 32
STAGES = 4
PAIR_BYTES = 30 * 1024 * 1024
PER = 8
CLASS_BUFFERS = (8, 6, 2)
CORE = 4
LOW = 5
VMEM_BYTES = 8 * 1024 * 1024


def device_index(y, core, x, z):
    y, x, z = y % SIDE, x % SIDE, z % SIDE
    return (((y & 1) * 2 + core) * 2 + (y >> 1)) * 16 + x * SIDE + z


def permute(value, move):
    pairs = []
    for y in range(SIDE):
        for core in range(2):
            for x in range(SIDE):
                for z in range(SIDE):
                    pairs.append((device_index(y, core, x, z), device_index(*move(y, core, x, z))))
    return lax.ppermute(value, AXES, pairs)


def toward(core):
    return 1 - 2 * core


def x_up(y, core, x, z):
    return (y, core, x + toward(core), z)


def x_down(y, core, x, z):
    return (y, core, x - toward(core), z)


def z_up(y, core, x, z):
    return (y, core, x, z + toward(core))


def z_down(y, core, x, z):
    return (y, core, x, z - toward(core))


def y_partner(y, core, x, z):
    return (3 - y, core, x, z)


def y_pair(y, core, x, z):
    return (y ^ 1, core, x, z)


def y_far(y, core, x, z):
    return (y + 2, core, x, z)


def core_swap(y, core, x, z):
    return (y, 1 - core, x, z)


def after(value, *others):
    return lax.optimization_barrier((value,) + others)[0]


def split_high_low(value):
    high = value.astype(jnp.bfloat16)
    low = (value - high.astype(jnp.float32)).astype(jnp.bfloat16)
    return high, low


def pair_kernel(count_ref, tiles_ref, out_ref, held, sems):
    count = count_ref[0]

    def copy(chunk):
        source = tiles_ref.at[pl.ds(chunk * CHUNK, CHUNK)]
        return pltpu.make_async_copy(source, held.at[chunk % STAGES], sems.at[chunk % STAGES])

    def when_live(chunk):
        return pl.when(chunk * CHUNK < count)

    for chunk in range(STAGES):
        when_live(chunk)(copy(chunk).start)
    for chunk in range(SLOTS // CHUNK):

        @when_live(chunk)
        def _():
            copy(chunk).wait()

            @pl.loop(0, CHUNK, unroll=8)
            def _(j):
                high, low = split_high_low(held[chunk % STAGES, j])
                out_ref[chunk * CHUNK + j, :, :TILE] = high
                out_ref[chunk * CHUNK + j, :, TILE:] = low

            if chunk + STAGES < SLOTS // CHUNK:
                when_live(chunk + STAGES)(copy(chunk + STAGES).start)


def pair_tiles(count, tiles):
    return pl.pallas_call(
        pair_kernel,
        name="pair_tiles",
        out_shape=pltpu.VMEM((SLOTS, TILE, 2 * TILE), jnp.bfloat16),
        in_specs=[smem(), anywhere()],
        out_specs=vmem(),
        scratch_shapes=[
            pltpu.VMEM((STAGES, CHUNK, TILE, TILE), jnp.float32),
            pltpu.SemaphoreType.DMA((STAGES,)),
        ],
        cost_estimate=cost(8),
        compiler_params=pltpu.CompilerParams(vmem_limit_bytes=PAIR_BYTES),
    )(count, tiles)


def class_range(bounds_ref, which):
    begin, end = bounds_ref[which], bounds_ref[which + 1]
    return begin, end, (end - begin + GROUP - 1) // GROUP


def forward_kernel(which, bounds_ref, order_ref, rows_ref, slots_ref, tiles_ref, *rest):
    number = CLASS_BUFFERS[which]
    base = sum(CLASS_BUFFERS[:which]) * PER
    buffers = rest[:number]
    rest = rest[number:]
    prior_ref = rest[0] if which else None
    pairs, total = rest[-2:]
    nrow = total.shape[0] - 1
    begin, end, groups = class_range(bounds_ref, which)
    if which:
        total[0:nrow] = prior_ref[...]
    else:
        total[0:nrow] = jnp.zeros((nrow, TILE, TILE), jnp.float32)
    for index in range(number):

        @pl.loop(0, PER, unroll=4)
        def _(j):
            high, low = split_high_low(buffers[index][j])
            pairs[index * PER + j, :, :TILE] = high
            pairs[index * PER + j, :, TILE:] = low

    @pl.loop(0, groups)
    def _(group):
        for j in range(GROUP):
            spot = group * GROUP + j
            place = jnp.minimum(begin + spot, SLOTS - 1)
            live = begin + spot < end
            row = jnp.where(live, rows_ref[place], nrow)
            slot = jnp.where(live, slots_ref[place] - base, 0)
            right = pairs[slot]
            product = jnp.dot(
                tiles_ref[order_ref[place]],
                jnp.concatenate([right, right], axis=0),
                preferred_element_type=jnp.float32,
            )
            total[row] += product[:, :TILE] + product[:, TILE:]

    if which == len(CLASS_BUFFERS) - 1:
        kept_ref, given_ref = rest[-4:-2]
        core = bounds_ref[CORE]
        half = nrow // 2
        kept_ref[...] = total[pl.ds(core * half, half)]
        given_ref[...] = total[pl.ds((1 - core) * half, half)]
    else:
        rest[-3][...] = total[0:nrow]


def backward_kernel(which, bounds_ref, order_ref, rows_ref, slots_ref, tiles_ref, slope_ref, *rest):
    number = CLASS_BUFFERS[which]
    base = sum(CLASS_BUFFERS[:which]) * PER
    buffers = rest[:number]
    pairs, total, out_sems = rest[number:]
    begin, end, groups = class_range(bounds_ref, which)
    for row in range(pairs.shape[0]):
        high, low = split_high_low(slope_ref[:, row * TILE : (row + 1) * TILE])
        pairs[row, :, :TILE] = high
        pairs[row, :, TILE:] = low

    @pl.loop(0, number * PER, unroll=4)
    def _(slot):
        total[slot] = jnp.zeros((TILE, TILE), jnp.float32)

    @pl.loop(0, groups)
    def _(group):
        for j in range(GROUP):
            spot = group * GROUP + j
            place = jnp.minimum(begin + spot, SLOTS - 1)
            live = begin + spot < end
            slot = jnp.where(live, slots_ref[place] - base, number * PER)
            right = tiles_ref[order_ref[place]]
            product = jnp.dot(
                pairs[rows_ref[place]],
                jnp.concatenate([right, right], axis=0),
                preferred_element_type=jnp.float32,
            )
            total[slot] += product[:, :TILE] + product[:, TILE:]

    copies = []
    for index in range(number):
        copy = pltpu.make_async_copy(
            total.at[pl.ds(index * PER, PER)], buffers[index], out_sems.at[index]
        )
        copy.start()
        copies.append(copy)
    for copy in copies:
        copy.wait()


def smem():
    return pl.BlockSpec(memory_space=pltpu.SMEM)


def vmem():
    return pl.BlockSpec(memory_space=pltpu.VMEM)


def anywhere():
    return pl.BlockSpec(memory_space=pl.ANY)


def cost(microseconds):
    return pl.CostEstimate(
        flops=int(microseconds * 1.1e9), bytes_accessed=1 << 20, transcendentals=0
    )


def forward_part(which, plan, tiles, buffers, prior, nrow):
    extra = [prior] if which else []
    number = CLASS_BUFFERS[which]
    out_shape = [jax.ShapeDtypeStruct((nrow, TILE, TILE), jnp.float32)]
    if which == len(CLASS_BUFFERS) - 1:
        out_shape = [jax.ShapeDtypeStruct((nrow // 2, TILE, TILE), jnp.float32)] * 2
    return pl.pallas_call(
        functools.partial(forward_kernel, which),
        name="forward_tiles_%d" % which,
        out_shape=out_shape,
        in_specs=[smem()] * 4 + [vmem()] * (1 + number + len(extra)),
        out_specs=[vmem()] * len(out_shape),
        scratch_shapes=[
            pltpu.VMEM((number * PER, TILE, 2 * TILE), jnp.bfloat16),
            pltpu.VMEM((nrow + 1, TILE, TILE), jnp.float32),
        ],
        cost_estimate=cost((6, 5, 2)[which]),
        compiler_params=pltpu.CompilerParams(vmem_limit_bytes=VMEM_BYTES),
    )(*plan, tiles, *buffers, *extra)


def backward_part(which, plan, tiles, slope):
    number = CLASS_BUFFERS[which]
    return pl.pallas_call(
        functools.partial(backward_kernel, which),
        name="backward_tiles_%d" % which,
        out_shape=[jax.ShapeDtypeStruct((PER, TILE, TILE), jnp.float32)] * number,
        in_specs=[smem()] * 4 + [vmem(), vmem()],
        out_specs=[anywhere()] * number,
        scratch_shapes=[
            pltpu.VMEM((slope.shape[1] // TILE, TILE, 2 * TILE), jnp.bfloat16),
            pltpu.VMEM((number * PER + 1, TILE, TILE), jnp.float32),
            pltpu.SemaphoreType.DMA((number,)),
        ],
        cost_estimate=cost((6, 5, 2)[which]),
        compiler_params=pltpu.CompilerParams(vmem_limit_bytes=VMEM_BYTES),
    )(*plan, tiles, slope)


def middle_kernel(
    bounds_ref, across_ref, weight_ref, cotangent_ref, kept_ref, other_ref, pairs_ref,
    activated_ref, spread_ref, weight_term_ref,
):
    core = bounds_ref[CORE]
    half = kept_ref.shape[0]
    weight_term = jnp.zeros((TILE, TILE), jnp.float32)
    for source, place in ((kept_ref, core), (other_ref, 1 - core)):
        for j in range(half):
            columns = pl.ds(pl.multiple_of((place * half + j) * TILE, TILE), TILE)
            block = source[j]
            value = lax.dot_general(
                across_ref[...],
                block,
                (((1,), (1,)), ((), ())),
                precision=HI,
                preferred_element_type=jnp.float32,
            )
            square = value * value
            bend = jnp.tanh(GELU_SCALE * (value + GELU_CUBE * (square * value)))
            activated_ref[:, columns] = 0.5 * value * (1.0 + bend)
            rate = 0.5 * (1.0 + bend) + 0.5 * value * (1.0 - bend * bend) * (
                GELU_SCALE * (1.0 + 3.0 * GELU_CUBE * square)
            )
            slope = cotangent_ref[:, columns] * rate
            weight_term += jnp.dot(
                slope, block, precision=HI, preferred_element_type=jnp.float32
            )
            spread_ref[:, columns] = jnp.dot(
                weight_ref[...], slope, precision=HI, preferred_element_type=jnp.float32
            )
    weight_term_ref[...] = jnp.transpose(weight_term)


def middle_part(bounds, across, weight, cotangent, kept, other, pairs):
    return pl.pallas_call(
        middle_kernel,
        name="middle",
        out_shape=[
            jax.ShapeDtypeStruct(cotangent.shape, jnp.float32),
            jax.ShapeDtypeStruct(cotangent.shape, jnp.float32),
            jax.ShapeDtypeStruct(weight.shape, jnp.float32),
        ],
        in_specs=[smem()] + [vmem()] * 6,
        out_specs=[vmem()] * 3,
        cost_estimate=cost(4),
        compiler_params=pltpu.CompilerParams(vmem_limit_bytes=VMEM_BYTES),
    )(bounds, across, weight, cotangent, kept, other, pairs)


def assemble_kernel(bounds_ref, own_ref, own_other_ref, across_ref, across_other_ref, out_ref):
    core, low = bounds_ref[CORE], bounds_ref[LOW]
    for source, chip, side in (
        (own_ref, low, core),
        (own_other_ref, low, 1 - core),
        (across_ref, 1 - low, core),
        (across_other_ref, 1 - low, 1 - core),
    ):
        for j in range(source.shape[0]):
            place = (chip * 2 + side) * source.shape[0] + j
            out_ref[:, pl.ds(pl.multiple_of(place * TILE, TILE), TILE)] = source[j]


def assemble(bounds, parts):
    return pl.pallas_call(
        assemble_kernel,
        name="assemble",
        out_shape=jax.ShapeDtypeStruct((TILE, 4 * parts[0].shape[0] * TILE), jnp.float32),
        in_specs=[smem()] + [vmem()] * 4,
        out_specs=vmem(),
        compiler_params=pltpu.CompilerParams(vmem_limit_bytes=VMEM_BYTES),
    )(bounds, *parts)


def make_plan(rows, cols, count, loop, wide):
    sign = 1 - 2 * (loop % 2)
    node_block = cols // 4
    part = cols % 4
    across = (node_block // 16) ^ (wide // 16)
    dx = ((node_block // 4 - wide // 4) * sign) % 4
    dz = ((node_block - wide) * sign) % 4
    is_first = part < 2
    ring = jnp.where(is_first, dz, dx)
    inner = jnp.where(is_first, dx * 2 + part, dz * 2 + part - 2)
    near = jnp.where(is_first, 0, 4) + ring
    apart = jnp.where(is_first, 8, 11) + jnp.where(ring == 3, 2, ring)
    apart = jnp.where(ring == 2, jnp.where(is_first, 14, 15), apart)
    buffer = jnp.where(across == 0, near, apart)
    slots = buffer * PER + inner
    spots = jnp.arange(SLOTS, dtype=jnp.int32)
    kind = jnp.where(buffer < 8, 0, jnp.where(buffer < 14, 1, 2))
    kind = jnp.where(spots < count[0], kind, 3)
    ahead = (kind[None, :] < kind[:, None]) | (
        (kind[None, :] == kind[:, None]) & (spots[None, :] < spots[:, None])
    )
    rank = jnp.sum(ahead.astype(jnp.int32), axis=1)
    here = rank[None, :] == spots[:, None]

    def sort(values):
        return jnp.sum(jnp.where(here, values[None, :], 0), axis=1)

    steps = jnp.arange(8, dtype=jnp.int32)
    bounds = jnp.sum((kind[None, :] < steps[:, None]).astype(jnp.int32), axis=1)
    bounds = jnp.where(steps == CORE, loop % 2, jnp.where(steps == LOW, loop // 2, bounds))
    return bounds, sort(spots), sort(rows), sort(slots)


def reduce_ring(parts, up, down, near):
    if near:
        one = parts[1] + permute(parts[2], up)
        three = parts[3]
    else:
        one = parts[1]
        three = parts[3] + permute(parts[2], down)
    return parts[0] + permute(one, up) + permute(three, down)


def quarter_tiles(features, index):
    feats = features.shape[0]
    split = features.reshape(feats, 4, 4, TILE)
    piece = lax.dynamic_index_in_dim(split, index, 1, keepdims=False)
    return jnp.transpose(piece, (1, 2, 0))


def gather_features(features, loop):
    own = quarter_tiles(features, loop)
    partner = permute(quarter_tiles(features, loop ^ 2), y_partner)
    row_one, row_three = permute(own[:2], x_down), permute(own[:2], x_up)
    column_one, column_three = permute(own[2:], z_down), permute(own[2:], z_up)
    row_two, column_two = permute(row_one, x_down), permute(column_one, z_down)
    row = jnp.concatenate([own[:2], row_one, row_two, row_three], axis=0)
    column = jnp.concatenate([own[2:], column_one, column_two, column_three], axis=0)
    return row, column, partner


def gather_near(row, column):
    first_one, second_one = permute(row, z_down), permute(column, x_down)
    first_three, second_three = permute(row, z_up), permute(column, x_up)
    first_two, second_two = permute(first_one, z_down), permute(second_one, x_down)
    return [row, first_one, first_two, first_three, column, second_one, second_two, second_three]


def gather_apart(near, partner, pairs):
    row_sent = permute(near[0][2:], y_far)
    column_sent = permute(after(near[4][2:], row_sent, pairs), y_far)
    row = jnp.concatenate([partner[:2], row_sent], axis=0)
    column = jnp.concatenate([partner[2:], column_sent], axis=0)
    first_three = permute(after(row, near[3]), z_up)
    second_three = permute(after(column, near[7]), x_up)
    first_one = permute(after(row, near[2]), z_down)
    second_one = permute(after(column, near[6]), x_down)
    return [row, first_one, first_three, column, second_one, second_three]


def scatter_terms(own, apart, apart_far, weight_term):
    row_sent = permute(apart_far[0], z_down)
    column_sent = permute(apart_far[1], x_down)
    weight_term = flip_add(after(weight_term, row_sent, apart[0]), "x", 1)
    row_one, column_one = permute(apart[1], z_up), permute(apart[4], x_up)
    row_three = permute(apart[2] + row_sent, z_down)
    column_three = permute(apart[5] + column_sent, x_down)
    weight_term = flip_add(after(weight_term, row_one), "x", 2)

    own_two = permute(after(own[2], row_one), z_up)
    own_column_two = permute(after(own[6], column_one), x_up)
    own_three = permute(after(own[3], row_three), z_down)
    own_column_three = permute(after(own[7], column_three), x_down)
    own_one = permute(own[1] + own_two, z_up)
    own_column_one = permute(own[5] + own_column_two, x_up)

    row = apart[0] + row_one + row_three
    column = apart[3] + column_one + column_three
    weight_term = flip_add(after(weight_term, row_three), "z", 1)
    row_far = permute(row[2:], y_far)
    column_far = permute(after(column[2:], row_far), y_far)
    weight_term = flip_add(after(weight_term, row_far), "z", 2)
    last_far = permute(jnp.concatenate([row[:2], column[:2]], axis=0), y_far)

    row = own[0] + own_one + own_three
    column = own[4] + own_column_one + own_column_three
    rows = [row[:2]] + [row[2 * i : 2 * i + 2] + row_far[2 * i - 2 : 2 * i] for i in (1, 2, 3)]
    columns = [column[:2]] + [
        column[2 * i : 2 * i + 2] + column_far[2 * i - 2 : 2 * i] for i in (1, 2, 3)
    ]
    half = reduce_ring(rows, x_up, x_down, True)
    other = reduce_ring(columns, z_up, z_down, True)
    weight_term = after(weight_term, column_far)
    weight_term = weight_term + permute(weight_term, y_far)
    return jnp.concatenate([half, other], axis=0) + last_far, weight_term


def flip_add(value, axis, step):
    if axis == "x":
        return value + permute(value, lambda y, c, x, z: (y, c, x ^ step, z))
    return value + permute(value, lambda y, c, x, z: (y, c, x, z ^ step))


def per_device(features, weight, cotangent, tiles, tile_rows, tile_cols, counts):
    nrow = features.shape[1] // TILE
    loop = lax.axis_index("loop")
    wide = lax.axis_index("wide")
    tile_collection = tiles.reshape(SLOTS, TILE, TILE)
    count = counts.reshape(1)
    plan = make_plan(tile_rows.reshape(SLOTS), tile_cols.reshape(SLOTS), count, loop, wide)
    across = weight.T

    row, column, partner = gather_features(features, loop)
    near = gather_near(row, column)
    plan, count, across = lax.optimization_barrier((plan, count, across, row, column))[:3]
    pairs = pair_tiles(count, tile_collection)
    apart = gather_apart(near, partner, pairs)
    partial = forward_part(0, plan, pairs, near, None, nrow)
    far = [permute(after(apart[2], *partial), z_up), permute(after(apart[5], *partial), x_up)]
    partial = forward_part(1, plan, pairs, apart, partial[0], nrow)
    kept, given = forward_part(2, plan, pairs, far, partial[0], nrow)

    kept = kept + permute(given, core_swap)
    kept = kept + permute(kept, y_pair)
    other = permute(kept, core_swap)
    activated, spread, weight_term = middle_part(
        plan[0], across, weight, cotangent, kept, other, pairs
    )
    apart_far = backward_part(2, plan, pairs, spread)
    apart = backward_part(1, plan, pairs, after(spread, *apart_far))
    own = backward_part(0, plan, pairs, after(spread, *apart))
    total, weight_grad = scatter_terms(own, apart, apart_far, weight_term)
    far_total = permute(total, y_pair)
    parts = [total, permute(total, core_swap), far_total, permute(far_total, core_swap)]
    return (activated, assemble(plan[0], parts), weight_grad)


def solution(mesh):
    return jax.shard_map(
        per_device,
        mesh=mesh,
        in_specs=(
            P(None, "wide"),
            P(),
            P(None, "wide"),
            P("loop", "wide", None, None, None),
            P("loop", "wide", None),
            P("loop", "wide", None),
            P("loop", "wide"),
        ),
        out_specs=(P(None, "wide"), P(None, "wide"), P()),
        check_vma=False,
    )
```

```python
import functools

import jax
import jax.numpy as jnp
from jax import lax
from jax.experimental import pallas as pl
from jax.experimental.pallas import tpu as pltpu
from jax.sharding import PartitionSpec as P

HI = lax.Precision.HIGHEST
GELU_SCALE = 0.7978845608028654
GELU_CUBE = 0.044715
AXES = ("loop", "wide")
SIDE = 4
TILE = 128
SLOTS = 256
GROUP = 16
CHUNK = 32
STAGES = 4
PAIR_BYTES = 30 * 1024 * 1024
PER = 8
CLASS_BUFFERS = (8, 6, 2)
CORE = 4
LOW = 5
VMEM_BYTES = 8 * 1024 * 1024


def device_index(y, core, x, z):
    y, x, z = y % SIDE, x % SIDE, z % SIDE
    return (((y & 1) * 2 + core) * 2 + (y >> 1)) * 16 + x * SIDE + z


def permute(value, move):
    pairs = []
    for y in range(SIDE):
        for core in range(2):
            for x in range(SIDE):
                for z in range(SIDE):
                    pairs.append((device_index(y, core, x, z), device_index(*move(y, core, x, z))))
    return lax.ppermute(value, AXES, pairs)


def toward(core):
    return 1 - 2 * core


def x_up(y, core, x, z):
    return (y, core, x + toward(core), z)


def x_down(y, core, x, z):
    return (y, core, x - toward(core), z)


def z_up(y, core, x, z):
    return (y, core, x, z + toward(core))


def z_down(y, core, x, z):
    return (y, core, x, z - toward(core))


def y_partner(y, core, x, z):
    return (3 - y, core, x, z)


def y_pair(y, core, x, z):
    return (y ^ 1, core, x, z)


def y_far(y, core, x, z):
    return (y + 2, core, x, z)


def core_swap(y, core, x, z):
    return (y, 1 - core, x, z)


def tie(*values):
    return lax.optimization_barrier(values)


def split_high_low(value):
    high = value.astype(jnp.bfloat16)
    low = (value - high.astype(jnp.float32)).astype(jnp.bfloat16)
    return high, low


def pair_kernel(count_ref, tiles_ref, out_ref, held, sems):
    count = count_ref[0]

    def copy(chunk):
        source = tiles_ref.at[pl.ds(chunk * CHUNK, CHUNK)]
        return pltpu.make_async_copy(source, held.at[chunk % STAGES], sems.at[chunk % STAGES])

    def when_live(chunk):
        return pl.when(chunk * CHUNK < count)

    for chunk in range(STAGES):
        when_live(chunk)(copy(chunk).start)
    for chunk in range(SLOTS // CHUNK):

        @when_live(chunk)
        def _():
            copy(chunk).wait()

            @pl.loop(0, CHUNK, unroll=8)
            def _(j):
                high, low = split_high_low(held[chunk % STAGES, j])
                out_ref[chunk * CHUNK + j, :, :TILE] = high
                out_ref[chunk * CHUNK + j, :, TILE:] = low

            if chunk + STAGES < SLOTS // CHUNK:
                when_live(chunk + STAGES)(copy(chunk + STAGES).start)


def pair_tiles(count, tiles):
    return pl.pallas_call(
        pair_kernel,
        name="pair_tiles",
        out_shape=pltpu.VMEM((SLOTS, TILE, 2 * TILE), jnp.bfloat16),
        in_specs=[smem(), anywhere()],
        out_specs=vmem(),
        scratch_shapes=[
            pltpu.VMEM((STAGES, CHUNK, TILE, TILE), jnp.float32),
            pltpu.SemaphoreType.DMA((STAGES,)),
        ],
        cost_estimate=cost(8),
        compiler_params=pltpu.CompilerParams(vmem_limit_bytes=PAIR_BYTES),
    )(count, tiles)


def class_range(bounds_ref, which):
    begin, end = bounds_ref[which], bounds_ref[which + 1]
    return begin, end, (end - begin + GROUP - 1) // GROUP


def forward_kernel(which, bounds_ref, order_ref, rows_ref, slots_ref, tiles_ref, *rest):
    number = CLASS_BUFFERS[which]
    base = sum(CLASS_BUFFERS[:which]) * PER
    buffers = rest[:number]
    rest = rest[number:]
    prior_ref = rest[0] if which else None
    pairs, total = rest[-2:]
    nrow = total.shape[0] - 1
    begin, end, groups = class_range(bounds_ref, which)
    if which:
        total[0:nrow] = prior_ref[...]
    else:
        total[0:nrow] = jnp.zeros((nrow, TILE, TILE), jnp.float32)
    for index in range(number):

        @pl.loop(0, PER, unroll=4)
        def _(j):
            high, low = split_high_low(buffers[index][j])
            pairs[index * PER + j, :, :TILE] = high
            pairs[index * PER + j, :, TILE:] = low

    @pl.loop(0, groups)
    def _(group):
        for j in range(GROUP):
            spot = group * GROUP + j
            place = jnp.minimum(begin + spot, SLOTS - 1)
            live = begin + spot < end
            row = jnp.where(live, rows_ref[place], nrow)
            slot = jnp.where(live, slots_ref[place] - base, 0)
            right = pairs[slot]
            product = jnp.dot(
                tiles_ref[order_ref[place]],
                jnp.concatenate([right, right], axis=0),
                preferred_element_type=jnp.float32,
            )
            total[row] += product[:, :TILE] + product[:, TILE:]

    if which == len(CLASS_BUFFERS) - 1:
        core = bounds_ref[CORE]
        part = nrow // 4
        for index, out_ref in enumerate(rest[-6:-2]):
            side = core if index < 2 else 1 - core
            out_ref[...] = total[pl.ds((side * 2 + index % 2) * part, part)]
    else:
        rest[-3][...] = total[0:nrow]


def backward_kernel(which, bounds_ref, order_ref, rows_ref, slots_ref, tiles_ref, slope_ref, *rest):
    number = CLASS_BUFFERS[which]
    base = sum(CLASS_BUFFERS[:which]) * PER
    buffers = rest[:number]
    total, out_sems = rest[number:]
    begin, end, groups = class_range(bounds_ref, which)
    @pl.loop(0, number * PER, unroll=4)
    def _(slot):
        total[slot] = jnp.zeros((TILE, TILE), jnp.float32)

    @pl.loop(0, groups)
    def _(group):
        for j in range(GROUP):
            spot = group * GROUP + j
            place = jnp.minimum(begin + spot, SLOTS - 1)
            live = begin + spot < end
            slot = jnp.where(live, slots_ref[place] - base, number * PER)
            right = tiles_ref[order_ref[place]]
            product = jnp.dot(
                slope_ref[rows_ref[place]],
                jnp.concatenate([right, right], axis=0),
                preferred_element_type=jnp.float32,
            )
            total[slot] += product[:, :TILE] + product[:, TILE:]

    copies = []
    for index in range(number):
        copy = pltpu.make_async_copy(
            total.at[pl.ds(index * PER, PER)], buffers[index], out_sems.at[index]
        )
        copy.start()
        copies.append(copy)
    for copy in copies:
        copy.wait()


def smem():
    return pl.BlockSpec(memory_space=pltpu.SMEM)


def vmem():
    return pl.BlockSpec(memory_space=pltpu.VMEM)


def anywhere():
    return pl.BlockSpec(memory_space=pl.ANY)


def cost(microseconds):
    return pl.CostEstimate(
        flops=int(microseconds * 1.1e9), bytes_accessed=1 << 20, transcendentals=0
    )


def forward_part(which, plan, tiles, buffers, prior, nrow):
    extra = [prior] if which else []
    number = CLASS_BUFFERS[which]
    out_shape = [jax.ShapeDtypeStruct((nrow, TILE, TILE), jnp.float32)]
    if which == len(CLASS_BUFFERS) - 1:
        out_shape = [jax.ShapeDtypeStruct((nrow // 4, TILE, TILE), jnp.float32)] * 4
    return pl.pallas_call(
        functools.partial(forward_kernel, which),
        name="forward_tiles_%d" % which,
        out_shape=out_shape,
        in_specs=[smem()] * 4 + [vmem()] * (1 + number + len(extra)),
        out_specs=[vmem()] * len(out_shape),
        scratch_shapes=[
            pltpu.VMEM((number * PER, TILE, 2 * TILE), jnp.bfloat16),
            pltpu.VMEM((nrow + 1, TILE, TILE), jnp.float32),
        ],
        cost_estimate=cost((6, 5, 2)[which]),
        compiler_params=pltpu.CompilerParams(vmem_limit_bytes=VMEM_BYTES),
    )(*plan, tiles, *buffers, *extra)


def backward_part(which, plan, tiles, slope):
    number = CLASS_BUFFERS[which]
    return pl.pallas_call(
        functools.partial(backward_kernel, which),
        name="backward_tiles_%d" % which,
        out_shape=[jax.ShapeDtypeStruct((PER, TILE, TILE), jnp.float32)] * number,
        in_specs=[smem()] * 4 + [vmem(), vmem()],
        out_specs=[anywhere()] * number,
        scratch_shapes=[
            pltpu.VMEM((number * PER + 1, TILE, TILE), jnp.float32),
            pltpu.SemaphoreType.DMA((number,)),
        ],
        cost_estimate=cost((6, 5, 2)[which]),
        compiler_params=pltpu.CompilerParams(vmem_limit_bytes=VMEM_BYTES),
    )(*plan, tiles, slope)


def triple_left(value):
    high, low = split_high_low(value)
    return jnp.concatenate([high, low, high], axis=1)


def triple_right(value, axis):
    high, low = split_high_low(value)
    return jnp.concatenate([high, high, low], axis=axis)


def middle_kernel(which, bounds_ref, across_ref, weight_ref, cotangent_ref, *rest):
    kept_ref, other_ref = rest[0:2]
    core = bounds_ref[CORE]
    part = kept_ref.shape[0]
    across = triple_left(across_ref[...])
    weight = triple_left(weight_ref[...])
    if which == 0:
        activated_ref, spread_ref, weight_term_ref = rest[-3:]
        weight_term = jnp.zeros((TILE, TILE), jnp.float32)
    else:
        early_activated_ref, early_spread_ref, early_term_ref = rest[3:6]
        activated_ref, spread_ref, weight_term_ref = rest[-3:]
        weight_term = early_term_ref[...]
    for index in range(2 * part):
        source = kept_ref if index < part else other_ref
        side = core if index < part else 1 - core
        row = (side * 2 + which) * part + index % part
        columns = pl.ds(pl.multiple_of(row * TILE, TILE), TILE)
        block = source[index % part]
        value = lax.dot_general(
            across,
            triple_right(block, 1),
            (((1,), (1,)), ((), ())),
            preferred_element_type=jnp.float32,
        )
        square = value * value
        bend = jnp.tanh(GELU_SCALE * (value + GELU_CUBE * (square * value)))
        activated = 0.5 * value * (1.0 + bend)
        rate = 0.5 * (1.0 + bend) + 0.5 * value * (1.0 - bend * bend) * (
            GELU_SCALE * (1.0 + 3.0 * GELU_CUBE * square)
        )
        slope = cotangent_ref[:, columns] * rate
        weight_term += jnp.dot(
            triple_left(slope), triple_right(block, 0), preferred_element_type=jnp.float32
        )
        spread = jnp.dot(weight, triple_right(slope, 0), preferred_element_type=jnp.float32)
        high, low = split_high_low(spread)
        if which == 0:
            activated_ref[index] = activated
            spread_ref[index, :, :TILE] = high
            spread_ref[index, :, TILE:] = low
        else:
            activated_ref[:, columns] = activated
            spread_ref[row, :, :TILE] = high
            spread_ref[row, :, TILE:] = low
            early = side * 2 * part + index % part
            early_columns = pl.ds(pl.multiple_of(early * TILE, TILE), TILE)
            activated_ref[:, early_columns] = early_activated_ref[index]
            spread_ref[early] = early_spread_ref[index]
    weight_term_ref[...] = jnp.transpose(weight_term) if which else weight_term


def middle_part(which, bounds, across, weight, cotangent, kept, other, pairs, early=()):
    part = kept.shape[0]
    rows = 4 * part if which else 2 * part
    activated = cotangent.shape if which else (rows, TILE, TILE)
    return pl.pallas_call(
        functools.partial(middle_kernel, which),
        name="middle_%d" % which,
        out_shape=[
            jax.ShapeDtypeStruct(activated, jnp.float32),
            jax.ShapeDtypeStruct((rows, TILE, 2 * TILE), jnp.bfloat16),
            jax.ShapeDtypeStruct(weight.shape, jnp.float32),
        ],
        in_specs=[smem()] + [vmem()] * (6 + len(early)),
        out_specs=[vmem()] * 3,
        cost_estimate=cost(2),
        compiler_params=pltpu.CompilerParams(vmem_limit_bytes=VMEM_BYTES),
    )(bounds, across, weight, cotangent, kept, other, pairs, *early)


def assemble_kernel(bounds_ref, own_ref, own_other_ref, across_ref, across_other_ref, out_ref):
    core, low = bounds_ref[CORE], bounds_ref[LOW]
    for source, chip, side in (
        (own_ref, low, core),
        (own_other_ref, low, 1 - core),
        (across_ref, 1 - low, core),
        (across_other_ref, 1 - low, 1 - core),
    ):
        for j in range(source.shape[0]):
            place = (chip * 2 + side) * source.shape[0] + j
            out_ref[:, pl.ds(pl.multiple_of(place * TILE, TILE), TILE)] = source[j]


def assemble(bounds, parts):
    return pl.pallas_call(
        assemble_kernel,
        name="assemble",
        out_shape=jax.ShapeDtypeStruct((TILE, 4 * parts[0].shape[0] * TILE), jnp.float32),
        in_specs=[smem()] + [vmem()] * 4,
        out_specs=vmem(),
        compiler_params=pltpu.CompilerParams(vmem_limit_bytes=VMEM_BYTES),
    )(bounds, *parts)


def make_plan(rows, cols, count, loop, wide):
    sign = 1 - 2 * (loop % 2)
    node_block = cols // 4
    part = cols % 4
    across = (node_block // 16) ^ (wide // 16)
    dx = ((node_block // 4 - wide // 4) * sign) % 4
    dz = ((node_block - wide) * sign) % 4
    is_first = part < 2
    ring = jnp.where(is_first, dz, dx)
    inner = jnp.where(is_first, dx * 2 + part, dz * 2 + part - 2)
    near = jnp.where(is_first, 0, 4) + ring
    apart = jnp.where(is_first, 8, 11) + jnp.where(ring == 3, 2, ring)
    apart = jnp.where(ring == 2, jnp.where(is_first, 14, 15), apart)
    buffer = jnp.where(across == 0, near, apart)
    slots = buffer * PER + inner
    spots = jnp.arange(SLOTS, dtype=jnp.int32)
    kind = jnp.where(buffer < 8, 0, jnp.where(buffer < 14, 1, 2))
    kind = jnp.where(spots < count[0], kind, 3)
    ahead = (kind[None, :] < kind[:, None]) | (
        (kind[None, :] == kind[:, None]) & (spots[None, :] < spots[:, None])
    )
    rank = jnp.sum(ahead.astype(jnp.int32), axis=1)
    here = rank[None, :] == spots[:, None]

    def sort(values):
        return jnp.sum(jnp.where(here, values[None, :], 0), axis=1)

    steps = jnp.arange(8, dtype=jnp.int32)
    bounds = jnp.sum((kind[None, :] < steps[:, None]).astype(jnp.int32), axis=1)
    bounds = jnp.where(steps == CORE, loop % 2, jnp.where(steps == LOW, loop // 2, bounds))
    return bounds, sort(spots), sort(rows), sort(slots)


def reduce_ring(parts, up, down, near):
    if near:
        one = parts[1] + permute(parts[2], up)
        three = parts[3]
    else:
        one = parts[1]
        three = parts[3] + permute(parts[2], down)
    return parts[0] + permute(one, up) + permute(three, down)


def quarter_tiles(features, index):
    feats = features.shape[0]
    split = features.reshape(feats, 4, 4, TILE)
    piece = lax.dynamic_index_in_dim(split, index, 1, keepdims=False)
    return jnp.transpose(piece, (1, 2, 0))


def gather_features(features, loop):
    own = quarter_tiles(features, loop)
    partner = permute(quarter_tiles(features, loop ^ 2), y_partner)
    row_one, row_three = permute(own[:2], x_down), permute(own[:2], x_up)
    column_one, column_three = permute(own[2:], z_down), permute(own[2:], z_up)
    row_two, column_two = permute(row_one, x_down), permute(column_one, z_down)
    row = jnp.concatenate([own[:2], row_one, row_two, row_three], axis=0)
    column = jnp.concatenate([own[2:], column_one, column_two, column_three], axis=0)
    return row, column, partner


def gather_near(row, column):
    first_one, second_one = permute(row, z_down), permute(column, x_down)
    first_three, second_three = permute(row, z_up), permute(column, x_up)
    first_two, second_two = permute(first_one, z_down), permute(second_one, x_down)
    return [row, first_one, first_two, first_three, column, second_one, second_two, second_three]


def gather_apart(near, partner):
    near = list(near)
    row_sent = permute(near[0][2:], y_far)
    column, row_sent = tie(near[4], row_sent)
    near[4] = column
    column_sent = permute(column[2:], y_far)
    row = jnp.concatenate([partner[:2], row_sent], axis=0)
    column = jnp.concatenate([partner[2:], column_sent], axis=0)
    row, near[3] = tie(row, near[3])
    first_three = permute(row, z_up)
    row, near[2] = tie(row, near[2])
    first_one = permute(row, z_down)
    column, near[7] = tie(column, near[7])
    second_three = permute(column, x_up)
    column, near[6] = tie(column, near[6])
    second_one = permute(column, x_down)
    return near, [row, first_one, first_three, column, second_one, second_three]


def scatter_terms(plan, pairs, spread, weight_term):
    apart_far = backward_part(2, plan, pairs, spread)
    spread, *apart_far = tie(spread, *apart_far)
    row_sent, column_sent = permute(apart_far[0], z_down), permute(apart_far[1], x_down)
    apart = backward_part(1, plan, pairs, spread)
    row_one, column_one = permute(apart[1], z_up), permute(apart[4], x_up)
    row_back, column_back = apart[2] + row_sent, apart[5] + column_sent
    spread, weight_term, row_back, column_back = tie(spread, weight_term, row_back, column_back)
    row_three, column_three = permute(row_back, z_down), permute(column_back, x_down)
    own = list(backward_part(0, plan, pairs, spread))
    weight_term = flip_add(weight_term, "x", 1)

    own[2], row_one = tie(own[2], row_one)
    own_two = permute(own[2], z_up)
    own[6], column_one = tie(own[6], column_one)
    own_column_two = permute(own[6], x_up)
    own[3], row_three = tie(own[3], row_three)
    own_three = permute(own[3], z_down)
    own[7], column_three = tie(own[7], column_three)
    own_column_three = permute(own[7], x_down)
    weight_term, own_two = tie(weight_term, own_two)
    weight_term = flip_add(weight_term, "x", 2)
    own_one = permute(own[1] + own_two, z_up)
    own_column_one = permute(own[5] + own_column_two, x_up)

    row = apart[0] + row_one + row_three
    column = apart[3] + column_one + column_three
    row_far = permute(row[2:], y_far)
    column, row_far, weight_term = tie(column, row_far, weight_term)
    column_far = permute(column[2:], y_far)
    weight_term = flip_add(weight_term, "z", 1)
    last, column_far, weight_term = tie(
        jnp.concatenate([row[:2], column[:2]], axis=0), column_far, weight_term
    )
    last_far = permute(last, y_far)
    weight_term = flip_add(weight_term, "z", 2)

    row = own[0] + own_one + own_three
    column = own[4] + own_column_one + own_column_three
    rows = [row[:2]] + [row[2 * i : 2 * i + 2] + row_far[2 * i - 2 : 2 * i] for i in (1, 2, 3)]
    columns = [column[:2]] + [
        column[2 * i : 2 * i + 2] + column_far[2 * i - 2 : 2 * i] for i in (1, 2, 3)
    ]
    half = reduce_ring(rows, x_up, x_down, True)
    other = reduce_ring(columns, z_up, z_down, True)
    total = jnp.concatenate([half, other], axis=0) + last_far
    total, weight_term = tie(total, weight_term)
    return total, weight_term + permute(weight_term, y_far)


def flip_add(value, axis, step):
    if axis == "x":
        return value + permute(value, lambda y, c, x, z: (y, c, x ^ step, z))
    return value + permute(value, lambda y, c, x, z: (y, c, x, z ^ step))


def per_device(features, weight, cotangent, tiles, tile_rows, tile_cols, counts):
    nrow = features.shape[1] // TILE
    loop = lax.axis_index("loop")
    wide = lax.axis_index("wide")
    tile_collection = tiles.reshape(SLOTS, TILE, TILE)
    count = counts.reshape(1)
    plan = make_plan(tile_rows.reshape(SLOTS), tile_cols.reshape(SLOTS), count, loop, wide)
    across = weight.T

    row, column, partner = gather_features(features, loop)
    plan, across, row, column = tie(plan, across, row, column)
    near = gather_near(row, column)
    count, near[1], near[5] = tie(count, near[1], near[5])
    pairs = pair_tiles(count, tile_collection)
    near, apart = gather_apart(near, partner)
    partial = forward_part(0, plan, pairs, near, None, nrow)
    apart[2], apart[5], partial = tie(apart[2], apart[5], partial[0])
    far = [permute(apart[2], z_up), permute(apart[5], x_up)]
    partial = forward_part(1, plan, pairs, apart, partial, nrow)
    *kept, given_first, given_second = forward_part(2, plan, pairs, far, partial[0], nrow)

    bounds = plan[0]
    kept = [kept[0] + permute(given_first, core_swap), kept[1] + permute(given_second, core_swap)]
    kept = [value + permute(value, y_pair) for value in kept]
    early = middle_part(
        0, bounds, across, weight, cotangent, kept[0], permute(kept[0], core_swap), pairs
    )
    activated, spread, weight_term = middle_part(
        1, bounds, across, weight, cotangent, kept[1], permute(kept[1], core_swap), pairs, early
    )
    total, weight_grad = scatter_terms(plan, pairs, spread, weight_term)
    far_total = permute(total, y_pair)
    parts = [total, permute(total, core_swap), far_total, permute(far_total, core_swap)]
    return (activated, assemble(bounds, parts), weight_grad)


def solution(mesh):
    return jax.shard_map(
        per_device,
        mesh=mesh,
        in_specs=(
            P(None, "wide"),
            P(),
            P(None, "wide"),
            P("loop", "wide", None, None, None),
            P("loop", "wide", None),
            P("loop", "wide", None),
            P("loop", "wide"),
        ),
        out_specs=(P(None, "wide"), P(None, "wide"), P()),
        check_vma=False,
    )
```

```python
import functools

import jax
import jax.numpy as jnp
from jax import lax
from jax.experimental import pallas as pl
from jax.experimental.pallas import tpu as pltpu
from jax.sharding import PartitionSpec as P

HI = lax.Precision.HIGHEST
GELU_SCALE = 0.7978845608028654
GELU_CUBE = 0.044715
AXES = ("y_lo", "core", "y_hi", "x", "z")
LOOP = ("y_lo", "core")
WIDE = ("y_hi", "x", "z")
SIDE = 4
TILE = 128
SLOTS = 256
GROUP = 16
CHUNK = 32
STAGES = 4
PAIR_BYTES = 30 * 1024 * 1024
PER = 16
HALF = 8
CLASS_SIZES = ((PER, PER, PER, HALF, HALF), (PER, PER, PER), (HALF, HALF))
CORE = 4
LOW = 5
VMEM_BYTES = 8 * 1024 * 1024


def device_index(y, core, x, z):
    y, x, z = y % SIDE, x % SIDE, z % SIDE
    return (((y & 1) * 2 + core) * 2 + (y >> 1)) * 16 + x * SIDE + z


def permute(value, move):
    pairs = []
    for y in range(SIDE):
        for core in range(2):
            for x in range(SIDE):
                for z in range(SIDE):
                    pairs.append((device_index(y, core, x, z), device_index(*move(y, core, x, z))))
    return lax.ppermute(value, AXES, pairs)


def along(first, step):
    def move(y, core, x, z):
        if (core == 0) == first:
            return (y, core, x + step, z)
        return (y, core, x, z + step)

    return move


u_up, u_down, u_far = along(True, 1), along(True, -1), along(True, 2)
v_up, v_down = along(False, 1), along(False, -1)


def y_partner(y, core, x, z):
    return (3 - y, core, x, z)


def y_pair(y, core, x, z):
    return (y ^ 1, core, x, z)


def y_far(y, core, x, z):
    return (y + 2, core, x, z)


def core_swap(y, core, x, z):
    return (y, 1 - core, x, z)


def tie(*values):
    return lax.optimization_barrier(values)


def split_high_low(value):
    high = value.astype(jnp.bfloat16)
    low = (value - high.astype(jnp.float32)).astype(jnp.bfloat16)
    return high, low


def pair_kernel(count_ref, tiles_ref, out_ref, held, sems):
    count = count_ref[0]

    def copy(chunk):
        source = tiles_ref.at[pl.ds(chunk * CHUNK, CHUNK)]
        return pltpu.make_async_copy(source, held.at[chunk % STAGES], sems.at[chunk % STAGES])

    def when_live(chunk):
        return pl.when(chunk * CHUNK < count)

    for chunk in range(STAGES):
        when_live(chunk)(copy(chunk).start)
    for chunk in range(SLOTS // CHUNK):

        @when_live(chunk)
        def _():
            copy(chunk).wait()

            @pl.loop(0, CHUNK, unroll=8)
            def _(j):
                high, low = split_high_low(held[chunk % STAGES, j])
                out_ref[chunk * CHUNK + j, :, :TILE] = high
                out_ref[chunk * CHUNK + j, :, TILE:] = low

            if chunk + STAGES < SLOTS // CHUNK:
                when_live(chunk + STAGES)(copy(chunk + STAGES).start)


def pair_tiles(count, tiles):
    return pl.pallas_call(
        pair_kernel,
        name="pair_tiles",
        out_shape=pltpu.VMEM((SLOTS, TILE, 2 * TILE), jnp.bfloat16),
        in_specs=[smem(), anywhere()],
        out_specs=vmem(),
        scratch_shapes=[
            pltpu.VMEM((STAGES, CHUNK, TILE, TILE), jnp.float32),
            pltpu.SemaphoreType.DMA((STAGES,)),
        ],
        cost_estimate=cost(8),
        compiler_params=pltpu.CompilerParams(vmem_limit_bytes=PAIR_BYTES),
    )(count, tiles)


def class_range(bounds_ref, which):
    begin, end = bounds_ref[which], bounds_ref[which + 1]
    return begin, end, (end - begin + GROUP - 1) // GROUP


def forward_kernel(which, bounds_ref, order_ref, rows_ref, slots_ref, tiles_ref, *rest):
    sizes = CLASS_SIZES[which]
    base = sum(sum(part) for part in CLASS_SIZES[:which])
    buffers = rest[: len(sizes)]
    rest = rest[len(sizes) :]
    prior_ref = rest[0] if which else None
    pairs, total = rest[-2:]
    nrow = total.shape[0] - 1
    begin, end, groups = class_range(bounds_ref, which)
    if which:
        total[0:nrow] = prior_ref[...]
    else:
        total[0:nrow] = jnp.zeros((nrow, TILE, TILE), jnp.float32)
    for index, size in enumerate(sizes):
        first = sum(sizes[:index])

        @pl.loop(0, size, unroll=4)
        def _(j):
            high, low = split_high_low(buffers[index][j])
            pairs[first + j, :, :TILE] = high
            pairs[first + j, :, TILE:] = low

    @pl.loop(0, groups)
    def _(group):
        for j in range(GROUP):
            spot = group * GROUP + j
            place = jnp.minimum(begin + spot, SLOTS - 1)
            live = begin + spot < end
            row = jnp.where(live, rows_ref[place], nrow)
            slot = jnp.where(live, slots_ref[place] - base, 0)
            right = pairs[slot]
            product = jnp.dot(
                tiles_ref[order_ref[place]],
                jnp.concatenate([right, right], axis=0),
                preferred_element_type=jnp.float32,
            )
            total[row] += product[:, :TILE] + product[:, TILE:]

    if which == len(CLASS_SIZES) - 1:
        core = bounds_ref[CORE]
        part = nrow // 4
        for index, out_ref in enumerate(rest[-6:-2]):
            side = core if index < 2 else 1 - core
            out_ref[...] = total[pl.ds((side * 2 + index % 2) * part, part)]
    else:
        rest[-3][...] = total[0:nrow]


def backward_kernel(which, bounds_ref, order_ref, rows_ref, slots_ref, tiles_ref, slope_ref, *rest):
    sizes = CLASS_SIZES[which]
    base = sum(sum(part) for part in CLASS_SIZES[:which])
    buffers = rest[: len(sizes)]
    total, out_sems = rest[len(sizes) :]
    begin, end, groups = class_range(bounds_ref, which)
    @pl.loop(0, sum(sizes), unroll=4)
    def _(slot):
        total[slot] = jnp.zeros((TILE, TILE), jnp.float32)

    @pl.loop(0, groups)
    def _(group):
        for j in range(GROUP):
            spot = group * GROUP + j
            place = jnp.minimum(begin + spot, SLOTS - 1)
            live = begin + spot < end
            slot = jnp.where(live, slots_ref[place] - base, sum(sizes))
            right = tiles_ref[order_ref[place]]
            product = jnp.dot(
                slope_ref[rows_ref[place]],
                jnp.concatenate([right, right], axis=0),
                preferred_element_type=jnp.float32,
            )
            total[slot] += product[:, :TILE] + product[:, TILE:]

    copies = []
    for index, size in enumerate(sizes):
        copy = pltpu.make_async_copy(
            total.at[pl.ds(sum(sizes[:index]), size)], buffers[index], out_sems.at[index]
        )
        copy.start()
        copies.append(copy)
    for copy in copies:
        copy.wait()


def smem():
    return pl.BlockSpec(memory_space=pltpu.SMEM)


def vmem():
    return pl.BlockSpec(memory_space=pltpu.VMEM)


def anywhere():
    return pl.BlockSpec(memory_space=pl.ANY)


def cost(microseconds):
    return pl.CostEstimate(
        flops=int(microseconds * 1.1e9), bytes_accessed=1 << 20, transcendentals=0
    )


def forward_part(which, plan, tiles, buffers, prior, nrow):
    extra = [prior] if which else []
    sizes = CLASS_SIZES[which]
    out_shape = [jax.ShapeDtypeStruct((nrow, TILE, TILE), jnp.float32)]
    if which == len(CLASS_SIZES) - 1:
        out_shape = [jax.ShapeDtypeStruct((nrow // 4, TILE, TILE), jnp.float32)] * 4
    return pl.pallas_call(
        functools.partial(forward_kernel, which),
        name="forward_tiles_%d" % which,
        out_shape=out_shape,
        in_specs=[smem()] * 4 + [vmem()] * (1 + len(sizes) + len(extra)),
        out_specs=[vmem()] * len(out_shape),
        scratch_shapes=[
            pltpu.VMEM((sum(sizes), TILE, 2 * TILE), jnp.bfloat16),
            pltpu.VMEM((nrow + 1, TILE, TILE), jnp.float32),
        ],
        cost_estimate=cost((6, 5, 2)[which]),
        compiler_params=pltpu.CompilerParams(vmem_limit_bytes=VMEM_BYTES),
    )(*plan, tiles, *buffers, *extra)


def backward_part(which, plan, tiles, slope):
    sizes = CLASS_SIZES[which]
    return pl.pallas_call(
        functools.partial(backward_kernel, which),
        name="backward_tiles_%d" % which,
        out_shape=[jax.ShapeDtypeStruct((size, TILE, TILE), jnp.float32) for size in sizes],
        in_specs=[smem()] * 4 + [vmem(), vmem()],
        out_specs=[anywhere()] * len(sizes),
        scratch_shapes=[
            pltpu.VMEM((sum(sizes) + 1, TILE, TILE), jnp.float32),
            pltpu.SemaphoreType.DMA((len(sizes),)),
        ],
        cost_estimate=cost((6, 5, 2)[which]),
        compiler_params=pltpu.CompilerParams(vmem_limit_bytes=VMEM_BYTES),
    )(*plan, tiles, slope)


def triple_left(value):
    high, low = split_high_low(value)
    return jnp.concatenate([high, low, high], axis=1)


def triple_right(value, axis):
    high, low = split_high_low(value)
    return jnp.concatenate([high, high, low], axis=axis)


def middle_kernel(which, bounds_ref, across_ref, weight_ref, cotangent_ref, *rest):
    kept_ref, other_ref = rest[0:2]
    core = bounds_ref[CORE]
    part = kept_ref.shape[0]
    across = triple_left(across_ref[...])
    weight = triple_left(weight_ref[...])
    if which == 0:
        activated_ref, spread_ref, weight_term_ref = rest[-3:]
        weight_term = jnp.zeros((TILE, TILE), jnp.float32)
    else:
        early_activated_ref, early_spread_ref, early_term_ref = rest[3:6]
        activated_ref, spread_ref, weight_term_ref = rest[-3:]
        weight_term = early_term_ref[...]
    for index in range(2 * part):
        source = kept_ref if index < part else other_ref
        side = core if index < part else 1 - core
        row = (side * 2 + which) * part + index % part
        columns = pl.ds(pl.multiple_of(row * TILE, TILE), TILE)
        block = source[index % part]
        value = lax.dot_general(
            across,
            triple_right(block, 1),
            (((1,), (1,)), ((), ())),
            preferred_element_type=jnp.float32,
        )
        square = value * value
        bend = jnp.tanh(GELU_SCALE * (value + GELU_CUBE * (square * value)))
        activated = 0.5 * value * (1.0 + bend)
        rate = 0.5 * (1.0 + bend) + 0.5 * value * (1.0 - bend * bend) * (
            GELU_SCALE * (1.0 + 3.0 * GELU_CUBE * square)
        )
        slope = cotangent_ref[:, columns] * rate
        weight_term += jnp.dot(
            triple_left(slope), triple_right(block, 0), preferred_element_type=jnp.float32
        )
        spread = jnp.dot(weight, triple_right(slope, 0), preferred_element_type=jnp.float32)
        high, low = split_high_low(spread)
        if which == 0:
            activated_ref[index] = activated
            spread_ref[index, :, :TILE] = high
            spread_ref[index, :, TILE:] = low
        else:
            activated_ref[:, columns] = activated
            spread_ref[row, :, :TILE] = high
            spread_ref[row, :, TILE:] = low
            early = side * 2 * part + index % part
            early_columns = pl.ds(pl.multiple_of(early * TILE, TILE), TILE)
            activated_ref[:, early_columns] = early_activated_ref[index]
            spread_ref[early] = early_spread_ref[index]
    weight_term_ref[...] = jnp.transpose(weight_term) if which else weight_term


def middle_part(which, bounds, across, weight, cotangent, kept, other, pairs, early=()):
    part = kept.shape[0]
    rows = 4 * part if which else 2 * part
    activated = cotangent.shape if which else (rows, TILE, TILE)
    return pl.pallas_call(
        functools.partial(middle_kernel, which),
        name="middle_%d" % which,
        out_shape=[
            jax.ShapeDtypeStruct(activated, jnp.float32),
            jax.ShapeDtypeStruct((rows, TILE, 2 * TILE), jnp.bfloat16),
            jax.ShapeDtypeStruct(weight.shape, jnp.float32),
        ],
        in_specs=[smem()] + [vmem()] * (6 + len(early)),
        out_specs=[vmem()] * 3,
        cost_estimate=cost(2),
        compiler_params=pltpu.CompilerParams(vmem_limit_bytes=VMEM_BYTES),
    )(bounds, across, weight, cotangent, kept, other, pairs, *early)


def assemble_kernel(bounds_ref, own_ref, own_other_ref, across_ref, across_other_ref, out_ref):
    core, low = bounds_ref[CORE], bounds_ref[LOW]
    for source, chip, side in (
        (own_ref, low, core),
        (own_other_ref, low, 1 - core),
        (across_ref, 1 - low, core),
        (across_other_ref, 1 - low, 1 - core),
    ):
        for j in range(source.shape[0]):
            place = (chip * 2 + side) * source.shape[0] + j
            out_ref[:, pl.ds(pl.multiple_of(place * TILE, TILE), TILE)] = source[j]


def assemble(bounds, parts):
    return pl.pallas_call(
        assemble_kernel,
        name="assemble",
        out_shape=jax.ShapeDtypeStruct((TILE, 4 * parts[0].shape[0] * TILE), jnp.float32),
        in_specs=[smem()] + [vmem()] * 4,
        out_specs=vmem(),
        compiler_params=pltpu.CompilerParams(vmem_limit_bytes=VMEM_BYTES),
    )(bounds, *parts)


def make_plan(rows, cols, count, loop, wide):
    core = loop % 2
    node_block = cols // 4
    across = (node_block // 16) ^ (wide // 16)
    dx = (node_block // 4 - wide // 4) % 4
    dz = (node_block - wide) % 4
    du = jnp.where(core == 0, dx, dz)
    dv = jnp.where(core == 0, dz, dx)
    place = jnp.where(dv == 2, 3, jnp.where(dv == 3, 2, dv))
    slots = (across * 4 + place) * PER + du * 4 + cols % 4
    spots = jnp.arange(SLOTS, dtype=jnp.int32)
    kind = jnp.where(across == 0, 0, jnp.where(place < 3, 1, 2))
    kind = jnp.where(spots < count[0], kind, 3)
    ahead = (kind[None, :] < kind[:, None]) | (
        (kind[None, :] == kind[:, None]) & (spots[None, :] < spots[:, None])
    )
    rank = jnp.sum(ahead.astype(jnp.int32), axis=1)
    here = rank[None, :] == spots[:, None]

    def sort(values):
        return jnp.sum(jnp.where(here, values[None, :], 0), axis=1)

    steps = jnp.arange(8, dtype=jnp.int32)
    bounds = jnp.sum((kind[None, :] < steps[:, None]).astype(jnp.int32), axis=1)
    bounds = jnp.where(steps == CORE, loop % 2, jnp.where(steps == LOW, loop // 2, bounds))
    return bounds, sort(spots), sort(rows), sort(slots)


def quarter_tiles(features, index):
    feats = features.shape[0]
    split = features.reshape(feats, 4, 4, TILE)
    piece = lax.dynamic_index_in_dim(split, index, 1, keepdims=False)
    return jnp.transpose(piece, (1, 2, 0))


def gather_own(features, loop):
    own = quarter_tiles(features, loop)
    one, three, two = permute(own, u_down), permute(own, u_up), permute(own, u_far)
    partner = permute(quarter_tiles(features, loop ^ 2), y_partner)
    return jnp.concatenate([own, one, two, three], axis=0), partner


def add_low(value, part):
    return lax.dynamic_update_slice_in_dim(value, value[:HALF] + part, 0, 0)


def add_high(value, part):
    return lax.dynamic_update_slice_in_dim(value, value[HALF:] + part, HALF, 0)


def scatter_terms(plan, pairs, spread):
    *far, spread = tie(*backward_part(2, plan, pairs, spread), spread)
    low, high = permute(far[0], v_up), permute(far[1], v_down)
    zero, one, three = backward_part(1, plan, pairs, spread)
    one, three, spread = tie(add_low(one, low), add_high(three, high), spread)
    one, three = permute(one, v_up), permute(three, v_down)
    own, own_one, own_three, low, high = backward_part(0, plan, pairs, spread)
    low, high = permute(low, v_up), permute(high, v_down)
    apart = zero + one + three
    apart_far = permute(apart[4:], y_far)
    own_one = permute(add_low(own_one, low), v_up)
    own_three = permute(add_high(own_three, high), v_down)
    last, apart_far = tie(apart[:4], apart_far)
    last = permute(last, y_far)
    total = own + own_one + own_three
    one = permute(total[4:8] + apart_far[0:4], u_up)
    two = permute(total[8:12] + apart_far[4:8], u_far)
    three = permute(total[12:16] + apart_far[8:12], u_down)
    return total[:4] + last + one + two + three


def per_device(features, weight, cotangent, tiles, tile_rows, tile_cols, counts):
    nrow = features.shape[1] // TILE
    loop = lax.axis_index(LOOP)
    wide = lax.axis_index(WIDE)
    tile_collection = tiles.reshape(SLOTS, TILE, TILE)
    count = counts.reshape(1)
    plan = make_plan(tile_rows.reshape(SLOTS), tile_cols.reshape(SLOTS), count, loop, wide)
    across = weight.T

    row, partner = gather_own(features, loop)
    plan, across, row, partner = tie(plan, across, row, partner)
    one, three = permute(row, v_down), permute(row, v_up)
    row_far = permute(row[4:], y_far)
    count, one = tie(count, one)
    pairs = pair_tiles(count, tile_collection)
    near = [row, one, three, permute(one[:HALF], v_down), permute(three[HALF:], v_up)]
    row = jnp.concatenate([partner, row_far], axis=0)
    one, three = permute(row, v_down), permute(row, v_up)
    partial = forward_part(0, plan, pairs, near, None, nrow)
    one, three, partial = tie(one, three, partial[0])
    far = [permute(one[:HALF], v_down), permute(three[HALF:], v_up)]
    partial = forward_part(1, plan, pairs, [row, one, three], partial, nrow)
    *kept, given_first, given_second = forward_part(2, plan, pairs, far, partial[0], nrow)

    bounds = plan[0]
    kept = [kept[0] + permute(given_first, core_swap), kept[1] + permute(given_second, core_swap)]
    kept = [value + permute(value, y_pair) for value in kept]
    early = middle_part(
        0, bounds, across, weight, cotangent, kept[0], permute(kept[0], core_swap), pairs
    )
    activated, spread, weight_term = middle_part(
        1, bounds, across, weight, cotangent, kept[1], permute(kept[1], core_swap), pairs, early
    )
    weight_grad = lax.psum(lax.psum(lax.psum(weight_term, "x"), "z"), "y_hi")
    total = scatter_terms(plan, pairs, spread)
    far_total = permute(total, y_pair)
    parts = [total, permute(total, core_swap), far_total, permute(far_total, core_swap)]
    return (activated, assemble(bounds, parts), weight_grad)


def solution(mesh):
    split = jax.sharding.Mesh(mesh.devices.reshape(2, 2, 2, SIDE, SIDE), AXES)
    return jax.shard_map(
        per_device,
        mesh=split,
        in_specs=(
            P(None, WIDE),
            P(),
            P(None, WIDE),
            P(LOOP, WIDE, None, None, None),
            P(LOOP, WIDE, None),
            P(LOOP, WIDE, None),
            P(LOOP, WIDE),
        ),
        out_specs=(P(None, WIDE), P(None, WIDE), P()),
        check_vma=False,
    )
```

```python
import functools

import jax
import jax.numpy as jnp
from jax import lax
from jax.experimental import pallas as pl
from jax.experimental.pallas import tpu as pltpu
from jax.sharding import PartitionSpec as P

HI = lax.Precision.HIGHEST
GELU_SCALE = 0.7978845608028654
GELU_CUBE = 0.044715
AXES = ("y_lo", "core", "y_hi", "x", "z")
LOOP = ("y_lo", "core")
WIDE = ("y_hi", "x", "z")
SIDE = 4
TILE = 128
SLOTS = 256
GROUP = 16
CHUNK = 32
STAGES = 4
PAIR_BYTES = 30 * 1024 * 1024
PER = 16
HALF = 8
FORWARD = (
    (1, 3, 48, (PER, PER, PER, HALF, HALF)),
    (0, 1, 0, (PER, PER, PER)),
    (3, 4, 112, (HALF, HALF)),
)
BACKWARD = (
    (2, 4, 96, (HALF, HALF, HALF, HALF)),
    (0, 2, 0, (PER, PER, PER, PER, PER, PER)),
)
CORE = 5
LOW = 6
VMEM_BYTES = 8 * 1024 * 1024


def device_index(y, core, x, z):
    y, x, z = y % SIDE, x % SIDE, z % SIDE
    return (((y & 1) * 2 + core) * 2 + (y >> 1)) * 16 + x * SIDE + z


def permute(value, move):
    pairs = []
    for y in range(SIDE):
        for core in range(2):
            for x in range(SIDE):
                for z in range(SIDE):
                    pairs.append((device_index(y, core, x, z), device_index(*move(y, core, x, z))))
    return lax.ppermute(value, AXES, pairs)


def along(first, step):
    def move(y, core, x, z):
        if (core == 0) == first:
            return (y, core, x + step, z)
        return (y, core, x, z + step)

    return move


u_up, u_down, u_far = along(True, 1), along(True, -1), along(True, 2)
v_up, v_down = along(False, 1), along(False, -1)


def y_partner(y, core, x, z):
    return (3 - y, core, x, z)


def y_pair(y, core, x, z):
    return (y ^ 1, core, x, z)


def y_far(y, core, x, z):
    return (y + 2, core, x, z)


def core_swap(y, core, x, z):
    return (y, 1 - core, x, z)


def tie(*values):
    return lax.optimization_barrier(values)


def split_high_low(value):
    high = value.astype(jnp.bfloat16)
    low = (value - high.astype(jnp.float32)).astype(jnp.bfloat16)
    return high, low


def pair_kernel(count_ref, tiles_ref, out_ref, held, sems):
    count = count_ref[0]

    def copy(chunk):
        source = tiles_ref.at[pl.ds(chunk * CHUNK, CHUNK)]
        return pltpu.make_async_copy(source, held.at[chunk % STAGES], sems.at[chunk % STAGES])

    def when_live(chunk):
        return pl.when(chunk * CHUNK < count)

    for chunk in range(STAGES):
        when_live(chunk)(copy(chunk).start)
    for chunk in range(SLOTS // CHUNK):

        @when_live(chunk)
        def _():
            copy(chunk).wait()

            @pl.loop(0, CHUNK, unroll=8)
            def _(j):
                high, low = split_high_low(held[chunk % STAGES, j])
                out_ref[chunk * CHUNK + j, :, :TILE] = high
                out_ref[chunk * CHUNK + j, :, TILE:] = low

            if chunk + STAGES < SLOTS // CHUNK:
                when_live(chunk + STAGES)(copy(chunk + STAGES).start)


def pair_tiles(count, tiles):
    return pl.pallas_call(
        pair_kernel,
        name="pair_tiles",
        out_shape=pltpu.VMEM((SLOTS, TILE, 2 * TILE), jnp.bfloat16),
        in_specs=[smem(), anywhere()],
        out_specs=vmem(),
        scratch_shapes=[
            pltpu.VMEM((STAGES, CHUNK, TILE, TILE), jnp.float32),
            pltpu.SemaphoreType.DMA((STAGES,)),
        ],
        cost_estimate=cost(8),
        compiler_params=pltpu.CompilerParams(vmem_limit_bytes=PAIR_BYTES),
    )(count, tiles)


def class_range(bounds_ref, first, last):
    begin, end = bounds_ref[first], bounds_ref[last]
    return begin, end, (end - begin + GROUP - 1) // GROUP


def forward_kernel(which, bounds_ref, order_ref, rows_ref, slots_ref, tiles_ref, *rest):
    first, last, base, sizes = FORWARD[which]
    buffers = rest[: len(sizes)]
    rest = rest[len(sizes) :]
    prior_ref = rest[0] if which else None
    pairs, total = rest[-2:]
    nrow = total.shape[0] - 1
    begin, end, groups = class_range(bounds_ref, first, last)
    if which:
        total[0:nrow] = prior_ref[...]
    else:
        total[0:nrow] = jnp.zeros((nrow, TILE, TILE), jnp.float32)
    for index, size in enumerate(sizes):
        start = sum(sizes[:index])

        @pl.loop(0, size, unroll=4)
        def _(j):
            high, low = split_high_low(buffers[index][j])
            pairs[start + j, :, :TILE] = high
            pairs[start + j, :, TILE:] = low

    @pl.loop(0, groups)
    def _(group):
        for j in range(GROUP):
            spot = group * GROUP + j
            place = jnp.minimum(begin + spot, SLOTS - 1)
            live = begin + spot < end
            row = jnp.where(live, rows_ref[place], nrow)
            slot = jnp.where(live, slots_ref[place] - base, 0)
            right = pairs[slot]
            product = jnp.dot(
                tiles_ref[order_ref[place]],
                jnp.concatenate([right, right], axis=0),
                preferred_element_type=jnp.float32,
            )
            total[row] += product[:, :TILE] + product[:, TILE:]

    if which == len(FORWARD) - 1:
        core = bounds_ref[CORE]
        part = nrow // 4
        for index, out_ref in enumerate(rest[-6:-2]):
            side = core if index < 2 else 1 - core
            out_ref[...] = total[pl.ds((side * 2 + index % 2) * part, part)]
    else:
        rest[-3][...] = total[0:nrow]


def backward_kernel(which, bounds_ref, order_ref, rows_ref, slots_ref, tiles_ref, slope_ref, *rest):
    first, last, base, sizes = BACKWARD[which]
    buffers = rest[: len(sizes)]
    total, out_sems = rest[len(sizes) :]
    begin, end, groups = class_range(bounds_ref, first, last)
    @pl.loop(0, sum(sizes), unroll=4)
    def _(slot):
        total[slot] = jnp.zeros((TILE, TILE), jnp.float32)

    @pl.loop(0, groups)
    def _(group):
        for j in range(GROUP):
            spot = group * GROUP + j
            place = jnp.minimum(begin + spot, SLOTS - 1)
            live = begin + spot < end
            slot = jnp.where(live, slots_ref[place] - base, sum(sizes))
            right = tiles_ref[order_ref[place]]
            product = jnp.dot(
                slope_ref[rows_ref[place]],
                jnp.concatenate([right, right], axis=0),
                preferred_element_type=jnp.float32,
            )
            total[slot] += product[:, :TILE] + product[:, TILE:]

    copies = []
    for index, size in enumerate(sizes):
        copy = pltpu.make_async_copy(
            total.at[pl.ds(sum(sizes[:index]), size)], buffers[index], out_sems.at[index]
        )
        copy.start()
        copies.append(copy)
    for copy in copies:
        copy.wait()


def smem():
    return pl.BlockSpec(memory_space=pltpu.SMEM)


def vmem():
    return pl.BlockSpec(memory_space=pltpu.VMEM)


def anywhere():
    return pl.BlockSpec(memory_space=pl.ANY)


def cost(microseconds):
    return pl.CostEstimate(
        flops=int(microseconds * 1.1e9), bytes_accessed=1 << 20, transcendentals=0
    )


def forward_part(which, plan, tiles, buffers, prior, nrow):
    extra = [prior] if which else []
    sizes = FORWARD[which][-1]
    out_shape = [jax.ShapeDtypeStruct((nrow, TILE, TILE), jnp.float32)]
    if which == len(FORWARD) - 1:
        out_shape = [jax.ShapeDtypeStruct((nrow // 4, TILE, TILE), jnp.float32)] * 4
    return pl.pallas_call(
        functools.partial(forward_kernel, which),
        name="forward_tiles_%d" % which,
        out_shape=out_shape,
        in_specs=[smem()] * 4 + [vmem()] * (1 + len(sizes) + len(extra)),
        out_specs=[vmem()] * len(out_shape),
        scratch_shapes=[
            pltpu.VMEM((sum(sizes), TILE, 2 * TILE), jnp.bfloat16),
            pltpu.VMEM((nrow + 1, TILE, TILE), jnp.float32),
        ],
        cost_estimate=cost((6, 5, 2)[which]),
        compiler_params=pltpu.CompilerParams(vmem_limit_bytes=VMEM_BYTES),
    )(*plan, tiles, *buffers, *extra)


def backward_part(which, plan, tiles, slope):
    sizes = BACKWARD[which][-1]
    return pl.pallas_call(
        functools.partial(backward_kernel, which),
        name="backward_tiles_%d" % which,
        out_shape=[jax.ShapeDtypeStruct((size, TILE, TILE), jnp.float32) for size in sizes],
        in_specs=[smem()] * 4 + [vmem(), vmem()],
        out_specs=[anywhere()] * len(sizes),
        scratch_shapes=[
            pltpu.VMEM((sum(sizes) + 1, TILE, TILE), jnp.float32),
            pltpu.SemaphoreType.DMA((len(sizes),)),
        ],
        cost_estimate=cost((6, 5, 2)[which]),
        compiler_params=pltpu.CompilerParams(vmem_limit_bytes=VMEM_BYTES),
    )(*plan, tiles, slope)


def triple_left(value):
    high, low = split_high_low(value)
    return jnp.concatenate([high, low, high], axis=1)


def triple_right(value, axis):
    high, low = split_high_low(value)
    return jnp.concatenate([high, high, low], axis=axis)


def middle_kernel(which, bounds_ref, across_ref, weight_ref, cotangent_ref, *rest):
    kept_ref, other_ref = rest[0:2]
    core = bounds_ref[CORE]
    part = kept_ref.shape[0]
    across = triple_left(across_ref[...])
    weight = triple_left(weight_ref[...])
    if which == 0:
        activated_ref, spread_ref, weight_term_ref = rest[-3:]
        weight_term = jnp.zeros((TILE, TILE), jnp.float32)
    else:
        early_activated_ref, early_spread_ref, early_term_ref = rest[3:6]
        activated_ref, spread_ref, weight_term_ref = rest[-3:]
        weight_term = early_term_ref[...]
    for index in range(2 * part):
        source = kept_ref if index < part else other_ref
        side = core if index < part else 1 - core
        row = (side * 2 + which) * part + index % part
        columns = pl.ds(pl.multiple_of(row * TILE, TILE), TILE)
        block = source[index % part]
        value = lax.dot_general(
            across,
            triple_right(block, 1),
            (((1,), (1,)), ((), ())),
            preferred_element_type=jnp.float32,
        )
        square = value * value
        bend = jnp.tanh(GELU_SCALE * (value + GELU_CUBE * (square * value)))
        activated = 0.5 * value * (1.0 + bend)
        rate = 0.5 * (1.0 + bend) + 0.5 * value * (1.0 - bend * bend) * (
            GELU_SCALE * (1.0 + 3.0 * GELU_CUBE * square)
        )
        slope = cotangent_ref[:, columns] * rate
        weight_term += jnp.dot(
            triple_left(slope), triple_right(block, 0), preferred_element_type=jnp.float32
        )
        spread = jnp.dot(weight, triple_right(slope, 0), preferred_element_type=jnp.float32)
        high, low = split_high_low(spread)
        if which == 0:
            activated_ref[index] = activated
            spread_ref[index, :, :TILE] = high
            spread_ref[index, :, TILE:] = low
        else:
            activated_ref[:, columns] = activated
            spread_ref[row, :, :TILE] = high
            spread_ref[row, :, TILE:] = low
            early = side * 2 * part + index % part
            early_columns = pl.ds(pl.multiple_of(early * TILE, TILE), TILE)
            activated_ref[:, early_columns] = early_activated_ref[index]
            spread_ref[early] = early_spread_ref[index]
    weight_term_ref[...] = jnp.transpose(weight_term) if which else weight_term


def middle_part(which, bounds, across, weight, cotangent, kept, other, pairs, early=()):
    part = kept.shape[0]
    rows = 4 * part if which else 2 * part
    activated = cotangent.shape if which else (rows, TILE, TILE)
    return pl.pallas_call(
        functools.partial(middle_kernel, which),
        name="middle_%d" % which,
        out_shape=[
            jax.ShapeDtypeStruct(activated, jnp.float32),
            jax.ShapeDtypeStruct((rows, TILE, 2 * TILE), jnp.bfloat16),
            jax.ShapeDtypeStruct(weight.shape, jnp.float32),
        ],
        in_specs=[smem()] + [vmem()] * (6 + len(early)),
        out_specs=[vmem()] * 3,
        cost_estimate=cost(2),
        compiler_params=pltpu.CompilerParams(vmem_limit_bytes=VMEM_BYTES),
    )(bounds, across, weight, cotangent, kept, other, pairs, *early)


def assemble_kernel(bounds_ref, own_ref, own_other_ref, across_ref, across_other_ref, out_ref):
    core, low = bounds_ref[CORE], bounds_ref[LOW]
    for source, chip, side in (
        (own_ref, low, core),
        (own_other_ref, low, 1 - core),
        (across_ref, 1 - low, core),
        (across_other_ref, 1 - low, 1 - core),
    ):
        for j in range(source.shape[0]):
            place = (chip * 2 + side) * source.shape[0] + j
            out_ref[:, pl.ds(pl.multiple_of(place * TILE, TILE), TILE)] = source[j]


def assemble(bounds, parts):
    return pl.pallas_call(
        assemble_kernel,
        name="assemble",
        out_shape=jax.ShapeDtypeStruct((TILE, 4 * parts[0].shape[0] * TILE), jnp.float32),
        in_specs=[smem()] + [vmem()] * 4,
        out_specs=vmem(),
        compiler_params=pltpu.CompilerParams(vmem_limit_bytes=VMEM_BYTES),
    )(bounds, *parts)


def make_plan(rows, cols, count, loop, wide):
    core = loop % 2
    node_block = cols // 4
    across = (node_block // 16) ^ (wide // 16)
    dx = (node_block // 4 - wide // 4) % 4
    dz = (node_block - wide) % 4
    du = jnp.where(core == 0, dx, dz)
    dv = jnp.where(core == 0, dz, dx)
    place = jnp.where(dv == 2, 3, jnp.where(dv == 3, 2, dv))
    start = jnp.where(
        place < 3, (1 - across) * 48 + place * PER, 96 + across * PER
    )
    slots = start + du * 4 + cols % 4
    spots = jnp.arange(SLOTS, dtype=jnp.int32)
    kind = jnp.where(place < 3, 1 - across, 2 + across)
    kind = jnp.where(spots < count[0], kind, 4)
    ahead = (kind[None, :] < kind[:, None]) | (
        (kind[None, :] == kind[:, None]) & (spots[None, :] < spots[:, None])
    )
    rank = jnp.sum(ahead.astype(jnp.int32), axis=1)
    here = rank[None, :] == spots[:, None]

    def sort(values):
        return jnp.sum(jnp.where(here, values[None, :], 0), axis=1)

    steps = jnp.arange(8, dtype=jnp.int32)
    bounds = jnp.sum((kind[None, :] < steps[:, None]).astype(jnp.int32), axis=1)
    bounds = jnp.where(steps == CORE, loop % 2, jnp.where(steps == LOW, loop // 2, bounds))
    return bounds, sort(spots), sort(rows), sort(slots)


def quarter_tiles(features, index):
    feats = features.shape[0]
    split = features.reshape(feats, 4, 4, TILE)
    piece = lax.dynamic_index_in_dim(split, index, 1, keepdims=False)
    return jnp.transpose(piece, (1, 2, 0))


def gather_own(features, loop):
    own = quarter_tiles(features, loop)
    one, three, two = permute(own, u_down), permute(own, u_up), permute(own, u_far)
    partner = permute(quarter_tiles(features, loop ^ 2), y_partner)
    return jnp.concatenate([own, one, two, three], axis=0), partner


def add_low(value, part):
    return lax.dynamic_update_slice_in_dim(value, value[:HALF] + part, 0, 0)


def add_high(value, part):
    return lax.dynamic_update_slice_in_dim(value, value[HALF:] + part, HALF, 0)


def flip_add(value, axis, step):
    if axis == "x":
        return value + permute(value, lambda y, c, x, z: (y, c, x ^ step, z))
    return value + permute(value, lambda y, c, x, z: (y, c, x, z ^ step))


def scatter_terms(plan, pairs, spread, weight_term):
    *far, spread = tie(*backward_part(0, plan, pairs, spread), spread)
    low, high = permute(far[2], v_up), permute(far[3], v_down)
    own_low, own_high = permute(far[0], v_up), permute(far[1], v_down)
    zero, one, three, own, own_one, own_three = backward_part(1, plan, pairs, spread)
    one, three = permute(add_low(one, low), v_up), permute(add_high(three, high), v_down)
    own_one = permute(add_low(own_one, own_low), v_up)
    own_three = permute(add_high(own_three, own_high), v_down)
    apart = zero + one + three
    apart_far = permute(apart[4:], y_far)
    last, apart_far = tie(apart[:4], apart_far)
    last = permute(last, y_far)
    own_three, weight_term = tie(own_three, weight_term)
    weight_term = flip_add(flip_add(weight_term, "x", 1), "x", 2)
    total = own + own_one + own_three
    total, weight_term = tie(total, weight_term)
    one = permute(total[4:8] + apart_far[0:4], u_up)
    two = permute(total[8:12] + apart_far[4:8], u_far)
    three = permute(total[12:16] + apart_far[8:12], u_down)
    total = total[:4] + last + one + two + three
    weight_term = flip_add(flip_add(weight_term, "z", 1), "z", 2)
    return total, weight_term + permute(weight_term, y_far)


def per_device(features, weight, cotangent, tiles, tile_rows, tile_cols, counts):
    nrow = features.shape[1] // TILE
    loop = lax.axis_index(LOOP)
    wide = lax.axis_index(WIDE)
    tile_collection = tiles.reshape(SLOTS, TILE, TILE)
    count = counts.reshape(1)
    plan = make_plan(tile_rows.reshape(SLOTS), tile_cols.reshape(SLOTS), count, loop, wide)
    across = weight.T

    row, partner = gather_own(features, loop)
    plan, across, row, partner = tie(plan, across, row, partner)
    one, three = permute(row, v_down), permute(row, v_up)
    row_far = permute(row[4:], y_far)
    count, one = tie(count, one)
    pairs = pair_tiles(count, tile_collection)
    near = [row, one, three, permute(one[:HALF], v_down), permute(three[HALF:], v_up)]
    row_far, near[3], near[4] = tie(row_far, near[3], near[4])
    row = jnp.concatenate([partner, row_far], axis=0)
    one, three = permute(row, v_down), permute(row, v_up)
    partial = forward_part(0, plan, pairs, near, None, nrow)
    one, three, partial = tie(one, three, partial[0])
    far = [permute(one[:HALF], v_down), permute(three[HALF:], v_up)]
    partial = forward_part(1, plan, pairs, [row, one, three], partial, nrow)
    *kept, given_first, given_second = forward_part(2, plan, pairs, far, partial[0], nrow)

    bounds = plan[0]
    kept = [kept[0] + permute(given_first, core_swap), kept[1] + permute(given_second, core_swap)]
    kept = [value + permute(value, y_pair) for value in kept]
    early = middle_part(
        0, bounds, across, weight, cotangent, kept[0], permute(kept[0], core_swap), pairs
    )
    activated, spread, weight_term = middle_part(
        1, bounds, across, weight, cotangent, kept[1], permute(kept[1], core_swap), pairs, early
    )
    total, weight_grad = scatter_terms(plan, pairs, spread, weight_term)
    far_total = permute(total, y_pair)
    parts = [total, permute(total, core_swap), far_total, permute(far_total, core_swap)]
    return (activated, assemble(bounds, parts), weight_grad)


def solution(mesh):
    split = jax.sharding.Mesh(mesh.devices.reshape(2, 2, 2, SIDE, SIDE), AXES)
    return jax.shard_map(
        per_device,
        mesh=split,
        in_specs=(
            P(None, WIDE),
            P(),
            P(None, WIDE),
            P(LOOP, WIDE, None, None, None),
            P(LOOP, WIDE, None),
            P(LOOP, WIDE, None),
            P(LOOP, WIDE),
        ),
        out_specs=(P(None, WIDE), P(None, WIDE), P()),
        check_vma=False,
    )
```

```python
import functools

import jax
import jax.numpy as jnp
from jax import lax
from jax.experimental import pallas as pl
from jax.experimental.pallas import tpu as pltpu
from jax.sharding import PartitionSpec as P

HI = lax.Precision.HIGHEST
GELU_SCALE = 0.7978845608028654
GELU_CUBE = 0.044715
AXES = ("y_lo", "core", "y_hi", "x", "z")
LOOP = ("y_lo", "core")
WIDE = ("y_hi", "x", "z")
SIDE = 4
TILE = 128
SLOTS = 256
GROUP = 16
CHUNK = 32
STAGES = 4
PAIR_BYTES = 30 * 1024 * 1024
PER = 16
HALF = 8
FORWARD = (
    (1, 3, 48, (HALF,) * 8),
    (0, 1, 0, (HALF,) * 6),
    (3, 4, 112, (HALF,) * 2),
)
BACKWARD = (
    (2, 4, 96, (HALF,) * 4),
    (0, 2, 0, (PER,) * 6),
)
CORE = 5
LOW = 6
VMEM_BYTES = 8 * 1024 * 1024


def device_index(y, core, x, z):
    y, x, z = y % SIDE, x % SIDE, z % SIDE
    return (((y & 1) * 2 + core) * 2 + (y >> 1)) * 16 + x * SIDE + z


def permute(value, move):
    pairs = []
    for y in range(SIDE):
        for core in range(2):
            for x in range(SIDE):
                for z in range(SIDE):
                    pairs.append((device_index(y, core, x, z), device_index(*move(y, core, x, z))))
    return lax.ppermute(value, AXES, pairs)


def along(first, step):
    def move(y, core, x, z):
        if (core == 0) == first:
            return (y, core, x + step, z)
        return (y, core, x, z + step)

    return move


u_up, u_down, u_far = along(True, 1), along(True, -1), along(True, 2)
v_up, v_down = along(False, 1), along(False, -1)


def y_partner(y, core, x, z):
    return (3 - y, core, x, z)


def y_pair(y, core, x, z):
    return (y ^ 1, core, x, z)


def y_far(y, core, x, z):
    return (y + 2, core, x, z)


def core_swap(y, core, x, z):
    return (y, 1 - core, x, z)


def tie(*values):
    return lax.optimization_barrier(values)


def split_high_low(value):
    high = value.astype(jnp.bfloat16)
    low = (value - high.astype(jnp.float32)).astype(jnp.bfloat16)
    return high, low


def pair_kernel(count_ref, tiles_ref, out_ref, held, sems):
    count = count_ref[0]

    def copy(chunk):
        source = tiles_ref.at[pl.ds(chunk * CHUNK, CHUNK)]
        return pltpu.make_async_copy(source, held.at[chunk % STAGES], sems.at[chunk % STAGES])

    def when_live(chunk):
        return pl.when(chunk * CHUNK < count)

    for chunk in range(STAGES):
        when_live(chunk)(copy(chunk).start)
    for chunk in range(SLOTS // CHUNK):

        @when_live(chunk)
        def _():
            copy(chunk).wait()

            @pl.loop(0, CHUNK, unroll=8)
            def _(j):
                high, low = split_high_low(held[chunk % STAGES, j])
                out_ref[chunk * CHUNK + j, :, :TILE] = high
                out_ref[chunk * CHUNK + j, :, TILE:] = low

            if chunk + STAGES < SLOTS // CHUNK:
                when_live(chunk + STAGES)(copy(chunk + STAGES).start)


def pair_tiles(count, tiles):
    return pl.pallas_call(
        pair_kernel,
        name="pair_tiles",
        out_shape=pltpu.VMEM((SLOTS, TILE, 2 * TILE), jnp.bfloat16),
        in_specs=[smem(), anywhere()],
        out_specs=vmem(),
        scratch_shapes=[
            pltpu.VMEM((STAGES, CHUNK, TILE, TILE), jnp.float32),
            pltpu.SemaphoreType.DMA((STAGES,)),
        ],
        cost_estimate=cost(8),
        compiler_params=pltpu.CompilerParams(vmem_limit_bytes=PAIR_BYTES),
    )(count, tiles)


def class_range(bounds_ref, first, last):
    begin, end = bounds_ref[first], bounds_ref[last]
    return begin, end, (end - begin + GROUP - 1) // GROUP


def forward_kernel(which, bounds_ref, order_ref, rows_ref, slots_ref, tiles_ref, *rest):
    first, last, base, sizes = FORWARD[which]
    buffers = rest[: len(sizes)]
    rest = rest[len(sizes) :]
    prior_ref = rest[0] if which else None
    pairs, total = rest[-2:]
    nrow = total.shape[0] - 1
    begin, end, groups = class_range(bounds_ref, first, last)
    if which:
        total[0:nrow] = prior_ref[...]
    else:
        total[0:nrow] = jnp.zeros((nrow, TILE, TILE), jnp.float32)
    for index, size in enumerate(sizes):
        start = sum(sizes[:index])

        @pl.loop(0, size, unroll=4)
        def _(j):
            high, low = split_high_low(buffers[index][j])
            pairs[start + j, :, :TILE] = high
            pairs[start + j, :, TILE:] = low

    @pl.loop(0, groups)
    def _(group):
        for j in range(GROUP):
            spot = group * GROUP + j
            place = jnp.minimum(begin + spot, SLOTS - 1)
            live = begin + spot < end
            row = jnp.where(live, rows_ref[place], nrow)
            slot = jnp.where(live, slots_ref[place] - base, 0)
            right = pairs[slot]
            product = jnp.dot(
                tiles_ref[order_ref[place]],
                jnp.concatenate([right, right], axis=0),
                preferred_element_type=jnp.float32,
            )
            total[row] += product[:, :TILE] + product[:, TILE:]

    if which == len(FORWARD) - 1:
        core = bounds_ref[CORE]
        part = nrow // 4
        for index, out_ref in enumerate(rest[-6:-2]):
            side = core if index < 2 else 1 - core
            out_ref[...] = total[pl.ds((side * 2 + index % 2) * part, part)]
    else:
        rest[-3][...] = total[0:nrow]


def backward_kernel(which, bounds_ref, order_ref, rows_ref, slots_ref, tiles_ref, slope_ref, *rest):
    first, last, base, sizes = BACKWARD[which]
    buffers = rest[: len(sizes)]
    total, out_sems = rest[len(sizes) :]
    begin, end, groups = class_range(bounds_ref, first, last)
    @pl.loop(0, sum(sizes), unroll=4)
    def _(slot):
        total[slot] = jnp.zeros((TILE, TILE), jnp.float32)

    @pl.loop(0, groups)
    def _(group):
        for j in range(GROUP):
            spot = group * GROUP + j
            place = jnp.minimum(begin + spot, SLOTS - 1)
            live = begin + spot < end
            slot = jnp.where(live, slots_ref[place] - base, sum(sizes))
            right = tiles_ref[order_ref[place]]
            product = jnp.dot(
                slope_ref[rows_ref[place]],
                jnp.concatenate([right, right], axis=0),
                preferred_element_type=jnp.float32,
            )
            total[slot] += product[:, :TILE] + product[:, TILE:]

    copies = []
    for index, size in enumerate(sizes):
        copy = pltpu.make_async_copy(
            total.at[pl.ds(sum(sizes[:index]), size)], buffers[index], out_sems.at[index]
        )
        copy.start()
        copies.append(copy)
    for copy in copies:
        copy.wait()


def smem():
    return pl.BlockSpec(memory_space=pltpu.SMEM)


def vmem():
    return pl.BlockSpec(memory_space=pltpu.VMEM)


def anywhere():
    return pl.BlockSpec(memory_space=pl.ANY)


def cost(microseconds):
    return pl.CostEstimate(
        flops=int(microseconds * 1.1e9), bytes_accessed=1 << 20, transcendentals=0
    )


def forward_part(which, plan, tiles, buffers, prior, nrow):
    extra = [prior] if which else []
    sizes = FORWARD[which][-1]
    out_shape = [jax.ShapeDtypeStruct((nrow, TILE, TILE), jnp.float32)]
    if which == len(FORWARD) - 1:
        out_shape = [jax.ShapeDtypeStruct((nrow // 4, TILE, TILE), jnp.float32)] * 4
    return pl.pallas_call(
        functools.partial(forward_kernel, which),
        name="forward_tiles_%d" % which,
        out_shape=out_shape,
        in_specs=[smem()] * 4 + [vmem()] * (1 + len(sizes) + len(extra)),
        out_specs=[vmem()] * len(out_shape),
        scratch_shapes=[
            pltpu.VMEM((sum(sizes), TILE, 2 * TILE), jnp.bfloat16),
            pltpu.VMEM((nrow + 1, TILE, TILE), jnp.float32),
        ],
        cost_estimate=cost((6, 5, 2)[which]),
        compiler_params=pltpu.CompilerParams(vmem_limit_bytes=VMEM_BYTES),
    )(*plan, tiles, *buffers, *extra)


def backward_part(which, plan, tiles, slope):
    sizes = BACKWARD[which][-1]
    return pl.pallas_call(
        functools.partial(backward_kernel, which),
        name="backward_tiles_%d" % which,
        out_shape=[jax.ShapeDtypeStruct((size, TILE, TILE), jnp.float32) for size in sizes],
        in_specs=[smem()] * 4 + [vmem(), vmem()],
        out_specs=[anywhere()] * len(sizes),
        scratch_shapes=[
            pltpu.VMEM((sum(sizes) + 1, TILE, TILE), jnp.float32),
            pltpu.SemaphoreType.DMA((len(sizes),)),
        ],
        cost_estimate=cost((6, 5, 2)[which]),
        compiler_params=pltpu.CompilerParams(vmem_limit_bytes=VMEM_BYTES),
    )(*plan, tiles, slope)


def triple_left(value):
    high, low = split_high_low(value)
    return jnp.concatenate([high, low, high], axis=1)


def triple_right(value, axis):
    high, low = split_high_low(value)
    return jnp.concatenate([high, high, low], axis=axis)


def middle_kernel(which, bounds_ref, across_ref, weight_ref, cotangent_ref, *rest):
    kept_ref, other_ref = rest[0:2]
    core = bounds_ref[CORE]
    part = kept_ref.shape[0]
    across = triple_left(across_ref[...])
    weight = triple_left(weight_ref[...])
    if which == 0:
        activated_ref, spread_ref, weight_term_ref = rest[-3:]
        weight_term = jnp.zeros((TILE, TILE), jnp.float32)
    else:
        early_activated_ref, early_spread_ref, early_term_ref = rest[3:6]
        activated_ref, spread_ref, weight_term_ref = rest[-3:]
        weight_term = early_term_ref[...]
    for index, source in enumerate((kept_ref, other_ref)):
        side = core if index == 0 else 1 - core
        row = (side * 2 + which) * part
        columns = pl.ds(pl.multiple_of(row * TILE, part * TILE), part * TILE)
        block = source[...].reshape(part * TILE, TILE)
        value = lax.dot_general(
            across,
            triple_right(block, 1),
            (((1,), (1,)), ((), ())),
            preferred_element_type=jnp.float32,
        )
        square = value * value
        bend = jnp.tanh(GELU_SCALE * (value + GELU_CUBE * (square * value)))
        activated = 0.5 * value * (1.0 + bend)
        rate = 0.5 * (1.0 + bend) + 0.5 * value * (1.0 - bend * bend) * (
            GELU_SCALE * (1.0 + 3.0 * GELU_CUBE * square)
        )
        slope = cotangent_ref[:, columns] * rate
        weight_term += jnp.dot(
            triple_left(slope), triple_right(block, 0), preferred_element_type=jnp.float32
        )
        spread = jnp.dot(weight, triple_right(slope, 0), preferred_element_type=jnp.float32)
        high, low = split_high_low(spread)
        place = index * part if which == 0 else row
        for j in range(part):
            spread_ref[place + j, :, :TILE] = high[:, j * TILE : (j + 1) * TILE]
            spread_ref[place + j, :, TILE:] = low[:, j * TILE : (j + 1) * TILE]
        if which == 0:
            activated_ref[index] = activated
        else:
            activated_ref[:, columns] = activated
            early = side * 2 * part
            early_columns = pl.ds(pl.multiple_of(early * TILE, part * TILE), part * TILE)
            activated_ref[:, early_columns] = early_activated_ref[index]
            spread_ref[pl.ds(early, part)] = early_spread_ref[index * part : (index + 1) * part]
    weight_term_ref[...] = jnp.transpose(weight_term) if which else weight_term


def middle_part(which, bounds, across, weight, cotangent, kept, other, pairs, early=()):
    part = kept.shape[0]
    rows = 4 * part if which else 2 * part
    activated = cotangent.shape if which else (2, TILE, part * TILE)
    return pl.pallas_call(
        functools.partial(middle_kernel, which),
        name="middle_%d" % which,
        out_shape=[
            jax.ShapeDtypeStruct(activated, jnp.float32),
            jax.ShapeDtypeStruct((rows, TILE, 2 * TILE), jnp.bfloat16),
            jax.ShapeDtypeStruct(weight.shape, jnp.float32),
        ],
        in_specs=[smem()] + [vmem()] * (6 + len(early)),
        out_specs=[vmem()] * 3,
        cost_estimate=cost(2),
        compiler_params=pltpu.CompilerParams(vmem_limit_bytes=VMEM_BYTES),
    )(bounds, across, weight, cotangent, kept, other, pairs, *early)


def assemble_kernel(bounds_ref, own_ref, own_other_ref, across_ref, across_other_ref, out_ref):
    core, low = bounds_ref[CORE], bounds_ref[LOW]
    for source, chip, side in (
        (own_ref, low, core),
        (own_other_ref, low, 1 - core),
        (across_ref, 1 - low, core),
        (across_other_ref, 1 - low, 1 - core),
    ):
        for j in range(source.shape[0]):
            place = (chip * 2 + side) * source.shape[0] + j
            out_ref[:, pl.ds(pl.multiple_of(place * TILE, TILE), TILE)] = source[j]


def assemble(bounds, parts):
    return pl.pallas_call(
        assemble_kernel,
        name="assemble",
        out_shape=jax.ShapeDtypeStruct((TILE, 4 * parts[0].shape[0] * TILE), jnp.float32),
        in_specs=[smem()] + [vmem()] * 4,
        out_specs=vmem(),
        compiler_params=pltpu.CompilerParams(vmem_limit_bytes=VMEM_BYTES),
    )(bounds, *parts)


def make_plan(rows, cols, count, loop, wide):
    core = loop % 2
    node_block = cols // 4
    across = (node_block // 16) ^ (wide // 16)
    dx = (node_block // 4 - wide // 4) % 4
    dz = (node_block - wide) % 4
    du = jnp.where(core == 0, dx, dz)
    dv = jnp.where(core == 0, dz, dx)
    place = jnp.where(dv == 2, 3, jnp.where(dv == 3, 2, dv))
    start = jnp.where(
        place < 3, (1 - across) * 48 + place * PER, 96 + across * PER
    )
    slots = start + du * 4 + cols % 4
    spots = jnp.arange(SLOTS, dtype=jnp.int32)
    kind = jnp.where(place < 3, 1 - across, 2 + across)
    kind = jnp.where(spots < count[0], kind, 4)
    ahead = (kind[None, :] < kind[:, None]) | (
        (kind[None, :] == kind[:, None]) & (spots[None, :] < spots[:, None])
    )
    rank = jnp.sum(ahead.astype(jnp.int32), axis=1)
    here = rank[None, :] == spots[:, None]

    def sort(values):
        return jnp.sum(jnp.where(here, values[None, :], 0), axis=1)

    steps = jnp.arange(8, dtype=jnp.int32)
    bounds = jnp.sum((kind[None, :] < steps[:, None]).astype(jnp.int32), axis=1)
    bounds = jnp.where(steps == CORE, loop % 2, jnp.where(steps == LOW, loop // 2, bounds))
    return bounds, sort(spots), sort(rows), sort(slots)


def quarter_tiles(features, index):
    feats = features.shape[0]
    split = features.reshape(feats, 4, 4, TILE)
    piece = lax.dynamic_index_in_dim(split, index, 1, keepdims=False)
    return jnp.transpose(piece, (1, 2, 0))


def gather_own(features, loop):
    own = quarter_tiles(features, loop)
    one, three, two = permute(own, u_down), permute(own, u_up), permute(own, u_far)
    partner = permute(quarter_tiles(features, loop ^ 2), y_partner)
    return own, one, two, three, partner


def gather_near(first, second):
    one_first, three_second = permute(first, v_down), permute(second, v_up)
    one_second, three_first = permute(second, v_down), permute(first, v_up)
    return [first, second, one_first, one_second, three_first, three_second]


def gather_far(near):
    return [permute(near[2], v_down), permute(near[5], v_up)]


def add_low(value, part):
    return lax.dynamic_update_slice_in_dim(value, value[:HALF] + part, 0, 0)


def add_high(value, part):
    return lax.dynamic_update_slice_in_dim(value, value[HALF:] + part, HALF, 0)


def flip_add(value, axis, step):
    if axis == "x":
        return value + permute(value, lambda y, c, x, z: (y, c, x ^ step, z))
    return value + permute(value, lambda y, c, x, z: (y, c, x, z ^ step))


def scatter_terms(plan, pairs, spread, weight_term):
    weight_term = weight_term + permute(weight_term, y_far)
    *far, spread = tie(*backward_part(0, plan, pairs, spread), spread)
    low, high = permute(far[2], v_up), permute(far[3], v_down)
    own_low, own_high = permute(far[0], v_up), permute(far[1], v_down)
    zero, one, three, own, own_one, own_three = backward_part(1, plan, pairs, spread)
    low, weight_term = tie(low, weight_term)
    one, three = permute(add_low(one, low), v_up), permute(add_high(three, high), v_down)
    own_one = permute(add_low(own_one, own_low), v_up)
    own_three = permute(add_high(own_three, own_high), v_down)
    apart = zero + one + three
    far_two = permute(apart[8:12], u_far)
    far_one, far_three = permute(apart[4:8], y_far), permute(apart[12:16], y_far)
    last = permute(apart[:4] + far_two, y_far)
    own_three, weight_term = tie(own_three, weight_term)
    weight_term = flip_add(flip_add(weight_term, "x", 1), "x", 2)
    total = own + own_one + own_three
    two = permute(total[8:12], u_far)
    one = permute(total[4:8] + far_one, u_up)
    three = permute(total[12:16] + far_three, u_down)
    return total[:4] + last + one + two + three, flip_add(weight_term, "z", 1)


def per_device(features, weight, cotangent, tiles, tile_rows, tile_cols, counts):
    nrow = features.shape[1] // TILE
    loop = lax.axis_index(LOOP)
    wide = lax.axis_index(WIDE)
    tile_collection = tiles.reshape(SLOTS, TILE, TILE)
    count = counts.reshape(1)
    plan = make_plan(tile_rows.reshape(SLOTS), tile_cols.reshape(SLOTS), count, loop, wide)
    across = weight.T

    own, one, two, three, partner = gather_own(features, loop)
    first = jnp.concatenate([own, one], axis=0)
    second = jnp.concatenate([two, three], axis=0)
    plan, across, first, second, one, partner = tie(plan, across, first, second, one, partner)
    near = gather_near(first, second)
    second_far, first_far = permute(second, y_far), permute(one, y_far)
    count, near[2] = tie(count, near[2])
    pairs = pair_tiles(count, tile_collection)
    far = gather_far(near)
    second_far, first_far, *far = tie(second_far, first_far, *far)
    apart = gather_near(jnp.concatenate([partner, first_far], axis=0), second_far)
    partial = forward_part(0, plan, pairs, near + far, None, nrow)
    apart[2], apart[5], partial = tie(apart[2], apart[5], partial[0])
    far = gather_far(apart)
    partial = forward_part(1, plan, pairs, apart, partial, nrow)
    *kept, given_first, given_second = forward_part(2, plan, pairs, far, partial[0], nrow)

    bounds = plan[0]
    kept = [kept[0] + permute(given_first, core_swap), kept[1] + permute(given_second, core_swap)]
    kept = [value + permute(value, y_pair) for value in kept]
    early = middle_part(
        0, bounds, across, weight, cotangent, kept[0], permute(kept[0], core_swap), pairs
    )
    activated, spread, weight_term = middle_part(
        1, bounds, across, weight, cotangent, kept[1], permute(kept[1], core_swap), pairs, early
    )
    total, weight_term = tie(*scatter_terms(plan, pairs, spread, weight_term))
    far_total, weight_grad = tie(permute(total, y_pair), flip_add(weight_term, "z", 2))
    parts = [total, permute(total, core_swap), far_total, permute(far_total, core_swap)]
    return (activated, assemble(bounds, parts), weight_grad)


def solution(mesh):
    split = jax.sharding.Mesh(mesh.devices.reshape(2, 2, 2, SIDE, SIDE), AXES)
    return jax.shard_map(
        per_device,
        mesh=split,
        in_specs=(
            P(None, WIDE),
            P(),
            P(None, WIDE),
            P(LOOP, WIDE, None, None, None),
            P(LOOP, WIDE, None),
            P(LOOP, WIDE, None),
            P(LOOP, WIDE),
        ),
        out_specs=(P(None, WIDE), P(None, WIDE), P()),
        check_vma=False,
    )
```

```python
import functools

import jax
import jax.numpy as jnp
from jax import lax
from jax.experimental import pallas as pl
from jax.experimental.pallas import tpu as pltpu
from jax.sharding import PartitionSpec as P

HI = lax.Precision.HIGHEST
GELU_SCALE = 0.7978845608028654
GELU_CUBE = 0.044715
AXES = ("y_lo", "core", "y_hi", "x", "z")
LOOP = ("y_lo", "core")
WIDE = ("y_hi", "x", "z")
SIDE = 4
TILE = 128
SLOTS = 256
GROUP = 16
CHUNK = 32
STAGES = 4
PAIR_BYTES = 30 * 1024 * 1024
PER = 16
HALF = 8
FORWARD = (
    (1, 3, 48, (HALF,) * 8),
    (0, 1, 0, (HALF,) * 6),
    (3, 4, 112, (HALF,) * 2),
)
BACKWARD = (
    (2, 4, 96, (PER, PER), (1, 1)),
    (0, 2, 0, (PER,) * 6, (0, 1, 0, 0, 0, 0)),
)
CORE = 5
LOW = 6
FIRST = 7
VMEM_BYTES = 8 * 1024 * 1024


def device_index(y, core, x, z):
    y, x, z = y % SIDE, x % SIDE, z % SIDE
    return (((y & 1) * 2 + core) * 2 + (y >> 1)) * 16 + x * SIDE + z


def permute(value, move):
    pairs = []
    for y in range(SIDE):
        for core in range(2):
            for x in range(SIDE):
                for z in range(SIDE):
                    pairs.append((device_index(y, core, x, z), device_index(*move(y, core, x, z))))
    return lax.ppermute(value, AXES, pairs)


def along(first, step):
    def move(y, core, x, z):
        if (core == 0) == first:
            return (y, core, x + step, z)
        return (y, core, x, z + step)

    return move


u_up, u_down, u_far = along(True, 1), along(True, -1), along(True, 2)
v_up, v_down = along(False, 1), along(False, -1)


def y_partner(y, core, x, z):
    return (3 - y, core, x, z)


def y_pair(y, core, x, z):
    return (y ^ 1, core, x, z)


def y_far(y, core, x, z):
    return (y + 2, core, x, z)


def core_swap(y, core, x, z):
    return (y, 1 - core, x, z)


def tie(*values):
    return lax.optimization_barrier(values)


def split_high_low(value):
    high = value.astype(jnp.bfloat16)
    low = (value - high.astype(jnp.float32)).astype(jnp.bfloat16)
    return high, low


def pair_kernel(count_ref, tiles_ref, out_ref, held, sems):
    count = count_ref[0]

    def copy(chunk):
        source = tiles_ref.at[pl.ds(chunk * CHUNK, CHUNK)]
        return pltpu.make_async_copy(source, held.at[chunk % STAGES], sems.at[chunk % STAGES])

    def when_live(chunk):
        return pl.when(chunk * CHUNK < count)

    for chunk in range(STAGES):
        when_live(chunk)(copy(chunk).start)
    for chunk in range(SLOTS // CHUNK):

        @when_live(chunk)
        def _():
            copy(chunk).wait()

            @pl.loop(0, CHUNK, unroll=8)
            def _(j):
                high, low = split_high_low(held[chunk % STAGES, j])
                out_ref[chunk * CHUNK + j, :, :TILE] = high
                out_ref[chunk * CHUNK + j, :, TILE:] = low

            if chunk + STAGES < SLOTS // CHUNK:
                when_live(chunk + STAGES)(copy(chunk + STAGES).start)


def pair_tiles(count, tiles):
    return pl.pallas_call(
        pair_kernel,
        name="pair_tiles",
        out_shape=pltpu.VMEM((SLOTS, TILE, 2 * TILE), jnp.bfloat16),
        in_specs=[smem(), anywhere()],
        out_specs=vmem(),
        scratch_shapes=[
            pltpu.VMEM((STAGES, CHUNK, TILE, TILE), jnp.float32),
            pltpu.SemaphoreType.DMA((STAGES,)),
        ],
        cost_estimate=cost(8),
        compiler_params=pltpu.CompilerParams(vmem_limit_bytes=PAIR_BYTES),
    )(count, tiles)


def class_range(bounds_ref, first, last):
    begin, end = bounds_ref[first], bounds_ref[last]
    return begin, end, (end - begin + GROUP - 1) // GROUP


def forward_kernel(which, bounds_ref, order_ref, rows_ref, slots_ref, tiles_ref, *rest):
    first, last, base, sizes = FORWARD[which]
    buffers = rest[: len(sizes)]
    rest = rest[len(sizes) :]
    prior_ref = rest[0] if which else None
    pairs, total = rest[-2:]
    nrow = total.shape[0] - 1
    begin, end, groups = class_range(bounds_ref, first, last)
    if which:
        total[0:nrow] = prior_ref[...]
    else:
        total[0:nrow] = jnp.zeros((nrow, TILE, TILE), jnp.float32)
    for index, size in enumerate(sizes):
        start = sum(sizes[:index])

        @pl.loop(0, size, unroll=4)
        def _(j):
            high, low = split_high_low(buffers[index][j])
            pairs[start + j, :, :TILE] = high
            pairs[start + j, :, TILE:] = low

    @pl.loop(0, groups)
    def _(group):
        for j in range(GROUP):
            spot = group * GROUP + j
            place = jnp.minimum(begin + spot, SLOTS - 1)
            live = begin + spot < end
            row = jnp.where(live, rows_ref[place], nrow)
            slot = jnp.where(live, slots_ref[place] - base, 0)
            right = pairs[slot]
            product = jnp.dot(
                tiles_ref[order_ref[place]],
                jnp.concatenate([right, right], axis=0),
                preferred_element_type=jnp.float32,
            )
            total[row] += product[:, :TILE] + product[:, TILE:]

    if which == len(FORWARD) - 1:
        core = bounds_ref[CORE]
        part = nrow // 4
        for index, out_ref in enumerate(rest[-6:-2]):
            side = core if index < 2 else 1 - core
            out_ref[...] = total[pl.ds((side * 2 + index % 2) * part, part)]
    else:
        rest[-3][...] = total[0:nrow]


def backward_kernel(which, bounds_ref, order_ref, rows_ref, slots_ref, tiles_ref, slope_ref, *rest):
    first, last, base, sizes, extra = BACKWARD[which]
    if which == 0:
        weight_term_ref, *rest = rest
    buffers = rest[: len(sizes)]
    total, out_sems, *rest = rest[len(sizes) :]
    if which == 0:
        (term_sems,) = rest
        term_copies = [
            pltpu.make_async_copy(weight_term_ref, buffer.at[PER], term_sems.at[index])
            for index, buffer in enumerate(buffers)
        ]
        for copy in term_copies:
            copy.start()
    begin, end, groups = class_range(bounds_ref, first, last)
    @pl.loop(0, sum(sizes), unroll=4)
    def _(slot):
        total[slot] = jnp.zeros((TILE, TILE), jnp.float32)

    @pl.loop(0, groups)
    def _(group):
        for j in range(GROUP):
            spot = group * GROUP + j
            place = jnp.minimum(begin + spot, SLOTS - 1)
            live = begin + spot < end
            slot = jnp.where(live, slots_ref[place] - base, sum(sizes))
            right = tiles_ref[order_ref[place]]
            product = jnp.dot(
                slope_ref[rows_ref[place]],
                jnp.concatenate([right, right], axis=0),
                preferred_element_type=jnp.float32,
            )
            total[slot] += product[:, :TILE] + product[:, TILE:]

    copies = []
    for index, size in enumerate(sizes):
        copy = pltpu.make_async_copy(
            total.at[pl.ds(sum(sizes[:index]), size)],
            buffers[index].at[pl.ds(0, size)],
            out_sems.at[index],
        )
        copy.start()
        copies.append(copy)
    if which == 0:
        copies += term_copies
    for copy in copies:
        copy.wait()


def smem():
    return pl.BlockSpec(memory_space=pltpu.SMEM)


def vmem():
    return pl.BlockSpec(memory_space=pltpu.VMEM)


def anywhere():
    return pl.BlockSpec(memory_space=pl.ANY)


def cost(microseconds):
    return pl.CostEstimate(
        flops=int(microseconds * 1.1e9), bytes_accessed=1 << 20, transcendentals=0
    )


def forward_part(which, plan, tiles, buffers, prior, nrow):
    extra = [prior] if which else []
    sizes = FORWARD[which][-1]
    out_shape = [jax.ShapeDtypeStruct((nrow, TILE, TILE), jnp.float32)]
    if which == len(FORWARD) - 1:
        out_shape = [jax.ShapeDtypeStruct((nrow // 4, TILE, TILE), jnp.float32)] * 4
    return pl.pallas_call(
        functools.partial(forward_kernel, which),
        name="forward_tiles_%d" % which,
        out_shape=out_shape,
        in_specs=[smem()] * 4 + [vmem()] * (1 + len(sizes) + len(extra)),
        out_specs=[vmem()] * len(out_shape),
        scratch_shapes=[
            pltpu.VMEM((sum(sizes), TILE, 2 * TILE), jnp.bfloat16),
            pltpu.VMEM((nrow + 1, TILE, TILE), jnp.float32),
        ],
        cost_estimate=cost((6, 5, 2)[which]),
        compiler_params=pltpu.CompilerParams(vmem_limit_bytes=VMEM_BYTES),
    )(*plan, tiles, *buffers, *extra)


def backward_part(which, plan, tiles, slope, weight_term=()):
    sizes, extra = BACKWARD[which][-2:]
    return pl.pallas_call(
        functools.partial(backward_kernel, which),
        name="backward_tiles_%d" % which,
        out_shape=[
            jax.ShapeDtypeStruct((size + more, TILE, TILE), jnp.float32)
            for size, more in zip(sizes, extra)
        ],
        in_specs=[smem()] * 4 + [vmem()] * (2 + len(weight_term)),
        out_specs=[anywhere()] * len(sizes),
        scratch_shapes=[
            pltpu.VMEM((sum(sizes) + 1, TILE, TILE), jnp.float32),
            pltpu.SemaphoreType.DMA((len(sizes),)),
        ]
        + [pltpu.SemaphoreType.DMA((2,))] * len(weight_term),
        cost_estimate=cost((3, 8)[which]),
        compiler_params=pltpu.CompilerParams(vmem_limit_bytes=VMEM_BYTES),
    )(*plan, tiles, slope, *weight_term)


def triple_left(value):
    high, low = split_high_low(value)
    return jnp.concatenate([high, low, high], axis=1)


def triple_right(value, axis):
    high, low = split_high_low(value)
    return jnp.concatenate([high, high, low], axis=axis)


def middle_kernel(which, bounds_ref, across_ref, weight_ref, cotangent_ref, *rest):
    kept_ref, other_ref = rest[0:2]
    core = bounds_ref[CORE]
    part = kept_ref.shape[0]
    across = triple_left(across_ref[...])
    weight = triple_left(weight_ref[...])
    if which == 0:
        activated_ref, spread_ref, weight_term_ref = rest[-3:]
        weight_term = jnp.zeros((TILE, TILE), jnp.float32)
    else:
        early_activated_ref, early_spread_ref, early_term_ref = rest[3:6]
        activated_ref, spread_ref, weight_term_ref = rest[-3:]
        weight_term = early_term_ref[...]
    for index, source in enumerate((kept_ref, other_ref)):
        side = core if index == 0 else 1 - core
        row = (side * 2 + which) * part
        columns = pl.ds(pl.multiple_of(row * TILE, part * TILE), part * TILE)
        block = source[...].reshape(part * TILE, TILE)
        value = lax.dot_general(
            across,
            triple_right(block, 1),
            (((1,), (1,)), ((), ())),
            preferred_element_type=jnp.float32,
        )
        square = value * value
        bend = jnp.tanh(GELU_SCALE * (value + GELU_CUBE * (square * value)))
        activated = 0.5 * value * (1.0 + bend)
        rate = 0.5 * (1.0 + bend) + 0.5 * value * (1.0 - bend * bend) * (
            GELU_SCALE * (1.0 + 3.0 * GELU_CUBE * square)
        )
        slope = cotangent_ref[:, columns] * rate
        weight_term += jnp.dot(
            triple_left(slope), triple_right(block, 0), preferred_element_type=jnp.float32
        )
        spread = jnp.dot(weight, triple_right(slope, 0), preferred_element_type=jnp.float32)
        high, low = split_high_low(spread)
        place = index * part if which == 0 else row
        for j in range(part):
            spread_ref[place + j, :, :TILE] = high[:, j * TILE : (j + 1) * TILE]
            spread_ref[place + j, :, TILE:] = low[:, j * TILE : (j + 1) * TILE]
        if which == 0:
            activated_ref[index] = activated
        else:
            activated_ref[:, columns] = activated
            early = side * 2 * part
            early_columns = pl.ds(pl.multiple_of(early * TILE, part * TILE), part * TILE)
            activated_ref[:, early_columns] = early_activated_ref[index]
            spread_ref[pl.ds(early, part)] = early_spread_ref[index * part : (index + 1) * part]
    weight_term_ref[...] = jnp.transpose(weight_term) if which else weight_term


def middle_part(which, bounds, across, weight, cotangent, kept, other, pairs, early=()):
    part = kept.shape[0]
    rows = 4 * part if which else 2 * part
    activated = cotangent.shape if which else (2, TILE, part * TILE)
    return pl.pallas_call(
        functools.partial(middle_kernel, which),
        name="middle_%d" % which,
        out_shape=[
            jax.ShapeDtypeStruct(activated, jnp.float32),
            jax.ShapeDtypeStruct((rows, TILE, 2 * TILE), jnp.bfloat16),
            jax.ShapeDtypeStruct(weight.shape, jnp.float32),
        ],
        in_specs=[smem()] + [vmem()] * (6 + len(early)),
        out_specs=[vmem()] * 3,
        cost_estimate=cost(2),
        compiler_params=pltpu.CompilerParams(vmem_limit_bytes=VMEM_BYTES),
    )(bounds, across, weight, cotangent, kept, other, pairs, *early)


def ring_sum_kernel(which, bounds_ref, own_ref, one_ref, two_ref, three_ref, out_ref):
    refs = (own_ref, one_ref, two_ref, three_ref)
    for place in range(SIDE):

        @pl.when(bounds_ref[FIRST + which] == place)
        def _():
            parts = [refs[(index - place) % SIDE] for index in range(SIDE)]
            out_ref[...] = (parts[0][...] + parts[1][...]) + (parts[2][...] + parts[3][...])


def ring_sum(which, bounds, parts):
    return pl.pallas_call(
        functools.partial(ring_sum_kernel, which),
        name="ring_sum_%d" % which,
        out_shape=jax.ShapeDtypeStruct((TILE, TILE), jnp.float32),
        in_specs=[smem()] + [vmem()] * SIDE,
        out_specs=vmem(),
        compiler_params=pltpu.CompilerParams(vmem_limit_bytes=VMEM_BYTES),
    )(bounds, *parts)


def assemble_kernel(
    bounds_ref, own_ref, own_other_ref, across_ref, across_other_ref, term_ref, out_ref, sum_ref
):
    core, low = bounds_ref[CORE], bounds_ref[LOW]
    for source, chip, side in (
        (own_ref, low, core),
        (own_other_ref, low, 1 - core),
        (across_ref, 1 - low, core),
        (across_other_ref, 1 - low, 1 - core),
    ):
        for j in range(4):
            place = (chip * 2 + side) * 4 + j
            out_ref[:, pl.ds(pl.multiple_of(place * TILE, TILE), TILE)] = source[j]

    @pl.when(core == 0)
    def _():
        sum_ref[...] = term_ref[...]

    @pl.when(core == 1)
    def _():
        sum_ref[...] = own_other_ref[4]


def assemble(bounds, parts):
    return pl.pallas_call(
        assemble_kernel,
        name="assemble",
        out_shape=[
            jax.ShapeDtypeStruct((TILE, 16 * TILE), jnp.float32),
            jax.ShapeDtypeStruct((TILE, TILE), jnp.float32),
        ],
        in_specs=[smem()] + [vmem()] * 5,
        out_specs=[vmem()] * 2,
        compiler_params=pltpu.CompilerParams(vmem_limit_bytes=VMEM_BYTES),
    )(bounds, *parts)


def make_plan(rows, cols, count, loop, wide):
    core = loop % 2
    node_block = cols // 4
    across = (node_block // 16) ^ (wide // 16)
    dx = (node_block // 4 - wide // 4) % 4
    dz = (node_block - wide) % 4
    du = jnp.where(core == 0, dx, dz)
    dv = jnp.where(core == 0, dz, dx)
    place = jnp.where(dv == 2, 3, jnp.where(dv == 3, 2, dv))
    start = jnp.where(
        place < 3, (1 - across) * 48 + place * PER, 96 + across * PER
    )
    slots = start + du * 4 + cols % 4
    spots = jnp.arange(SLOTS, dtype=jnp.int32)
    kind = jnp.where(place < 3, 1 - across, 2 + across)
    kind = jnp.where(spots < count[0], kind, 4)
    ahead = (kind[None, :] < kind[:, None]) | (
        (kind[None, :] == kind[:, None]) & (spots[None, :] < spots[:, None])
    )
    rank = jnp.sum(ahead.astype(jnp.int32), axis=1)
    here = rank[None, :] == spots[:, None]

    def sort(values):
        return jnp.sum(jnp.where(here, values[None, :], 0), axis=1)

    inner = du * 4 + cols % 4
    back_slots = jnp.where(
        place < 3, slots, 96 + (inner // HALF) * PER + across * HALF + inner % HALF
    )
    steps = jnp.arange(9, dtype=jnp.int32)
    bounds = jnp.sum((kind[None, :] < steps[:, None]).astype(jnp.int32), axis=1)
    bounds = jnp.where(steps == CORE, loop % 2, jnp.where(steps == LOW, loop // 2, bounds))
    ring = jnp.where(core == 0, wide // 4 % 4, wide % 4)
    other_ring = jnp.where(core == 0, wide % 4, wide // 4 % 4)
    bounds = jnp.where(steps == FIRST, ring, jnp.where(steps == FIRST + 1, other_ring, bounds))
    return bounds, sort(spots), sort(rows), sort(slots), sort(back_slots)


def quarter_tiles(features, index):
    feats = features.shape[0]
    split = features.reshape(feats, 4, 4, TILE)
    piece = lax.dynamic_index_in_dim(split, index, 1, keepdims=False)
    return jnp.transpose(piece, (1, 2, 0))


def gather_own(features, loop):
    own = quarter_tiles(features, loop)
    one, three, two = permute(own, u_down), permute(own, u_up), permute(own, u_far)
    partner = permute(quarter_tiles(features, loop ^ 2), y_partner)
    return own, one, two, three, partner


def with_tile(value, tile):
    return jnp.concatenate([value, tile[None]], axis=0)


def add_part(value, part, start):
    size = part.shape[0]
    return lax.dynamic_update_slice_in_dim(value, value[start : start + size] + part, start, 0)


def scatter_terms(plan, pairs, spread, weight_term):
    back_plan = plan[:3] + plan[4:]
    up, down, spread = tie(*backward_part(0, back_plan, pairs, spread, (weight_term,)), spread)
    up, down = permute(up, v_up), permute(down, v_down)
    zero, one, three, own, own_one, own_three = backward_part(1, back_plan, pairs, spread)
    one = lax.dynamic_update_slice_in_dim(add_part(one, up[HALF:PER], 0), up[PER:], PER, 0)
    three = add_part(three, down[HALF:PER], HALF)
    one, three = permute(one, v_up), permute(three, v_down)
    own_one = permute(add_part(own_one, up[:HALF], 0), v_up)
    own_three = permute(add_part(own_three, down[:HALF], HALF), v_down)
    weight_term = ring_sum(1, plan[0], (weight_term, down[PER], one[PER], up[PER]))
    apart = zero + one[:PER] + three
    apart_two = permute(apart[8:12], u_far)
    apart_far = permute(
        jnp.concatenate([apart[4:8], apart[12:16], weight_term[None]], axis=0), y_far
    )
    last, apart_far = tie(apart[:4] + apart_two, apart_far)
    last = permute(last, y_far)
    weight_term = weight_term + apart_far[8]
    total = own + own_one + own_three
    two = permute(with_tile(total[8:12], weight_term), u_far)
    one = permute(with_tile(total[4:8] + apart_far[:4], weight_term), u_up)
    three = permute(with_tile(total[12:16] + apart_far[4:8], weight_term), u_down)
    weight_term = ring_sum(0, plan[0], (weight_term, three[4], two[4], one[4]))
    return total[:4] + last + one[:4] + two[:4] + three[:4], weight_term


def per_device(features, weight, cotangent, tiles, tile_rows, tile_cols, counts):
    nrow = features.shape[1] // TILE
    loop = lax.axis_index(LOOP)
    wide = lax.axis_index(WIDE)
    tile_collection = tiles.reshape(SLOTS, TILE, TILE)
    count = counts.reshape(1)
    plan = make_plan(tile_rows.reshape(SLOTS), tile_cols.reshape(SLOTS), count, loop, wide)
    across = weight.T

    own, one, two, three, partner = gather_own(features, loop)
    first = jnp.concatenate([own, one], axis=0)
    second = jnp.concatenate([two, three], axis=0)
    plan, across, first, second, one, partner = tie(plan, across, first, second, one, partner)
    one_first, three_second = permute(first, v_down), permute(second, v_up)
    second_far = permute(second, y_far)
    count, first = tie(count, first)
    pairs = pair_tiles(count, tile_collection)
    first, second, one, pairs = tie(first, second, one, pairs)
    one_second, three_first = permute(second, v_down), permute(first, v_up)
    first_far = permute(one, y_far)
    near = [first, second, one_first, one_second, three_first, three_second]
    far = [permute(one_first, v_down), permute(three_second, v_up)]
    second_far, first_far, *far = tie(second_far, first_far, *far)
    first, second = jnp.concatenate([partner, first_far], axis=0), second_far
    one_first, three_second = permute(first, v_down), permute(second, v_up)
    partial = forward_part(0, plan[:4], pairs, near + far, None, nrow)
    first, second, partial = tie(first, second, partial[0])
    one_second, three_first = permute(second, v_down), permute(first, v_up)
    apart = [first, second, one_first, one_second, three_first, three_second]
    far = [permute(one_first, v_down), permute(three_second, v_up)]
    partial = forward_part(1, plan[:4], pairs, apart, partial, nrow)
    *kept, given_first, given_second = forward_part(2, plan[:4], pairs, far, partial[0], nrow)

    bounds = plan[0]
    kept = [kept[0] + permute(given_first, core_swap), kept[1] + permute(given_second, core_swap)]
    kept = [value + permute(value, y_pair) for value in kept]
    early = middle_part(
        0, bounds, across, weight, cotangent, kept[0], permute(kept[0], core_swap), pairs
    )
    activated, spread, weight_term = middle_part(
        1, bounds, across, weight, cotangent, kept[1], permute(kept[1], core_swap), pairs, early
    )
    total, weight_term = scatter_terms(plan, pairs, spread, weight_term)
    far_total = permute(total, y_pair)
    own_other = permute(with_tile(total, weight_term), core_swap)
    parts = [total, own_other, far_total, permute(far_total, core_swap), weight_term]
    return (activated, *assemble(bounds, parts))


def solution(mesh):
    split = jax.sharding.Mesh(mesh.devices.reshape(2, 2, 2, SIDE, SIDE), AXES)
    return jax.shard_map(
        per_device,
        mesh=split,
        in_specs=(
            P(None, WIDE),
            P(),
            P(None, WIDE),
            P(LOOP, WIDE, None, None, None),
            P(LOOP, WIDE, None),
            P(LOOP, WIDE, None),
            P(LOOP, WIDE),
        ),
        out_specs=(P(None, WIDE), P(None, WIDE), P()),
        check_vma=False,
    )
```

```python
import functools

import jax
import jax.numpy as jnp
from jax import lax
from jax.experimental import pallas as pl
from jax.experimental.pallas import tpu as pltpu
from jax.sharding import PartitionSpec as P

HI = lax.Precision.HIGHEST
GELU_SCALE = 0.7978845608028654
GELU_CUBE = 0.044715
AXES = ("y_lo", "core", "y_hi", "x", "z")
LOOP = ("y_lo", "core")
WIDE = ("y_hi", "x", "z")
SIDE = 4
TILE = 128
SLOTS = 256
GROUP = 16
CHUNK = 32
STAGES = 4
PAIR_BYTES = 30 * 1024 * 1024
PER = 16
HALF = 8
FORWARD = (
    (1, 3, 48, (HALF,) * 8),
    (0, 1, 0, (HALF,) * 6),
    (3, 4, 112, (HALF,) * 2),
)
BACKWARD = (
    (2, 4, 96, (PER, PER), (1, 1)),
    (0, 2, 0, (PER,) * 6, (0, 1, 0, 0, 0, 0)),
)
CORE = 5
LOW = 6
FIRST = 7
VMEM_BYTES = 8 * 1024 * 1024


def device_index(y, core, x, z):
    y, x, z = y % SIDE, x % SIDE, z % SIDE
    return (((y & 1) * 2 + core) * 2 + (y >> 1)) * 16 + x * SIDE + z


def permute(value, move):
    pairs = []
    for y in range(SIDE):
        for core in range(2):
            for x in range(SIDE):
                for z in range(SIDE):
                    pairs.append((device_index(y, core, x, z), device_index(*move(y, core, x, z))))
    return lax.ppermute(value, AXES, pairs)


def along(first, step):
    def move(y, core, x, z):
        if (core == 0) == first:
            return (y, core, x + step, z)
        return (y, core, x, z + step)

    return move


u_up, u_down, u_far = along(True, 1), along(True, -1), along(True, 2)
v_up, v_down = along(False, 1), along(False, -1)


def y_partner(y, core, x, z):
    return (3 - y, core, x, z)


def y_pair(y, core, x, z):
    return (y ^ 1, core, x, z)


def y_far(y, core, x, z):
    return (y + 2, core, x, z)


def core_swap(y, core, x, z):
    return (y, 1 - core, x, z)


def tie(*values):
    return lax.optimization_barrier(values)


def split_high_low(value):
    high = value.astype(jnp.bfloat16)
    low = (value - high.astype(jnp.float32)).astype(jnp.bfloat16)
    return high, low


def pair_kernel(count_ref, tiles_ref, out_ref, held, sems):
    count = count_ref[0]

    def copy(chunk):
        source = tiles_ref.at[pl.ds(chunk * CHUNK, CHUNK)]
        return pltpu.make_async_copy(source, held.at[chunk % STAGES], sems.at[chunk % STAGES])

    def when_live(chunk):
        return pl.when(chunk * CHUNK < count)

    for chunk in range(STAGES):
        when_live(chunk)(copy(chunk).start)
    for chunk in range(SLOTS // CHUNK):

        @when_live(chunk)
        def _():
            copy(chunk).wait()

            @pl.loop(0, CHUNK, unroll=8)
            def _(j):
                high, low = split_high_low(held[chunk % STAGES, j])
                out_ref[chunk * CHUNK + j, :, :TILE] = high
                out_ref[chunk * CHUNK + j, :, TILE:] = low

            if chunk + STAGES < SLOTS // CHUNK:
                when_live(chunk + STAGES)(copy(chunk + STAGES).start)


def pair_tiles(count, tiles):
    return pl.pallas_call(
        pair_kernel,
        name="pair_tiles",
        out_shape=pltpu.VMEM((SLOTS, TILE, 2 * TILE), jnp.bfloat16),
        in_specs=[smem(), anywhere()],
        out_specs=vmem(),
        scratch_shapes=[
            pltpu.VMEM((STAGES, CHUNK, TILE, TILE), jnp.float32),
            pltpu.SemaphoreType.DMA((STAGES,)),
        ],
        cost_estimate=cost(8),
        compiler_params=pltpu.CompilerParams(vmem_limit_bytes=PAIR_BYTES),
    )(count, tiles)


def class_range(bounds_ref, first, last):
    begin, end = bounds_ref[first], bounds_ref[last]
    return begin, end, (end - begin + GROUP - 1) // GROUP


def forward_kernel(which, bounds_ref, order_ref, rows_ref, slots_ref, tiles_ref, *rest):
    first, last, base, sizes = FORWARD[which]
    buffers = rest[: len(sizes)]
    rest = rest[len(sizes) :]
    prior_ref = rest[0] if which else None
    pairs, total = rest[-2:]
    nrow = total.shape[0] - 1
    begin, end, groups = class_range(bounds_ref, first, last)
    if which:
        total[0:nrow] = prior_ref[...]
    else:
        total[0:nrow] = jnp.zeros((nrow, TILE, TILE), jnp.float32)
    for index, size in enumerate(sizes):
        start = sum(sizes[:index])

        @pl.loop(0, size, unroll=4)
        def _(j):
            high, low = split_high_low(buffers[index][j])
            pairs[start + j, :, :TILE] = high
            pairs[start + j, :, TILE:] = low

    @pl.loop(0, groups)
    def _(group):
        for j in range(GROUP):
            spot = group * GROUP + j
            place = jnp.minimum(begin + spot, SLOTS - 1)
            live = begin + spot < end
            row = jnp.where(live, rows_ref[place], nrow)
            slot = jnp.where(live, slots_ref[place] - base, 0)
            right = pairs[slot]
            product = jnp.dot(
                tiles_ref[order_ref[place]],
                jnp.concatenate([right, right], axis=0),
                preferred_element_type=jnp.float32,
            )
            total[row] += product[:, :TILE] + product[:, TILE:]

    if which == len(FORWARD) - 1:
        core = bounds_ref[CORE]
        part = nrow // 4
        for index, out_ref in enumerate(rest[-6:-2]):
            side = core if index < 2 else 1 - core
            out_ref[...] = total[pl.ds((side * 2 + index % 2) * part, part)]
    else:
        rest[-3][...] = total[0:nrow]


def backward_kernel(which, bounds_ref, order_ref, rows_ref, slots_ref, tiles_ref, slope_ref, *rest):
    first, last, base, sizes, extra = BACKWARD[which]
    if which == 0:
        weight_term_ref, *rest = rest
    buffers = rest[: len(sizes)]
    total, out_sems, *rest = rest[len(sizes) :]
    if which == 0:
        (term_sems,) = rest
        term_copies = [
            pltpu.make_async_copy(weight_term_ref, buffer.at[PER], term_sems.at[index])
            for index, buffer in enumerate(buffers)
        ]
        for copy in term_copies:
            copy.start()
    begin, end, groups = class_range(bounds_ref, first, last)
    @pl.loop(0, sum(sizes), unroll=4)
    def _(slot):
        total[slot] = jnp.zeros((TILE, TILE), jnp.float32)

    @pl.loop(0, groups)
    def _(group):
        for j in range(GROUP):
            spot = group * GROUP + j
            place = jnp.minimum(begin + spot, SLOTS - 1)
            live = begin + spot < end
            slot = jnp.where(live, slots_ref[place] - base, sum(sizes))
            right = tiles_ref[order_ref[place]]
            product = jnp.dot(
                slope_ref[rows_ref[place]],
                jnp.concatenate([right, right], axis=0),
                preferred_element_type=jnp.float32,
            )
            total[slot] += product[:, :TILE] + product[:, TILE:]

    copies = []
    for index, size in enumerate(sizes):
        copy = pltpu.make_async_copy(
            total.at[pl.ds(sum(sizes[:index]), size)],
            buffers[index].at[pl.ds(0, size)],
            out_sems.at[index],
        )
        copy.start()
        copies.append(copy)
    if which == 0:
        copies += term_copies
    for copy in copies:
        copy.wait()


def smem():
    return pl.BlockSpec(memory_space=pltpu.SMEM)


def vmem():
    return pl.BlockSpec(memory_space=pltpu.VMEM)


def anywhere():
    return pl.BlockSpec(memory_space=pl.ANY)


def cost(microseconds):
    return pl.CostEstimate(
        flops=int(microseconds * 1.1e9), bytes_accessed=1 << 20, transcendentals=0
    )


def forward_part(which, plan, tiles, buffers, prior, nrow):
    extra = [prior] if which else []
    sizes = FORWARD[which][-1]
    out_shape = [jax.ShapeDtypeStruct((nrow, TILE, TILE), jnp.float32)]
    if which == len(FORWARD) - 1:
        out_shape = [jax.ShapeDtypeStruct((nrow // 4, TILE, TILE), jnp.float32)] * 4
    return pl.pallas_call(
        functools.partial(forward_kernel, which),
        name="forward_tiles_%d" % which,
        out_shape=out_shape,
        in_specs=[smem()] * 4 + [vmem()] * (1 + len(sizes) + len(extra)),
        out_specs=[vmem()] * len(out_shape),
        scratch_shapes=[
            pltpu.VMEM((sum(sizes), TILE, 2 * TILE), jnp.bfloat16),
            pltpu.VMEM((nrow + 1, TILE, TILE), jnp.float32),
        ],
        cost_estimate=cost((6, 5, 2)[which]),
        compiler_params=pltpu.CompilerParams(vmem_limit_bytes=VMEM_BYTES),
    )(*plan, tiles, *buffers, *extra)


def backward_part(which, plan, tiles, slope, weight_term=()):
    sizes, extra = BACKWARD[which][-2:]
    return pl.pallas_call(
        functools.partial(backward_kernel, which),
        name="backward_tiles_%d" % which,
        out_shape=[
            jax.ShapeDtypeStruct((size + more, TILE, TILE), jnp.float32)
            for size, more in zip(sizes, extra)
        ],
        in_specs=[smem()] * 4 + [vmem()] * (2 + len(weight_term)),
        out_specs=[anywhere()] * len(sizes),
        scratch_shapes=[
            pltpu.VMEM((sum(sizes) + 1, TILE, TILE), jnp.float32),
            pltpu.SemaphoreType.DMA((len(sizes),)),
        ]
        + [pltpu.SemaphoreType.DMA((2,))] * len(weight_term),
        cost_estimate=cost((3, 8)[which]),
        compiler_params=pltpu.CompilerParams(vmem_limit_bytes=VMEM_BYTES),
    )(*plan, tiles, slope, *weight_term)


def triple_left(value):
    high, low = split_high_low(value)
    return jnp.concatenate([high, low, high], axis=1)


def triple_right(value, axis):
    high, low = split_high_low(value)
    return jnp.concatenate([high, high, low], axis=axis)


def middle_kernel(which, bounds_ref, across_ref, weight_ref, cotangent_ref, *rest):
    kept_ref, other_ref = rest[0:2]
    core = bounds_ref[CORE]
    part = kept_ref.shape[0]
    across = triple_left(across_ref[...])
    weight = triple_left(weight_ref[...])
    if which == 0:
        activated_ref, spread_ref, weight_term_ref = rest[-3:]
        weight_term = jnp.zeros((TILE, TILE), jnp.float32)
    else:
        early_activated_ref, early_spread_ref, early_term_ref = rest[3:6]
        activated_ref, spread_ref, weight_term_ref = rest[-3:]
        weight_term = early_term_ref[...]
    for index, source in enumerate((kept_ref, other_ref)):
        side = core if index == 0 else 1 - core
        row = (side * 2 + which) * part
        columns = pl.ds(pl.multiple_of(row * TILE, part * TILE), part * TILE)
        block = source[...].reshape(part * TILE, TILE)
        value = lax.dot_general(
            across,
            triple_right(block, 1),
            (((1,), (1,)), ((), ())),
            preferred_element_type=jnp.float32,
        )
        square = value * value
        bend = jnp.tanh(GELU_SCALE * (value + GELU_CUBE * (square * value)))
        activated = 0.5 * value * (1.0 + bend)
        rate = 0.5 * (1.0 + bend) + 0.5 * value * (1.0 - bend * bend) * (
            GELU_SCALE * (1.0 + 3.0 * GELU_CUBE * square)
        )
        slope = cotangent_ref[:, columns] * rate
        weight_term += jnp.dot(
            triple_left(slope), triple_right(block, 0), preferred_element_type=jnp.float32
        )
        spread = jnp.dot(weight, triple_right(slope, 0), preferred_element_type=jnp.float32)
        high, low = split_high_low(spread)
        place = index * part if which == 0 else row
        for j in range(part):
            spread_ref[place + j, :, :TILE] = high[:, j * TILE : (j + 1) * TILE]
            spread_ref[place + j, :, TILE:] = low[:, j * TILE : (j + 1) * TILE]
        if which == 0:
            activated_ref[index] = activated
        else:
            activated_ref[:, columns] = activated
            early = side * 2 * part
            early_columns = pl.ds(pl.multiple_of(early * TILE, part * TILE), part * TILE)
            activated_ref[:, early_columns] = early_activated_ref[index]
            spread_ref[pl.ds(early, part)] = early_spread_ref[index * part : (index + 1) * part]
    weight_term_ref[...] = jnp.transpose(weight_term) if which else weight_term


def middle_part(which, bounds, across, weight, cotangent, kept, other, pairs, early=()):
    part = kept.shape[0]
    rows = 4 * part if which else 2 * part
    activated = cotangent.shape if which else (2, TILE, part * TILE)
    return pl.pallas_call(
        functools.partial(middle_kernel, which),
        name="middle_%d" % which,
        out_shape=[
            jax.ShapeDtypeStruct(activated, jnp.float32),
            jax.ShapeDtypeStruct((rows, TILE, 2 * TILE), jnp.bfloat16),
            jax.ShapeDtypeStruct(weight.shape, jnp.float32),
        ],
        in_specs=[smem()] + [vmem()] * (6 + len(early)),
        out_specs=[vmem()] * 3,
        cost_estimate=cost(2),
        compiler_params=pltpu.CompilerParams(vmem_limit_bytes=VMEM_BYTES),
    )(bounds, across, weight, cotangent, kept, other, pairs, *early)


def ring_sum_kernel(which, bounds_ref, own_ref, one_ref, two_ref, three_ref, out_ref):
    refs = (own_ref, one_ref, two_ref, three_ref)
    for place in range(SIDE):

        @pl.when(bounds_ref[FIRST + which] == place)
        def _():
            parts = [refs[(index - place) % SIDE] for index in range(SIDE)]
            out_ref[...] = (parts[0][...] + parts[1][...]) + (parts[2][...] + parts[3][...])


def ring_sum(which, bounds, parts):
    return pl.pallas_call(
        functools.partial(ring_sum_kernel, which),
        name="ring_sum_%d" % which,
        out_shape=jax.ShapeDtypeStruct((TILE, TILE), jnp.float32),
        in_specs=[smem()] + [vmem()] * SIDE,
        out_specs=vmem(),
        compiler_params=pltpu.CompilerParams(vmem_limit_bytes=VMEM_BYTES),
    )(bounds, *parts)


def assemble_kernel(
    bounds_ref, own_ref, own_other_ref, across_ref, across_other_ref, term_ref, out_ref, sum_ref
):
    core, low = bounds_ref[CORE], bounds_ref[LOW]
    for source, chip, side in (
        (own_ref, low, core),
        (own_other_ref, low, 1 - core),
        (across_ref, 1 - low, core),
        (across_other_ref, 1 - low, 1 - core),
    ):
        for j in range(4):
            place = (chip * 2 + side) * 4 + j
            out_ref[:, pl.ds(pl.multiple_of(place * TILE, TILE), TILE)] = source[j]

    @pl.when(core == 0)
    def _():
        sum_ref[...] = term_ref[...]

    @pl.when(core == 1)
    def _():
        sum_ref[...] = own_other_ref[4]


def assemble(bounds, parts):
    return pl.pallas_call(
        assemble_kernel,
        name="assemble",
        out_shape=[
            jax.ShapeDtypeStruct((TILE, 16 * TILE), jnp.float32),
            jax.ShapeDtypeStruct((TILE, TILE), jnp.float32),
        ],
        in_specs=[smem()] + [vmem()] * 5,
        out_specs=[vmem()] * 2,
        compiler_params=pltpu.CompilerParams(vmem_limit_bytes=VMEM_BYTES),
    )(bounds, *parts)


def make_plan(rows, cols, count, loop, wide):
    core = loop % 2
    node_block = cols // 4
    across = (node_block // 16) ^ (wide // 16)
    dx = (node_block // 4 - wide // 4) % 4
    dz = (node_block - wide) % 4
    du = jnp.where(core == 0, dx, dz)
    dv = jnp.where(core == 0, dz, dx)
    place = jnp.where(dv == 2, 3, jnp.where(dv == 3, 2, dv))
    start = jnp.where(
        place < 3, (1 - across) * 48 + place * PER, 96 + across * PER
    )
    slots = start + du * 4 + cols % 4
    spots = jnp.arange(SLOTS, dtype=jnp.int32)
    kind = jnp.where(place < 3, 1 - across, 2 + across)
    kind = jnp.where(spots < count[0], kind, 4)
    ahead = (kind[None, :] < kind[:, None]) | (
        (kind[None, :] == kind[:, None]) & (spots[None, :] < spots[:, None])
    )
    rank = jnp.sum(ahead.astype(jnp.int32), axis=1)
    here = rank[None, :] == spots[:, None]

    def sort(values):
        return jnp.sum(jnp.where(here, values[None, :], 0), axis=1)

    inner = du * 4 + cols % 4
    back_slots = jnp.where(
        place < 3, slots, 96 + (inner // HALF) * PER + across * HALF + inner % HALF
    )
    steps = jnp.arange(9, dtype=jnp.int32)
    bounds = jnp.sum((kind[None, :] < steps[:, None]).astype(jnp.int32), axis=1)
    bounds = jnp.where(steps == CORE, loop % 2, jnp.where(steps == LOW, loop // 2, bounds))
    ring = jnp.where(core == 0, wide // 4 % 4, wide % 4)
    other_ring = jnp.where(core == 0, wide % 4, wide // 4 % 4)
    bounds = jnp.where(steps == FIRST, ring, jnp.where(steps == FIRST + 1, other_ring, bounds))
    return bounds, sort(spots), sort(rows), sort(slots), sort(back_slots)


def quarter_tiles(features, index):
    feats = features.shape[0]
    split = features.reshape(feats, 4, 4, TILE)
    piece = lax.dynamic_index_in_dim(split, index, 1, keepdims=False)
    return jnp.transpose(piece, (1, 2, 0))


def gather_own(features, loop):
    own = quarter_tiles(features, loop)
    one, three, two = permute(own, u_down), permute(own, u_up), permute(own, u_far)
    partner = permute(quarter_tiles(features, loop ^ 2), y_partner)
    return own, one, two, three, partner


def with_tile(value, tile):
    return jnp.concatenate([value, tile[None]], axis=0)


def add_part(value, part, start):
    size = part.shape[0]
    return lax.dynamic_update_slice_in_dim(value, value[start : start + size] + part, start, 0)


def scatter_terms(plan, pairs, spread, weight_term):
    back_plan = plan[:3] + plan[4:]
    up, down, spread = tie(*backward_part(0, back_plan, pairs, spread, (weight_term,)), spread)
    up, down = permute(up, v_up), permute(down, v_down)
    zero, one, three, own, own_one, own_three = backward_part(1, back_plan, pairs, spread)
    one = lax.dynamic_update_slice_in_dim(add_part(one, up[HALF:PER], 0), up[PER:], PER, 0)
    three = add_part(three, down[HALF:PER], HALF)
    one, three = permute(one, v_up), permute(three, v_down)
    own_one = permute(add_part(own_one, up[:HALF], 0), v_up)
    own_three = permute(add_part(own_three, down[:HALF], HALF), v_down)
    weight_term = ring_sum(1, plan[0], (weight_term, down[PER], one[PER], up[PER]))
    apart = zero + one[:PER] + three
    apart_two = permute(apart[8:12], u_far)
    apart_far = permute(
        jnp.concatenate([apart[4:8], apart[12:16], weight_term[None]], axis=0), y_far
    )
    last, apart_far = tie(apart[:4] + apart_two, apart_far)
    last = permute(last, y_far)
    weight_term = weight_term + apart_far[8]
    total = own + own_one + own_three
    two = permute(with_tile(total[8:12], weight_term), u_far)
    one = permute(with_tile(total[4:8] + apart_far[:4], weight_term), u_up)
    three = permute(with_tile(total[12:16] + apart_far[4:8], weight_term), u_down)
    weight_term = ring_sum(0, plan[0], (weight_term, three[4], two[4], one[4]))
    return total[:4] + last + one[:4] + two[:4] + three[:4], weight_term


def per_device(features, weight, cotangent, tiles, tile_rows, tile_cols, counts):
    nrow = features.shape[1] // TILE
    loop = lax.axis_index(LOOP)
    wide = lax.axis_index(WIDE)
    tile_collection = tiles.reshape(SLOTS, TILE, TILE)
    count = counts.reshape(1)
    plan = make_plan(tile_rows.reshape(SLOTS), tile_cols.reshape(SLOTS), count, loop, wide)
    across = weight.T

    own, one, two, three, partner = gather_own(features, loop)
    first = jnp.concatenate([own, one], axis=0)
    second = jnp.concatenate([two, three], axis=0)
    plan, across, first, second, partner = tie(plan, across, first, second, partner)
    one_first, three_second = permute(first, v_down), permute(second, v_up)
    second_far = permute(second, y_far)
    one_second, three_first = permute(second, v_down), permute(first, v_up)
    partner_one = permute(partner, u_down)
    count, one_first = tie(count, one_first)
    pairs = pair_tiles(count, tile_collection)
    near = [first, second, one_first, one_second, three_first, three_second]
    far = [permute(one_first, v_down), permute(three_second, v_up)]
    second_far, partner_one, *far = tie(second_far, partner_one, *far)
    first, second = jnp.concatenate([partner, partner_one], axis=0), second_far
    one_first, three_second = permute(first, v_down), permute(second, v_up)
    partial = forward_part(0, plan[:4], pairs, near + far, None, nrow)
    first, second, partial = tie(first, second, partial[0])
    one_second, three_first = permute(second, v_down), permute(first, v_up)
    apart = [first, second, one_first, one_second, three_first, three_second]
    far = [permute(one_first, v_down), permute(three_second, v_up)]
    partial = forward_part(1, plan[:4], pairs, apart, partial, nrow)
    *kept, given_first, given_second = forward_part(2, plan[:4], pairs, far, partial[0], nrow)

    bounds = plan[0]
    kept = [kept[0] + permute(given_first, core_swap), kept[1] + permute(given_second, core_swap)]
    kept = [value + permute(value, y_pair) for value in kept]
    early = middle_part(
        0, bounds, across, weight, cotangent, kept[0], permute(kept[0], core_swap), pairs
    )
    activated, spread, weight_term = middle_part(
        1, bounds, across, weight, cotangent, kept[1], permute(kept[1], core_swap), pairs, early
    )
    total, weight_term = scatter_terms(plan, pairs, spread, weight_term)
    far_total = permute(total, y_pair)
    own_other = permute(with_tile(total, weight_term), core_swap)
    parts = [total, own_other, far_total, permute(far_total, core_swap), weight_term]
    return (activated, *assemble(bounds, parts))


def solution(mesh):
    split = jax.sharding.Mesh(mesh.devices.reshape(2, 2, 2, SIDE, SIDE), AXES)
    return jax.shard_map(
        per_device,
        mesh=split,
        in_specs=(
            P(None, WIDE),
            P(),
            P(None, WIDE),
            P(LOOP, WIDE, None, None, None),
            P(LOOP, WIDE, None),
            P(LOOP, WIDE, None),
            P(LOOP, WIDE),
        ),
        out_specs=(P(None, WIDE), P(None, WIDE), P()),
        check_vma=False,
    )
```

```python
import functools

import jax
import jax.numpy as jnp
from jax import lax
from jax.experimental import pallas as pl
from jax.experimental.pallas import tpu as pltpu
from jax.sharding import PartitionSpec as P

HI = lax.Precision.HIGHEST
GELU_SCALE = 0.7978845608028654
GELU_CUBE = 0.044715
AXES = ("y_lo", "core", "y_hi", "x", "z")
LOOP = ("y_lo", "core")
WIDE = ("y_hi", "x", "z")
SIDE = 4
TILE = 128
SLOTS = 256
GROUP = 16
CHUNK = 32
STAGES = 4
PAIR_BYTES = 30 * 1024 * 1024
PER = 16
HALF = 8
FORWARD = (
    (1, 3, 48, (HALF,) * 8),
    (0, 1, 0, (HALF,) * 6),
    (3, 4, 112, (HALF,) * 2),
)
BACKWARD = (
    (2, 4, 96, (PER, PER), (1, 1)),
    (0, 2, 0, (PER,) * 6, (0, 1, 0, 0, 0, 0)),
)
CORE = 5
LOW = 6
FIRST = 7
VMEM_BYTES = 8 * 1024 * 1024


def device_index(y, core, x, z):
    y, x, z = y % SIDE, x % SIDE, z % SIDE
    return (((y & 1) * 2 + core) * 2 + (y >> 1)) * 16 + x * SIDE + z


def permute(value, move):
    pairs = []
    for y in range(SIDE):
        for core in range(2):
            for x in range(SIDE):
                for z in range(SIDE):
                    pairs.append((device_index(y, core, x, z), device_index(*move(y, core, x, z))))
    return lax.ppermute(value, AXES, pairs)


def along(first, step):
    def move(y, core, x, z):
        if (core == 0) == first:
            return (y, core, x + step, z)
        return (y, core, x, z + step)

    return move


u_up, u_down, u_far = along(True, 1), along(True, -1), along(True, 2)
v_up, v_down = along(False, 1), along(False, -1)


def y_partner(y, core, x, z):
    return (3 - y, core, x, z)


def y_pair(y, core, x, z):
    return (y ^ 1, core, x, z)


def y_far(y, core, x, z):
    return (y + 2, core, x, z)


def core_swap(y, core, x, z):
    return (y, 1 - core, x, z)


def tie(*values):
    return lax.optimization_barrier(values)


def split_high_low(value):
    high = value.astype(jnp.bfloat16)
    low = (value - high.astype(jnp.float32)).astype(jnp.bfloat16)
    return high, low


def pair_kernel(count_ref, tiles_ref, out_ref, held, sems):
    count = count_ref[0]

    def copy(chunk):
        source = tiles_ref.at[pl.ds(chunk * CHUNK, CHUNK)]
        return pltpu.make_async_copy(source, held.at[chunk % STAGES], sems.at[chunk % STAGES])

    def when_live(chunk):
        return pl.when(chunk * CHUNK < count)

    for chunk in range(STAGES):
        when_live(chunk)(copy(chunk).start)
    for chunk in range(SLOTS // CHUNK):

        @when_live(chunk)
        def _():
            copy(chunk).wait()

            @pl.loop(0, CHUNK, unroll=8)
            def _(j):
                high, low = split_high_low(held[chunk % STAGES, j])
                out_ref[chunk * CHUNK + j, :, :TILE] = high
                out_ref[chunk * CHUNK + j, :, TILE:] = low

            if chunk + STAGES < SLOTS // CHUNK:
                when_live(chunk + STAGES)(copy(chunk + STAGES).start)


def pair_tiles(count, tiles):
    return pl.pallas_call(
        pair_kernel,
        name="pair_tiles",
        out_shape=pltpu.VMEM((SLOTS, TILE, 2 * TILE), jnp.bfloat16),
        in_specs=[smem(), anywhere()],
        out_specs=vmem(),
        scratch_shapes=[
            pltpu.VMEM((STAGES, CHUNK, TILE, TILE), jnp.float32),
            pltpu.SemaphoreType.DMA((STAGES,)),
        ],
        cost_estimate=cost(8),
        compiler_params=pltpu.CompilerParams(vmem_limit_bytes=PAIR_BYTES),
    )(count, tiles)


def class_range(bounds_ref, first, last):
    begin, end = bounds_ref[first], bounds_ref[last]
    return begin, end, (end - begin + GROUP - 1) // GROUP


def forward_kernel(which, bounds_ref, order_ref, rows_ref, slots_ref, tiles_ref, *rest):
    first, last, base, sizes = FORWARD[which]
    buffers = rest[: len(sizes)]
    rest = rest[len(sizes) :]
    prior_ref = rest[0] if which else None
    pairs, total = rest[-2:]
    nrow = total.shape[0] - 1
    begin, end, groups = class_range(bounds_ref, first, last)
    if which:
        total[0:nrow] = prior_ref[...]
    else:
        total[0:nrow] = jnp.zeros((nrow, TILE, TILE), jnp.float32)
    for index, size in enumerate(sizes):
        start = sum(sizes[:index])

        @pl.loop(0, size, unroll=4)
        def _(j):
            high, low = split_high_low(buffers[index][j])
            pairs[start + j, :, :TILE] = high
            pairs[start + j, :, TILE:] = low

    @pl.loop(0, groups)
    def _(group):
        for j in range(GROUP):
            spot = group * GROUP + j
            place = jnp.minimum(begin + spot, SLOTS - 1)
            live = begin + spot < end
            row = jnp.where(live, rows_ref[place], nrow)
            slot = jnp.where(live, slots_ref[place] - base, 0)
            right = pairs[slot]
            product = jnp.dot(
                tiles_ref[order_ref[place]],
                jnp.concatenate([right, right], axis=0),
                preferred_element_type=jnp.float32,
            )
            total[row] += product[:, :TILE] + product[:, TILE:]

    if which == len(FORWARD) - 1:
        core = bounds_ref[CORE]
        part = nrow // 4
        for index, out_ref in enumerate(rest[-6:-2]):
            side = core if index < 2 else 1 - core
            out_ref[...] = total[pl.ds((side * 2 + index % 2) * part, part)]
    else:
        rest[-3][...] = total[0:nrow]


def backward_kernel(which, bounds_ref, order_ref, rows_ref, slots_ref, tiles_ref, slope_ref, *rest):
    first, last, base, sizes, extra = BACKWARD[which]
    if which == 0:
        weight_term_ref, *rest = rest
    buffers = rest[: len(sizes)]
    total, out_sems, *rest = rest[len(sizes) :]
    if which == 0:
        (term_sems,) = rest
        term_copies = [
            pltpu.make_async_copy(weight_term_ref, buffer.at[PER], term_sems.at[index])
            for index, buffer in enumerate(buffers)
        ]
        for copy in term_copies:
            copy.start()
    begin, end, groups = class_range(bounds_ref, first, last)
    @pl.loop(0, sum(sizes), unroll=4)
    def _(slot):
        total[slot] = jnp.zeros((TILE, TILE), jnp.float32)

    @pl.loop(0, groups)
    def _(group):
        for j in range(GROUP):
            spot = group * GROUP + j
            place = jnp.minimum(begin + spot, SLOTS - 1)
            live = begin + spot < end
            slot = jnp.where(live, slots_ref[place] - base, sum(sizes))
            right = tiles_ref[order_ref[place]]
            product = jnp.dot(
                slope_ref[rows_ref[place]],
                jnp.concatenate([right, right], axis=0),
                preferred_element_type=jnp.float32,
            )
            total[slot] += product[:, :TILE] + product[:, TILE:]

    copies = []
    for index, size in enumerate(sizes):
        copy = pltpu.make_async_copy(
            total.at[pl.ds(sum(sizes[:index]), size)],
            buffers[index].at[pl.ds(0, size)],
            out_sems.at[index],
        )
        copy.start()
        copies.append(copy)
    if which == 0:
        copies += term_copies
    for copy in copies:
        copy.wait()


def smem():
    return pl.BlockSpec(memory_space=pltpu.SMEM)


def vmem():
    return pl.BlockSpec(memory_space=pltpu.VMEM)


def anywhere():
    return pl.BlockSpec(memory_space=pl.ANY)


def cost(microseconds):
    return pl.CostEstimate(
        flops=int(microseconds * 1.1e9), bytes_accessed=1 << 20, transcendentals=0
    )


def forward_part(which, plan, tiles, buffers, prior, nrow):
    extra = [prior] if which else []
    sizes = FORWARD[which][-1]
    out_shape = [jax.ShapeDtypeStruct((nrow, TILE, TILE), jnp.float32)]
    if which == len(FORWARD) - 1:
        out_shape = [jax.ShapeDtypeStruct((nrow // 4, TILE, TILE), jnp.float32)] * 4
    return pl.pallas_call(
        functools.partial(forward_kernel, which),
        name="forward_tiles_%d" % which,
        out_shape=out_shape,
        in_specs=[smem()] * 4 + [vmem()] * (1 + len(sizes) + len(extra)),
        out_specs=[vmem()] * len(out_shape),
        scratch_shapes=[
            pltpu.VMEM((sum(sizes), TILE, 2 * TILE), jnp.bfloat16),
            pltpu.VMEM((nrow + 1, TILE, TILE), jnp.float32),
        ],
        cost_estimate=cost((6, 5, 2)[which]),
        compiler_params=pltpu.CompilerParams(vmem_limit_bytes=VMEM_BYTES),
    )(*plan, tiles, *buffers, *extra)


def backward_part(which, plan, tiles, slope, weight_term=()):
    sizes, extra = BACKWARD[which][-2:]
    return pl.pallas_call(
        functools.partial(backward_kernel, which),
        name="backward_tiles_%d" % which,
        out_shape=[
            jax.ShapeDtypeStruct((size + more, TILE, TILE), jnp.float32)
            for size, more in zip(sizes, extra)
        ],
        in_specs=[smem()] * 4 + [vmem()] * (2 + len(weight_term)),
        out_specs=[anywhere()] * len(sizes),
        scratch_shapes=[
            pltpu.VMEM((sum(sizes) + 1, TILE, TILE), jnp.float32),
            pltpu.SemaphoreType.DMA((len(sizes),)),
        ]
        + [pltpu.SemaphoreType.DMA((2,))] * len(weight_term),
        cost_estimate=cost((3, 8)[which]),
        compiler_params=pltpu.CompilerParams(vmem_limit_bytes=VMEM_BYTES),
    )(*plan, tiles, slope, *weight_term)


def triple_left(value):
    high, low = split_high_low(value)
    return jnp.concatenate([high, low, high], axis=1)


def triple_right(value, axis):
    high, low = split_high_low(value)
    return jnp.concatenate([high, high, low], axis=axis)


def middle_kernel(which, bounds_ref, across_ref, weight_ref, cotangent_ref, *rest):
    kept_ref, other_ref = rest[0:2]
    core = bounds_ref[CORE]
    part = kept_ref.shape[0]
    across = triple_left(across_ref[...])
    weight = triple_left(weight_ref[...])
    if which == 0:
        activated_ref, spread_ref, weight_term_ref = rest[-3:]
        weight_term = jnp.zeros((TILE, TILE), jnp.float32)
    else:
        early_activated_ref, early_spread_ref, early_term_ref = rest[3:6]
        activated_ref, spread_ref, weight_term_ref = rest[-3:]
        weight_term = early_term_ref[...]
    for index, source in enumerate((kept_ref, other_ref)):
        side = core if index == 0 else 1 - core
        row = (side * 2 + which) * part
        columns = pl.ds(pl.multiple_of(row * TILE, part * TILE), part * TILE)
        block = source[...].reshape(part * TILE, TILE)
        value = lax.dot_general(
            across,
            triple_right(block, 1),
            (((1,), (1,)), ((), ())),
            preferred_element_type=jnp.float32,
        )
        square = value * value
        bend = jnp.tanh(GELU_SCALE * (value + GELU_CUBE * (square * value)))
        activated = 0.5 * value * (1.0 + bend)
        rate = 0.5 * (1.0 + bend) + 0.5 * value * (1.0 - bend * bend) * (
            GELU_SCALE * (1.0 + 3.0 * GELU_CUBE * square)
        )
        slope = cotangent_ref[:, columns] * rate
        weight_term += jnp.dot(
            triple_left(slope), triple_right(block, 0), preferred_element_type=jnp.float32
        )
        spread = jnp.dot(weight, triple_right(slope, 0), preferred_element_type=jnp.float32)
        high, low = split_high_low(spread)
        place = index * part if which == 0 else row
        for j in range(part):
            spread_ref[place + j, :, :TILE] = high[:, j * TILE : (j + 1) * TILE]
            spread_ref[place + j, :, TILE:] = low[:, j * TILE : (j + 1) * TILE]
        if which == 0:
            activated_ref[index] = activated
        else:
            activated_ref[:, columns] = activated
            early = side * 2 * part
            early_columns = pl.ds(pl.multiple_of(early * TILE, part * TILE), part * TILE)
            activated_ref[:, early_columns] = early_activated_ref[index]
            spread_ref[pl.ds(early, part)] = early_spread_ref[index * part : (index + 1) * part]
    weight_term_ref[...] = jnp.transpose(weight_term) if which else weight_term


def middle_part(which, bounds, across, weight, cotangent, kept, other, pairs, early=()):
    part = kept.shape[0]
    rows = 4 * part if which else 2 * part
    activated = cotangent.shape if which else (2, TILE, part * TILE)
    return pl.pallas_call(
        functools.partial(middle_kernel, which),
        name="middle_%d" % which,
        out_shape=[
            jax.ShapeDtypeStruct(activated, jnp.float32),
            jax.ShapeDtypeStruct((rows, TILE, 2 * TILE), jnp.bfloat16),
            jax.ShapeDtypeStruct(weight.shape, jnp.float32),
        ],
        in_specs=[smem()] + [vmem()] * (6 + len(early)),
        out_specs=[vmem()] * 3,
        cost_estimate=cost(2),
        compiler_params=pltpu.CompilerParams(vmem_limit_bytes=VMEM_BYTES),
    )(bounds, across, weight, cotangent, kept, other, pairs, *early)


def ring_sum_kernel(which, bounds_ref, own_ref, one_ref, two_ref, three_ref, out_ref):
    refs = (own_ref, one_ref, two_ref, three_ref)
    for place in range(SIDE):

        @pl.when(bounds_ref[FIRST + which] == place)
        def _():
            parts = [refs[(index - place) % SIDE] for index in range(SIDE)]
            out_ref[...] = (parts[0][...] + parts[1][...]) + (parts[2][...] + parts[3][...])


def ring_sum(which, bounds, parts):
    return pl.pallas_call(
        functools.partial(ring_sum_kernel, which),
        name="ring_sum_%d" % which,
        out_shape=jax.ShapeDtypeStruct((TILE, TILE), jnp.float32),
        in_specs=[smem()] + [vmem()] * SIDE,
        out_specs=vmem(),
        compiler_params=pltpu.CompilerParams(vmem_limit_bytes=VMEM_BYTES),
    )(bounds, *parts)


def assemble_kernel(
    bounds_ref, own_ref, own_other_ref, across_ref, across_other_ref, term_ref, out_ref, sum_ref
):
    core, low = bounds_ref[CORE], bounds_ref[LOW]
    for source, chip, side in (
        (own_ref, low, core),
        (own_other_ref, low, 1 - core),
        (across_ref, 1 - low, core),
        (across_other_ref, 1 - low, 1 - core),
    ):
        for j in range(4):
            place = (chip * 2 + side) * 4 + j
            out_ref[:, pl.ds(pl.multiple_of(place * TILE, TILE), TILE)] = source[j]

    @pl.when(core == 0)
    def _():
        sum_ref[...] = term_ref[...]

    @pl.when(core == 1)
    def _():
        sum_ref[...] = own_other_ref[4]


def assemble(bounds, parts):
    return pl.pallas_call(
        assemble_kernel,
        name="assemble",
        out_shape=[
            jax.ShapeDtypeStruct((TILE, 16 * TILE), jnp.float32),
            jax.ShapeDtypeStruct((TILE, TILE), jnp.float32),
        ],
        in_specs=[smem()] + [vmem()] * 5,
        out_specs=[vmem()] * 2,
        compiler_params=pltpu.CompilerParams(vmem_limit_bytes=VMEM_BYTES),
    )(bounds, *parts)


def make_plan(rows, cols, count, loop, wide):
    core = loop % 2
    node_block = cols // 4
    across = (node_block // 16) ^ (wide // 16)
    dx = (node_block // 4 - wide // 4) % 4
    dz = (node_block - wide) % 4
    du = jnp.where(core == 0, dx, dz)
    dv = jnp.where(core == 0, dz, dx)
    place = jnp.where(dv == 2, 3, jnp.where(dv == 3, 2, dv))
    start = jnp.where(
        place < 3, (1 - across) * 48 + place * PER, 96 + across * PER
    )
    slots = start + du * 4 + cols % 4
    spots = jnp.arange(SLOTS, dtype=jnp.int32)
    kind = jnp.where(place < 3, 1 - across, 2 + across)
    kind = jnp.where(spots < count[0], kind, 4)
    ahead = (kind[None, :] < kind[:, None]) | (
        (kind[None, :] == kind[:, None]) & (spots[None, :] < spots[:, None])
    )
    rank = jnp.sum(ahead.astype(jnp.int32), axis=1)
    here = rank[None, :] == spots[:, None]

    def sort(values):
        return jnp.sum(jnp.where(here, values[None, :], 0), axis=1)

    inner = du * 4 + cols % 4
    back_slots = jnp.where(
        place < 3, slots, 96 + (inner // HALF) * PER + across * HALF + inner % HALF
    )
    steps = jnp.arange(9, dtype=jnp.int32)
    bounds = jnp.sum((kind[None, :] < steps[:, None]).astype(jnp.int32), axis=1)
    bounds = jnp.where(steps == CORE, loop % 2, jnp.where(steps == LOW, loop // 2, bounds))
    ring = jnp.where(core == 0, wide // 4 % 4, wide % 4)
    other_ring = jnp.where(core == 0, wide % 4, wide // 4 % 4)
    bounds = jnp.where(steps == FIRST, ring, jnp.where(steps == FIRST + 1, other_ring, bounds))
    return bounds, sort(spots), sort(rows), sort(slots), sort(back_slots)


def quarter_tiles(features, index):
    feats = features.shape[0]
    split = features.reshape(feats, 4, 4, TILE)
    piece = lax.dynamic_index_in_dim(split, index, 1, keepdims=False)
    return jnp.transpose(piece, (1, 2, 0))


def gather_own(features, loop):
    own = quarter_tiles(features, loop)
    one, three, two = permute(own, u_down), permute(own, u_up), permute(own, u_far)
    partner = permute(quarter_tiles(features, loop ^ 2), y_partner)
    return own, one, two, three, partner


def with_tile(value, tile):
    return jnp.concatenate([value, tile[None]], axis=0)


def add_part(value, part, start):
    size = part.shape[0]
    return lax.dynamic_update_slice_in_dim(value, value[start : start + size] + part, start, 0)


def scatter_terms(plan, pairs, spread, weight_term):
    back_plan = plan[:3] + plan[4:]
    up, down, spread = tie(*backward_part(0, back_plan, pairs, spread, (weight_term,)), spread)
    up, down = permute(up, v_up), permute(down, v_down)
    zero, one, three, own, own_one, own_three = backward_part(1, back_plan, pairs, spread)
    one = lax.dynamic_update_slice_in_dim(add_part(one, up[HALF:PER], 0), up[PER:], PER, 0)
    three = add_part(three, down[HALF:PER], HALF)
    one, three = permute(one, v_up), permute(three, v_down)
    own_one = permute(add_part(own_one, up[:HALF], 0), v_up)
    own_three = permute(add_part(own_three, down[:HALF], HALF), v_down)
    weight_term = ring_sum(1, plan[0], (weight_term, down[PER], one[PER], up[PER]))
    apart = zero + one[:PER] + three
    apart_two = permute(apart[8:12], u_far)
    apart_far = permute(
        jnp.concatenate([apart[4:8], apart[12:16], weight_term[None]], axis=0), y_far
    )
    last, apart_far = tie(apart[:4] + apart_two, apart_far)
    last = permute(last, y_far)
    weight_term = weight_term + apart_far[8]
    total = own + own_one + own_three
    two = permute(with_tile(total[8:12], weight_term), u_far)
    one = permute(with_tile(total[4:8] + apart_far[:4], weight_term), u_up)
    three = permute(with_tile(total[12:16] + apart_far[4:8], weight_term), u_down)
    weight_term = ring_sum(0, plan[0], (weight_term, three[4], two[4], one[4]))
    return total[:4] + last + one[:4] + two[:4] + three[:4], weight_term


def per_device(features, weight, cotangent, tiles, tile_rows, tile_cols, counts):
    nrow = features.shape[1] // TILE
    loop = lax.axis_index(LOOP)
    wide = lax.axis_index(WIDE)
    tile_collection = tiles.reshape(SLOTS, TILE, TILE)
    count = counts.reshape(1)
    plan = make_plan(tile_rows.reshape(SLOTS), tile_cols.reshape(SLOTS), count, loop, wide)
    across = weight.T

    own, one, two, three, partner = gather_own(features, loop)
    first = jnp.concatenate([own, one], axis=0)
    second = jnp.concatenate([two, three], axis=0)
    plan, across, first, second, partner = tie(plan, across, first, second, partner)
    one_first, three_second = permute(first, v_down), permute(second, v_up)
    second_far = permute(second, y_far)
    one_second, three_first = permute(second, v_down), permute(first, v_up)
    count, one_first, partner = tie(count, one_first, partner)
    partner_one = permute(partner, u_down)
    pairs = pair_tiles(count, tile_collection)
    near = [first, second, one_first, one_second, three_first, three_second]
    far = [permute(one_first, v_down), permute(three_second, v_up)]
    second_far, partner_one, *far = tie(second_far, partner_one, *far)
    first, second = jnp.concatenate([partner, partner_one], axis=0), second_far
    one_first, three_second = permute(first, v_down), permute(second, v_up)
    partial = forward_part(0, plan[:4], pairs, near + far, None, nrow)
    first, second, partial = tie(first, second, partial[0])
    one_second, three_first = permute(second, v_down), permute(first, v_up)
    apart = [first, second, one_first, one_second, three_first, three_second]
    far = [permute(one_first, v_down), permute(three_second, v_up)]
    partial = forward_part(1, plan[:4], pairs, apart, partial, nrow)
    *kept, given_first, given_second = forward_part(2, plan[:4], pairs, far, partial[0], nrow)

    bounds = plan[0]
    kept = [kept[0] + permute(given_first, core_swap), kept[1] + permute(given_second, core_swap)]
    kept = [value + permute(value, y_pair) for value in kept]
    early = middle_part(
        0, bounds, across, weight, cotangent, kept[0], permute(kept[0], core_swap), pairs
    )
    activated, spread, weight_term = middle_part(
        1, bounds, across, weight, cotangent, kept[1], permute(kept[1], core_swap), pairs, early
    )
    total, weight_term = scatter_terms(plan, pairs, spread, weight_term)
    far_total = permute(total, y_pair)
    own_other = permute(with_tile(total, weight_term), core_swap)
    parts = [total, own_other, far_total, permute(far_total, core_swap), weight_term]
    return (activated, *assemble(bounds, parts))


def solution(mesh):
    split = jax.sharding.Mesh(mesh.devices.reshape(2, 2, 2, SIDE, SIDE), AXES)
    return jax.shard_map(
        per_device,
        mesh=split,
        in_specs=(
            P(None, WIDE),
            P(),
            P(None, WIDE),
            P(LOOP, WIDE, None, None, None),
            P(LOOP, WIDE, None),
            P(LOOP, WIDE, None),
            P(LOOP, WIDE),
        ),
        out_specs=(P(None, WIDE), P(None, WIDE), P()),
        check_vma=False,
    )
```

```python
import functools

import jax
import jax.numpy as jnp
from jax import lax
from jax.experimental import pallas as pl
from jax.experimental.pallas import tpu as pltpu
from jax.sharding import PartitionSpec as P

HI = lax.Precision.HIGHEST
GELU_SCALE = 0.7978845608028654
GELU_CUBE = 0.044715
AXES = ("y_lo", "core", "y_hi", "x", "z")
LOOP = ("y_lo", "core")
WIDE = ("y_hi", "x", "z")
SIDE = 4
TILE = 128
SLOTS = 256
GROUP = 16
CHUNK = 32
STAGES = 4
PAIR_BYTES = 30 * 1024 * 1024
PER = 16
HALF = 8
FORWARD = (
    (1, 3, 48, (HALF,) * 8),
    (0, 1, 0, (HALF,) * 6),
    (3, 4, 112, (HALF,) * 2),
)
BACKWARD = (
    (2, 4, 96, (PER, PER), (1, 1)),
    (0, 2, 0, (PER,) * 6, (0, 1, 0, 0, 0, 0)),
)
CORE = 5
LOW = 6
FIRST = 7
VMEM_BYTES = 8 * 1024 * 1024


def device_index(y, core, x, z):
    y, x, z = y % SIDE, x % SIDE, z % SIDE
    return (((y & 1) * 2 + core) * 2 + (y >> 1)) * 16 + x * SIDE + z


def permute(value, move):
    pairs = []
    for y in range(SIDE):
        for core in range(2):
            for x in range(SIDE):
                for z in range(SIDE):
                    pairs.append((device_index(y, core, x, z), device_index(*move(y, core, x, z))))
    return lax.ppermute(value, AXES, pairs)


def along(first, step):
    def move(y, core, x, z):
        if (core == 0) == first:
            return (y, core, x + step, z)
        return (y, core, x, z + step)

    return move


u_up, u_down, u_far = along(True, 1), along(True, -1), along(True, 2)
v_up, v_down = along(False, 1), along(False, -1)


def y_partner(y, core, x, z):
    return (3 - y, core, x, z)


def y_pair(y, core, x, z):
    return (y ^ 1, core, x, z)


def y_far(y, core, x, z):
    return (y + 2, core, x, z)


def core_swap(y, core, x, z):
    return (y, 1 - core, x, z)


def tie(*values):
    return lax.optimization_barrier(values)


def split_high_low(value):
    high = value.astype(jnp.bfloat16)
    low = (value - high.astype(jnp.float32)).astype(jnp.bfloat16)
    return high, low


def pair_kernel(count_ref, tiles_ref, out_ref, held, sems):
    count = count_ref[0]

    def copy(chunk):
        source = tiles_ref.at[pl.ds(chunk * CHUNK, CHUNK)]
        return pltpu.make_async_copy(source, held.at[chunk % STAGES], sems.at[chunk % STAGES])

    def when_live(chunk):
        return pl.when(chunk * CHUNK < count)

    for chunk in range(STAGES):
        when_live(chunk)(copy(chunk).start)
    for chunk in range(SLOTS // CHUNK):

        @when_live(chunk)
        def _():
            copy(chunk).wait()

            @pl.loop(0, CHUNK, unroll=8)
            def _(j):
                high, low = split_high_low(held[chunk % STAGES, j])
                out_ref[chunk * CHUNK + j, :, :TILE] = high
                out_ref[chunk * CHUNK + j, :, TILE:] = low

            if chunk + STAGES < SLOTS // CHUNK:
                when_live(chunk + STAGES)(copy(chunk + STAGES).start)


def pair_tiles(count, tiles):
    return pl.pallas_call(
        pair_kernel,
        name="pair_tiles",
        out_shape=pltpu.VMEM((SLOTS, TILE, 2 * TILE), jnp.bfloat16),
        in_specs=[smem(), anywhere()],
        out_specs=vmem(),
        scratch_shapes=[
            pltpu.VMEM((STAGES, CHUNK, TILE, TILE), jnp.float32),
            pltpu.SemaphoreType.DMA((STAGES,)),
        ],
        cost_estimate=cost(8),
        compiler_params=pltpu.CompilerParams(vmem_limit_bytes=PAIR_BYTES),
    )(count, tiles)


def class_range(bounds_ref, first, last):
    begin, end = bounds_ref[first], bounds_ref[last]
    return begin, end, (end - begin + GROUP - 1) // GROUP


def forward_kernel(which, bounds_ref, order_ref, rows_ref, slots_ref, tiles_ref, *rest):
    first, last, base, sizes = FORWARD[which]
    buffers = rest[: len(sizes)]
    rest = rest[len(sizes) :]
    prior_ref = rest[0] if which else None
    pairs, total = rest[-2:]
    nrow = total.shape[0] - 1
    begin, end, groups = class_range(bounds_ref, first, last)
    if which:
        total[0:nrow] = prior_ref[...]
    else:
        total[0:nrow] = jnp.zeros((nrow, TILE, TILE), jnp.float32)
    for index, size in enumerate(sizes):
        start = sum(sizes[:index])

        @pl.loop(0, size, unroll=4)
        def _(j):
            high, low = split_high_low(buffers[index][j])
            pairs[start + j, :, :TILE] = high
            pairs[start + j, :, TILE:] = low

    @pl.loop(0, groups)
    def _(group):
        for j in range(GROUP):
            spot = group * GROUP + j
            place = jnp.minimum(begin + spot, SLOTS - 1)
            live = begin + spot < end
            row = jnp.where(live, rows_ref[place], nrow)
            slot = jnp.where(live, slots_ref[place] - base, 0)
            right = pairs[slot]
            product = jnp.dot(
                tiles_ref[order_ref[place]],
                jnp.concatenate([right, right], axis=0),
                preferred_element_type=jnp.float32,
            )
            total[row] += product[:, :TILE] + product[:, TILE:]

    if which == len(FORWARD) - 1:
        core = bounds_ref[CORE]
        part = nrow // 4
        for index, out_ref in enumerate(rest[-6:-2]):
            side = core if index < 2 else 1 - core
            out_ref[...] = total[pl.ds((side * 2 + index % 2) * part, part)]
    else:
        rest[-3][...] = total[0:nrow]


def backward_kernel(which, bounds_ref, order_ref, rows_ref, slots_ref, tiles_ref, slope_ref, *rest):
    first, last, base, sizes, extra = BACKWARD[which]
    if which == 0:
        weight_term_ref, *rest = rest
    buffers = rest[: len(sizes)]
    total, out_sems, *rest = rest[len(sizes) :]
    if which == 0:
        (term_sems,) = rest
        term_copies = [
            pltpu.make_async_copy(weight_term_ref, buffer.at[PER], term_sems.at[index])
            for index, buffer in enumerate(buffers)
        ]
        for copy in term_copies:
            copy.start()
    begin, end, groups = class_range(bounds_ref, first, last)
    @pl.loop(0, sum(sizes), unroll=4)
    def _(slot):
        total[slot] = jnp.zeros((TILE, TILE), jnp.float32)

    @pl.loop(0, groups)
    def _(group):
        for j in range(GROUP):
            spot = group * GROUP + j
            place = jnp.minimum(begin + spot, SLOTS - 1)
            live = begin + spot < end
            slot = jnp.where(live, slots_ref[place] - base, sum(sizes))
            right = tiles_ref[order_ref[place]]
            product = jnp.dot(
                slope_ref[rows_ref[place]],
                jnp.concatenate([right, right], axis=0),
                preferred_element_type=jnp.float32,
            )
            total[slot] += product[:, :TILE] + product[:, TILE:]

    copies = []
    for index, size in enumerate(sizes):
        copy = pltpu.make_async_copy(
            total.at[pl.ds(sum(sizes[:index]), size)],
            buffers[index].at[pl.ds(0, size)],
            out_sems.at[index],
        )
        copy.start()
        copies.append(copy)
    if which == 0:
        copies += term_copies
    for copy in copies:
        copy.wait()


def smem():
    return pl.BlockSpec(memory_space=pltpu.SMEM)


def vmem():
    return pl.BlockSpec(memory_space=pltpu.VMEM)


def anywhere():
    return pl.BlockSpec(memory_space=pl.ANY)


def cost(microseconds):
    return pl.CostEstimate(
        flops=int(microseconds * 1.1e9), bytes_accessed=1 << 20, transcendentals=0
    )


def forward_part(which, plan, tiles, buffers, prior, nrow):
    extra = [prior] if which else []
    sizes = FORWARD[which][-1]
    out_shape = [jax.ShapeDtypeStruct((nrow, TILE, TILE), jnp.float32)]
    if which == len(FORWARD) - 1:
        out_shape = [jax.ShapeDtypeStruct((nrow // 4, TILE, TILE), jnp.float32)] * 4
    return pl.pallas_call(
        functools.partial(forward_kernel, which),
        name="forward_tiles_%d" % which,
        out_shape=out_shape,
        in_specs=[smem()] * 4 + [vmem()] * (1 + len(sizes) + len(extra)),
        out_specs=[vmem()] * len(out_shape),
        scratch_shapes=[
            pltpu.VMEM((sum(sizes), TILE, 2 * TILE), jnp.bfloat16),
            pltpu.VMEM((nrow + 1, TILE, TILE), jnp.float32),
        ],
        cost_estimate=cost((6, 5, 2)[which]),
        compiler_params=pltpu.CompilerParams(vmem_limit_bytes=VMEM_BYTES),
    )(*plan, tiles, *buffers, *extra)


def backward_part(which, plan, tiles, slope, weight_term=()):
    sizes, extra = BACKWARD[which][-2:]
    return pl.pallas_call(
        functools.partial(backward_kernel, which),
        name="backward_tiles_%d" % which,
        out_shape=[
            jax.ShapeDtypeStruct((size + more, TILE, TILE), jnp.float32)
            for size, more in zip(sizes, extra)
        ],
        in_specs=[smem()] * 4 + [vmem()] * (2 + len(weight_term)),
        out_specs=[anywhere()] * len(sizes),
        scratch_shapes=[
            pltpu.VMEM((sum(sizes) + 1, TILE, TILE), jnp.float32),
            pltpu.SemaphoreType.DMA((len(sizes),)),
        ]
        + [pltpu.SemaphoreType.DMA((2,))] * len(weight_term),
        cost_estimate=cost((3, 8)[which]),
        compiler_params=pltpu.CompilerParams(vmem_limit_bytes=VMEM_BYTES),
    )(*plan, tiles, slope, *weight_term)


def triple_left(value):
    high, low = split_high_low(value)
    return jnp.concatenate([high, low, high], axis=1)


def triple_right(value, axis):
    high, low = split_high_low(value)
    return jnp.concatenate([high, high, low], axis=axis)


def middle_kernel(which, bounds_ref, across_ref, weight_ref, cotangent_ref, *rest):
    kept_ref, other_ref = rest[0:2]
    core = bounds_ref[CORE]
    part = kept_ref.shape[0]
    across = triple_left(across_ref[...])
    weight = triple_left(weight_ref[...])
    if which == 0:
        activated_ref, spread_ref, weight_term_ref = rest[-3:]
        weight_term = jnp.zeros((TILE, TILE), jnp.float32)
    else:
        early_activated_ref, early_spread_ref, early_term_ref = rest[3:6]
        activated_ref, spread_ref, weight_term_ref = rest[-3:]
        weight_term = early_term_ref[...]
    for index, source in enumerate((kept_ref, other_ref)):
        side = core if index == 0 else 1 - core
        row = (side * 2 + which) * part
        columns = pl.ds(pl.multiple_of(row * TILE, part * TILE), part * TILE)
        block = source[...].reshape(part * TILE, TILE)
        value = lax.dot_general(
            across,
            triple_right(block, 1),
            (((1,), (1,)), ((), ())),
            preferred_element_type=jnp.float32,
        )
        square = value * value
        bend = jnp.tanh(GELU_SCALE * (value + GELU_CUBE * (square * value)))
        activated = 0.5 * value * (1.0 + bend)
        rate = 0.5 * (1.0 + bend) + 0.5 * value * (1.0 - bend * bend) * (
            GELU_SCALE * (1.0 + 3.0 * GELU_CUBE * square)
        )
        slope = cotangent_ref[:, columns] * rate
        weight_term += jnp.dot(
            triple_left(slope), triple_right(block, 0), preferred_element_type=jnp.float32
        )
        spread = jnp.dot(weight, triple_right(slope, 0), preferred_element_type=jnp.float32)
        high, low = split_high_low(spread)
        place = index * part if which == 0 else row
        for j in range(part):
            spread_ref[place + j, :, :TILE] = high[:, j * TILE : (j + 1) * TILE]
            spread_ref[place + j, :, TILE:] = low[:, j * TILE : (j + 1) * TILE]
        if which == 0:
            activated_ref[index] = activated
        else:
            activated_ref[:, columns] = activated
            early = side * 2 * part
            early_columns = pl.ds(pl.multiple_of(early * TILE, part * TILE), part * TILE)
            activated_ref[:, early_columns] = early_activated_ref[index]
            spread_ref[pl.ds(early, part)] = early_spread_ref[index * part : (index + 1) * part]
    weight_term_ref[...] = jnp.transpose(weight_term) if which else weight_term


def middle_part(which, bounds, across, weight, cotangent, kept, other, pairs, early=()):
    part = kept.shape[0]
    rows = 4 * part if which else 2 * part
    activated = cotangent.shape if which else (2, TILE, part * TILE)
    return pl.pallas_call(
        functools.partial(middle_kernel, which),
        name="middle_%d" % which,
        out_shape=[
            jax.ShapeDtypeStruct(activated, jnp.float32),
            jax.ShapeDtypeStruct((rows, TILE, 2 * TILE), jnp.bfloat16),
            jax.ShapeDtypeStruct(weight.shape, jnp.float32),
        ],
        in_specs=[smem()] + [vmem()] * (6 + len(early)),
        out_specs=[vmem()] * 3,
        cost_estimate=cost(2),
        compiler_params=pltpu.CompilerParams(vmem_limit_bytes=VMEM_BYTES),
    )(bounds, across, weight, cotangent, kept, other, pairs, *early)


def ring_sum_kernel(which, bounds_ref, own_ref, one_ref, two_ref, three_ref, out_ref):
    refs = (own_ref, one_ref, two_ref, three_ref)
    for place in range(SIDE):

        @pl.when(bounds_ref[FIRST + which] == place)
        def _():
            parts = [refs[(index - place) % SIDE] for index in range(SIDE)]
            out_ref[...] = (parts[0][...] + parts[1][...]) + (parts[2][...] + parts[3][...])


def ring_sum(which, bounds, parts):
    return pl.pallas_call(
        functools.partial(ring_sum_kernel, which),
        name="ring_sum_%d" % which,
        out_shape=jax.ShapeDtypeStruct((TILE, TILE), jnp.float32),
        in_specs=[smem()] + [vmem()] * SIDE,
        out_specs=vmem(),
        compiler_params=pltpu.CompilerParams(vmem_limit_bytes=VMEM_BYTES),
    )(bounds, *parts)


def assemble_kernel(
    bounds_ref, own_ref, own_other_ref, across_ref, across_other_ref, term_ref, out_ref, sum_ref
):
    core, low = bounds_ref[CORE], bounds_ref[LOW]
    for source, chip, side in (
        (own_ref, low, core),
        (own_other_ref, low, 1 - core),
        (across_ref, 1 - low, core),
        (across_other_ref, 1 - low, 1 - core),
    ):
        for j in range(4):
            place = (chip * 2 + side) * 4 + j
            out_ref[:, pl.ds(pl.multiple_of(place * TILE, TILE), TILE)] = source[j]

    @pl.when(core == 0)
    def _():
        sum_ref[...] = term_ref[...]

    @pl.when(core == 1)
    def _():
        sum_ref[...] = own_other_ref[4]


def assemble(bounds, parts):
    return pl.pallas_call(
        assemble_kernel,
        name="assemble",
        out_shape=[
            jax.ShapeDtypeStruct((TILE, 16 * TILE), jnp.float32),
            jax.ShapeDtypeStruct((TILE, TILE), jnp.float32),
        ],
        in_specs=[smem()] + [vmem()] * 5,
        out_specs=[vmem()] * 2,
        compiler_params=pltpu.CompilerParams(vmem_limit_bytes=VMEM_BYTES),
    )(bounds, *parts)


def make_plan(rows, cols, count, loop, wide):
    core = loop % 2
    node_block = cols // 4
    across = (node_block // 16) ^ (wide // 16)
    dx = (node_block // 4 - wide // 4) % 4
    dz = (node_block - wide) % 4
    du = jnp.where(core == 0, dx, dz)
    dv = jnp.where(core == 0, dz, dx)
    place = jnp.where(dv == 2, 3, jnp.where(dv == 3, 2, dv))
    start = jnp.where(
        place < 3, (1 - across) * 48 + place * PER, 96 + across * PER
    )
    slots = start + du * 4 + cols % 4
    spots = jnp.arange(SLOTS, dtype=jnp.int32)
    kind = jnp.where(place < 3, 1 - across, 2 + across)
    kind = jnp.where(spots < count[0], kind, 4)
    ahead = (kind[None, :] < kind[:, None]) | (
        (kind[None, :] == kind[:, None]) & (spots[None, :] < spots[:, None])
    )
    rank = jnp.sum(ahead.astype(jnp.int32), axis=1)
    here = rank[None, :] == spots[:, None]

    def sort(values):
        return jnp.sum(jnp.where(here, values[None, :], 0), axis=1)

    inner = du * 4 + cols % 4
    back_slots = jnp.where(
        place < 3, slots, 96 + (inner // HALF) * PER + across * HALF + inner % HALF
    )
    steps = jnp.arange(9, dtype=jnp.int32)
    bounds = jnp.sum((kind[None, :] < steps[:, None]).astype(jnp.int32), axis=1)
    bounds = jnp.where(steps == CORE, loop % 2, jnp.where(steps == LOW, loop // 2, bounds))
    ring = jnp.where(core == 0, wide // 4 % 4, wide % 4)
    other_ring = jnp.where(core == 0, wide % 4, wide // 4 % 4)
    bounds = jnp.where(steps == FIRST, ring, jnp.where(steps == FIRST + 1, other_ring, bounds))
    return bounds, sort(spots), sort(rows), sort(slots), sort(back_slots)


def quarter_tiles(features, index):
    feats = features.shape[0]
    split = features.reshape(feats, 4, 4, TILE)
    piece = lax.dynamic_index_in_dim(split, index, 1, keepdims=False)
    return jnp.transpose(piece, (1, 2, 0))


def gather_own(features, loop):
    own = quarter_tiles(features, loop)
    one, three, two = permute(own, u_down), permute(own, u_up), permute(own, u_far)
    partner = permute(quarter_tiles(features, loop ^ 2), y_partner)
    return own, one, two, three, partner


def with_tile(value, tile):
    return jnp.concatenate([value, tile[None]], axis=0)


def add_part(value, part, start):
    size = part.shape[0]
    return lax.dynamic_update_slice_in_dim(value, value[start : start + size] + part, start, 0)


def scatter_terms(plan, pairs, spread, weight_term):
    back_plan = plan[:3] + plan[4:]
    up, down, spread = tie(*backward_part(0, back_plan, pairs, spread, (weight_term,)), spread)
    up, down = permute(up, v_up), permute(down, v_down)
    zero, one, three, own, own_one, own_three = backward_part(1, back_plan, pairs, spread)
    one = lax.dynamic_update_slice_in_dim(add_part(one, up[HALF:PER], 0), up[PER:], PER, 0)
    three = add_part(three, down[HALF:PER], HALF)
    one, three = permute(one, v_up), permute(three, v_down)
    own_one = permute(add_part(own_one, up[:HALF], 0), v_up)
    own_three = permute(add_part(own_three, down[:HALF], HALF), v_down)
    weight_term = ring_sum(1, plan[0], (weight_term, down[PER], one[PER], up[PER]))
    apart = zero + one[:PER] + three
    apart_one = permute(with_tile(apart[4:8], weight_term), u_up)
    apart_two = permute(with_tile(apart[8:12], weight_term), u_far)
    apart_three = permute(with_tile(apart[12:16], weight_term), u_down)
    weight_term = ring_sum(0, plan[0], (weight_term, apart_three[4], apart_two[4], apart_one[4]))
    last = apart[:4] + apart_one[:4] + apart_two[:4] + apart_three[:4]
    last = permute(with_tile(last, weight_term), y_far)
    total = own + own_one + own_three
    one = permute(total[4:8], u_up)
    two = permute(total[8:12], u_far)
    three = permute(total[12:16], u_down)
    return total[:4] + last[:4] + one + two + three, weight_term + last[4]


def per_device(features, weight, cotangent, tiles, tile_rows, tile_cols, counts):
    nrow = features.shape[1] // TILE
    loop = lax.axis_index(LOOP)
    wide = lax.axis_index(WIDE)
    tile_collection = tiles.reshape(SLOTS, TILE, TILE)
    count = counts.reshape(1)
    plan = make_plan(tile_rows.reshape(SLOTS), tile_cols.reshape(SLOTS), count, loop, wide)
    across = weight.T

    own, one, two, three, partner = gather_own(features, loop)
    first = jnp.concatenate([own, one], axis=0)
    second = jnp.concatenate([two, three], axis=0)
    plan, across, first, second, partner = tie(plan, across, first, second, partner)
    one_first, three_second = permute(first, v_down), permute(second, v_up)
    second_far = permute(second, y_far)
    one_second, three_first = permute(second, v_down), permute(first, v_up)
    partner_one = permute(partner, u_down)
    count, one_first = tie(count, one_first)
    pairs = pair_tiles(count, tile_collection)
    near = [first, second, one_first, one_second, three_first, three_second]
    far = [permute(one_first, v_down), permute(three_second, v_up)]
    second_far, partner_one, *far = tie(second_far, partner_one, *far)
    first, second = jnp.concatenate([partner, partner_one], axis=0), second_far
    one_first, three_second = permute(first, v_down), permute(second, v_up)
    partial = forward_part(0, plan[:4], pairs, near + far, None, nrow)
    first, second, partial = tie(first, second, partial[0])
    one_second, three_first = permute(second, v_down), permute(first, v_up)
    apart = [first, second, one_first, one_second, three_first, three_second]
    far = [permute(one_first, v_down), permute(three_second, v_up)]
    partial = forward_part(1, plan[:4], pairs, apart, partial, nrow)
    *kept, given_first, given_second = forward_part(2, plan[:4], pairs, far, partial[0], nrow)

    bounds = plan[0]
    kept = [kept[0] + permute(given_first, core_swap), kept[1] + permute(given_second, core_swap)]
    received = [permute(value, y_pair) for value in kept]
    first = kept[0] + received[0]
    early = middle_part(
        0, bounds, across, weight, cotangent, first, permute(first, core_swap), pairs
    )
    received, *early = tie(received[1], *early)
    second = kept[1] + received
    activated, spread, weight_term = middle_part(
        1, bounds, across, weight, cotangent, second, permute(second, core_swap), pairs, early
    )
    total, weight_term = scatter_terms(plan, pairs, spread, weight_term)
    far_total = permute(total, y_pair)
    own_other = permute(with_tile(total, weight_term), core_swap)
    parts = [total, own_other, far_total, permute(far_total, core_swap), weight_term]
    return (activated, *assemble(bounds, parts))


def solution(mesh):
    split = jax.sharding.Mesh(mesh.devices.reshape(2, 2, 2, SIDE, SIDE), AXES)
    return jax.shard_map(
        per_device,
        mesh=split,
        in_specs=(
            P(None, WIDE),
            P(),
            P(None, WIDE),
            P(LOOP, WIDE, None, None, None),
            P(LOOP, WIDE, None),
            P(LOOP, WIDE, None),
            P(LOOP, WIDE),
        ),
        out_specs=(P(None, WIDE), P(None, WIDE), P()),
        check_vma=False,
    )
```

```python
import functools

import jax
import jax.numpy as jnp
from jax import lax
from jax.experimental import pallas as pl
from jax.experimental.pallas import tpu as pltpu
from jax.sharding import PartitionSpec as P

HI = lax.Precision.HIGHEST
GELU_SCALE = 0.7978845608028654
GELU_CUBE = 0.044715
AXES = ("y_lo", "core", "y_hi", "x", "z")
LOOP = ("y_lo", "core")
WIDE = ("y_hi", "x", "z")
SIDE = 4
TILE = 128
SLOTS = 256
GROUP = 16
CHUNK = 32
STAGES = 4
PAIR_BYTES = 30 * 1024 * 1024
PER = 16
HALF = 8
FORWARD = (
    (1, 3, 48, (HALF,) * 8),
    (0, 1, 0, (HALF,) * 6),
    (3, 4, 112, (HALF,) * 2),
)
BACKWARD = (
    (2, 4, 96, (PER, PER), (1, 1)),
    (0, 2, 0, (PER,) * 6, (0, 1, 0, 0, 0, 0)),
)
CORE = 5
LOW = 6
FIRST = 7
VMEM_BYTES = 8 * 1024 * 1024


def device_index(y, core, x, z):
    y, x, z = y % SIDE, x % SIDE, z % SIDE
    return (((y & 1) * 2 + core) * 2 + (y >> 1)) * 16 + x * SIDE + z


def permute(value, move):
    pairs = []
    for y in range(SIDE):
        for core in range(2):
            for x in range(SIDE):
                for z in range(SIDE):
                    pairs.append((device_index(y, core, x, z), device_index(*move(y, core, x, z))))
    return lax.ppermute(value, AXES, pairs)


def along(first, step):
    def move(y, core, x, z):
        if (core == 0) == first:
            return (y, core, x + step, z)
        return (y, core, x, z + step)

    return move


u_up, u_down, u_far = along(True, 1), along(True, -1), along(True, 2)
v_up, v_down = along(False, 1), along(False, -1)


def y_partner(y, core, x, z):
    return (3 - y, core, x, z)


def y_pair(y, core, x, z):
    return (y ^ 1, core, x, z)


def y_far(y, core, x, z):
    return (y + 2, core, x, z)


def core_swap(y, core, x, z):
    return (y, 1 - core, x, z)


def tie(*values):
    return lax.optimization_barrier(values)


def split_high_low(value):
    high = value.astype(jnp.bfloat16)
    low = (value - high.astype(jnp.float32)).astype(jnp.bfloat16)
    return high, low


def pair_kernel(count_ref, tiles_ref, out_ref, held, sems):
    count = count_ref[0]

    def copy(chunk):
        source = tiles_ref.at[pl.ds(chunk * CHUNK, CHUNK)]
        return pltpu.make_async_copy(source, held.at[chunk % STAGES], sems.at[chunk % STAGES])

    def when_live(chunk):
        return pl.when(chunk * CHUNK < count)

    for chunk in range(STAGES):
        when_live(chunk)(copy(chunk).start)
    for chunk in range(SLOTS // CHUNK):

        @when_live(chunk)
        def _():
            copy(chunk).wait()

            @pl.loop(0, CHUNK, unroll=8)
            def _(j):
                high, low = split_high_low(held[chunk % STAGES, j])
                out_ref[chunk * CHUNK + j, :, :TILE] = high
                out_ref[chunk * CHUNK + j, :, TILE:] = low

            if chunk + STAGES < SLOTS // CHUNK:
                when_live(chunk + STAGES)(copy(chunk + STAGES).start)


def pair_tiles(count, tiles):
    return pl.pallas_call(
        pair_kernel,
        name="pair_tiles",
        out_shape=pltpu.VMEM((SLOTS, TILE, 2 * TILE), jnp.bfloat16),
        in_specs=[smem(), anywhere()],
        out_specs=vmem(),
        scratch_shapes=[
            pltpu.VMEM((STAGES, CHUNK, TILE, TILE), jnp.float32),
            pltpu.SemaphoreType.DMA((STAGES,)),
        ],
        cost_estimate=cost(8),
        compiler_params=pltpu.CompilerParams(vmem_limit_bytes=PAIR_BYTES),
    )(count, tiles)


def class_range(bounds_ref, first, last):
    begin, end = bounds_ref[first], bounds_ref[last]
    return begin, end, (end - begin + GROUP - 1) // GROUP


def forward_kernel(which, bounds_ref, order_ref, rows_ref, slots_ref, tiles_ref, *rest):
    first, last, base, sizes = FORWARD[which]
    buffers = rest[: len(sizes)]
    rest = rest[len(sizes) :]
    prior_ref = rest[0] if which else None
    pairs, total = rest[-2:]
    nrow = total.shape[0] - 1
    begin, end, groups = class_range(bounds_ref, first, last)
    if which:
        total[0:nrow] = prior_ref[...]
    else:
        total[0:nrow] = jnp.zeros((nrow, TILE, TILE), jnp.float32)
    for index, size in enumerate(sizes):
        start = sum(sizes[:index])

        @pl.loop(0, size, unroll=4)
        def _(j):
            high, low = split_high_low(buffers[index][j])
            pairs[start + j, :, :TILE] = high
            pairs[start + j, :, TILE:] = low

    @pl.loop(0, groups)
    def _(group):
        for j in range(GROUP):
            spot = group * GROUP + j
            place = jnp.minimum(begin + spot, SLOTS - 1)
            live = begin + spot < end
            row = jnp.where(live, rows_ref[place], nrow)
            slot = jnp.where(live, slots_ref[place] - base, 0)
            right = pairs[slot]
            product = jnp.dot(
                tiles_ref[order_ref[place]],
                jnp.concatenate([right, right], axis=0),
                preferred_element_type=jnp.float32,
            )
            total[row] += product[:, :TILE] + product[:, TILE:]

    if which == len(FORWARD) - 1:
        core = bounds_ref[CORE]
        part = nrow // 4
        for index, out_ref in enumerate(rest[-6:-2]):
            side = core if index < 2 else 1 - core
            out_ref[...] = total[pl.ds((side * 2 + index % 2) * part, part)]
    else:
        rest[-3][...] = total[0:nrow]


def backward_kernel(which, bounds_ref, order_ref, rows_ref, slots_ref, tiles_ref, slope_ref, *rest):
    first, last, base, sizes, extra = BACKWARD[which]
    if which == 0:
        weight_term_ref, *rest = rest
    buffers = rest[: len(sizes)]
    total, out_sems, *rest = rest[len(sizes) :]
    if which == 0:
        (term_sems,) = rest
        term_copies = [
            pltpu.make_async_copy(weight_term_ref, buffer.at[PER], term_sems.at[index])
            for index, buffer in enumerate(buffers)
        ]
        for copy in term_copies:
            copy.start()
    begin, end, groups = class_range(bounds_ref, first, last)
    @pl.loop(0, sum(sizes), unroll=4)
    def _(slot):
        total[slot] = jnp.zeros((TILE, TILE), jnp.float32)

    @pl.loop(0, groups)
    def _(group):
        for j in range(GROUP):
            spot = group * GROUP + j
            place = jnp.minimum(begin + spot, SLOTS - 1)
            live = begin + spot < end
            slot = jnp.where(live, slots_ref[place] - base, sum(sizes))
            right = tiles_ref[order_ref[place]]
            product = jnp.dot(
                slope_ref[rows_ref[place]],
                jnp.concatenate([right, right], axis=0),
                preferred_element_type=jnp.float32,
            )
            total[slot] += product[:, :TILE] + product[:, TILE:]

    copies = []
    for index, size in enumerate(sizes):
        copy = pltpu.make_async_copy(
            total.at[pl.ds(sum(sizes[:index]), size)],
            buffers[index].at[pl.ds(0, size)],
            out_sems.at[index],
        )
        copy.start()
        copies.append(copy)
    if which == 0:
        copies += term_copies
    for copy in copies:
        copy.wait()


def smem():
    return pl.BlockSpec(memory_space=pltpu.SMEM)


def vmem():
    return pl.BlockSpec(memory_space=pltpu.VMEM)


def anywhere():
    return pl.BlockSpec(memory_space=pl.ANY)


def cost(microseconds):
    return pl.CostEstimate(
        flops=int(microseconds * 1.1e9), bytes_accessed=1 << 20, transcendentals=0
    )


def forward_part(which, plan, tiles, buffers, prior, nrow):
    extra = [prior] if which else []
    sizes = FORWARD[which][-1]
    out_shape = [jax.ShapeDtypeStruct((nrow, TILE, TILE), jnp.float32)]
    if which == len(FORWARD) - 1:
        out_shape = [jax.ShapeDtypeStruct((nrow // 4, TILE, TILE), jnp.float32)] * 4
    return pl.pallas_call(
        functools.partial(forward_kernel, which),
        name="forward_tiles_%d" % which,
        out_shape=out_shape,
        in_specs=[smem()] * 4 + [vmem()] * (1 + len(sizes) + len(extra)),
        out_specs=[vmem()] * len(out_shape),
        scratch_shapes=[
            pltpu.VMEM((sum(sizes), TILE, 2 * TILE), jnp.bfloat16),
            pltpu.VMEM((nrow + 1, TILE, TILE), jnp.float32),
        ],
        cost_estimate=cost((6, 5, 2)[which]),
        compiler_params=pltpu.CompilerParams(vmem_limit_bytes=VMEM_BYTES),
    )(*plan, tiles, *buffers, *extra)


def backward_part(which, plan, tiles, slope, weight_term=()):
    sizes, extra = BACKWARD[which][-2:]
    return pl.pallas_call(
        functools.partial(backward_kernel, which),
        name="backward_tiles_%d" % which,
        out_shape=[
            jax.ShapeDtypeStruct((size + more, TILE, TILE), jnp.float32)
            for size, more in zip(sizes, extra)
        ],
        in_specs=[smem()] * 4 + [vmem()] * (2 + len(weight_term)),
        out_specs=[anywhere()] * len(sizes),
        scratch_shapes=[
            pltpu.VMEM((sum(sizes) + 1, TILE, TILE), jnp.float32),
            pltpu.SemaphoreType.DMA((len(sizes),)),
        ]
        + [pltpu.SemaphoreType.DMA((2,))] * len(weight_term),
        cost_estimate=cost((3, 8)[which]),
        compiler_params=pltpu.CompilerParams(vmem_limit_bytes=VMEM_BYTES),
    )(*plan, tiles, slope, *weight_term)


def triple_left(value):
    high, low = split_high_low(value)
    return jnp.concatenate([high, low, high], axis=1)


def triple_right(value, axis):
    high, low = split_high_low(value)
    return jnp.concatenate([high, high, low], axis=axis)


def middle_kernel(which, bounds_ref, across_ref, weight_ref, cotangent_ref, *rest):
    kept_ref, other_ref = rest[0:2]
    core = bounds_ref[CORE]
    part = kept_ref.shape[0]
    across = triple_left(across_ref[...])
    weight = triple_left(weight_ref[...])
    if which == 0:
        activated_ref, spread_ref, weight_term_ref = rest[-3:]
        weight_term = jnp.zeros((TILE, TILE), jnp.float32)
    else:
        early_activated_ref, early_spread_ref, early_term_ref = rest[3:6]
        activated_ref, spread_ref, weight_term_ref = rest[-3:]
        weight_term = early_term_ref[...]
    for index, source in enumerate((kept_ref, other_ref)):
        side = core if index == 0 else 1 - core
        row = (side * 2 + which) * part
        columns = pl.ds(pl.multiple_of(row * TILE, part * TILE), part * TILE)
        block = source[...].reshape(part * TILE, TILE)
        value = lax.dot_general(
            across,
            triple_right(block, 1),
            (((1,), (1,)), ((), ())),
            preferred_element_type=jnp.float32,
        )
        square = value * value
        bend = jnp.tanh(GELU_SCALE * (value + GELU_CUBE * (square * value)))
        activated = 0.5 * value * (1.0 + bend)
        rate = 0.5 * (1.0 + bend) + 0.5 * value * (1.0 - bend * bend) * (
            GELU_SCALE * (1.0 + 3.0 * GELU_CUBE * square)
        )
        slope = cotangent_ref[:, columns] * rate
        weight_term += jnp.dot(
            triple_left(slope), triple_right(block, 0), preferred_element_type=jnp.float32
        )
        spread = jnp.dot(weight, triple_right(slope, 0), preferred_element_type=jnp.float32)
        high, low = split_high_low(spread)
        place = index * part if which == 0 else row
        for j in range(part):
            spread_ref[place + j, :, :TILE] = high[:, j * TILE : (j + 1) * TILE]
            spread_ref[place + j, :, TILE:] = low[:, j * TILE : (j + 1) * TILE]
        if which == 0:
            activated_ref[index] = activated
        else:
            activated_ref[:, columns] = activated
            early = side * 2 * part
            early_columns = pl.ds(pl.multiple_of(early * TILE, part * TILE), part * TILE)
            activated_ref[:, early_columns] = early_activated_ref[index]
            spread_ref[pl.ds(early, part)] = early_spread_ref[index * part : (index + 1) * part]
    weight_term_ref[...] = jnp.transpose(weight_term) if which else weight_term


def middle_part(which, bounds, across, weight, cotangent, kept, other, pairs, early=()):
    part = kept.shape[0]
    rows = 4 * part if which else 2 * part
    activated = cotangent.shape if which else (2, TILE, part * TILE)
    return pl.pallas_call(
        functools.partial(middle_kernel, which),
        name="middle_%d" % which,
        out_shape=[
            jax.ShapeDtypeStruct(activated, jnp.float32),
            jax.ShapeDtypeStruct((rows, TILE, 2 * TILE), jnp.bfloat16),
            jax.ShapeDtypeStruct(weight.shape, jnp.float32),
        ],
        in_specs=[smem()] + [vmem()] * (6 + len(early)),
        out_specs=[vmem()] * 3,
        cost_estimate=cost(2),
        compiler_params=pltpu.CompilerParams(vmem_limit_bytes=VMEM_BYTES),
    )(bounds, across, weight, cotangent, kept, other, pairs, *early)


def ring_sum_kernel(which, bounds_ref, own_ref, one_ref, two_ref, three_ref, out_ref):
    refs = (own_ref, one_ref, two_ref, three_ref)
    for place in range(SIDE):

        @pl.when(bounds_ref[FIRST + which] == place)
        def _():
            parts = [refs[(index - place) % SIDE] for index in range(SIDE)]
            out_ref[...] = (parts[0][...] + parts[1][...]) + (parts[2][...] + parts[3][...])


def ring_sum(which, bounds, parts):
    return pl.pallas_call(
        functools.partial(ring_sum_kernel, which),
        name="ring_sum_%d" % which,
        out_shape=jax.ShapeDtypeStruct((TILE, TILE), jnp.float32),
        in_specs=[smem()] + [vmem()] * SIDE,
        out_specs=vmem(),
        compiler_params=pltpu.CompilerParams(vmem_limit_bytes=VMEM_BYTES),
    )(bounds, *parts)


def assemble_kernel(
    bounds_ref, own_ref, own_other_ref, across_ref, across_other_ref, term_ref, out_ref, sum_ref
):
    core, low = bounds_ref[CORE], bounds_ref[LOW]
    for source, chip, side in (
        (own_ref, low, core),
        (own_other_ref, low, 1 - core),
        (across_ref, 1 - low, core),
        (across_other_ref, 1 - low, 1 - core),
    ):
        for j in range(4):
            place = (chip * 2 + side) * 4 + j
            out_ref[:, pl.ds(pl.multiple_of(place * TILE, TILE), TILE)] = source[j]

    @pl.when(core == 0)
    def _():
        sum_ref[...] = term_ref[...]

    @pl.when(core == 1)
    def _():
        sum_ref[...] = own_other_ref[4]


def assemble(bounds, parts):
    return pl.pallas_call(
        assemble_kernel,
        name="assemble",
        out_shape=[
            jax.ShapeDtypeStruct((TILE, 16 * TILE), jnp.float32),
            jax.ShapeDtypeStruct((TILE, TILE), jnp.float32),
        ],
        in_specs=[smem()] + [vmem()] * 5,
        out_specs=[vmem()] * 2,
        compiler_params=pltpu.CompilerParams(vmem_limit_bytes=VMEM_BYTES),
    )(bounds, *parts)


def make_plan(rows, cols, count, loop, wide):
    core = loop % 2
    node_block = cols // 4
    across = (node_block // 16) ^ (wide // 16)
    dx = (node_block // 4 - wide // 4) % 4
    dz = (node_block - wide) % 4
    du = jnp.where(core == 0, dx, dz)
    dv = jnp.where(core == 0, dz, dx)
    place = jnp.where(dv == 2, 3, jnp.where(dv == 3, 2, dv))
    start = jnp.where(
        place < 3, (1 - across) * 48 + place * PER, 96 + across * PER
    )
    slots = start + du * 4 + cols % 4
    spots = jnp.arange(SLOTS, dtype=jnp.int32)
    kind = jnp.where(place < 3, 1 - across, 2 + across)
    kind = jnp.where(spots < count[0], kind, 4)
    ahead = (kind[None, :] < kind[:, None]) | (
        (kind[None, :] == kind[:, None]) & (spots[None, :] < spots[:, None])
    )
    rank = jnp.sum(ahead.astype(jnp.int32), axis=1)
    here = rank[None, :] == spots[:, None]

    def sort(values):
        return jnp.sum(jnp.where(here, values[None, :], 0), axis=1)

    inner = du * 4 + cols % 4
    back_slots = jnp.where(
        place < 3, slots, 96 + (inner // HALF) * PER + across * HALF + inner % HALF
    )
    steps = jnp.arange(9, dtype=jnp.int32)
    bounds = jnp.sum((kind[None, :] < steps[:, None]).astype(jnp.int32), axis=1)
    bounds = jnp.where(steps == CORE, loop % 2, jnp.where(steps == LOW, loop // 2, bounds))
    ring = jnp.where(core == 0, wide // 4 % 4, wide % 4)
    other_ring = jnp.where(core == 0, wide % 4, wide // 4 % 4)
    bounds = jnp.where(steps == FIRST, ring, jnp.where(steps == FIRST + 1, other_ring, bounds))
    return bounds, sort(spots), sort(rows), sort(slots), sort(back_slots)


def quarter_tiles(features, index):
    feats = features.shape[0]
    split = features.reshape(feats, 4, 4, TILE)
    piece = lax.dynamic_index_in_dim(split, index, 1, keepdims=False)
    return jnp.transpose(piece, (1, 2, 0))


def gather_own(features, loop):
    own = quarter_tiles(features, loop)
    one, three, two = permute(own, u_down), permute(own, u_up), permute(own, u_far)
    partner = permute(quarter_tiles(features, loop ^ 2), y_partner)
    return own, one, two, three, partner


def with_tile(value, tile):
    return jnp.concatenate([value, tile[None]], axis=0)


def add_part(value, part, start):
    size = part.shape[0]
    return lax.dynamic_update_slice_in_dim(value, value[start : start + size] + part, start, 0)


def scatter_terms(plan, pairs, spread, weight_term):
    back_plan = plan[:3] + plan[4:]
    up, down, spread = tie(*backward_part(0, back_plan, pairs, spread, (weight_term,)), spread)
    up, down = permute(up, v_up), permute(down, v_down)
    zero, one, three, own, own_one, own_three = backward_part(1, back_plan, pairs, spread)
    one = lax.dynamic_update_slice_in_dim(add_part(one, up[HALF:PER], 0), up[PER:], PER, 0)
    three = add_part(three, down[HALF:PER], HALF)
    one, three = permute(one, v_up), permute(three, v_down)
    own_one = permute(add_part(own_one, up[:HALF], 0), v_up)
    own_three = permute(add_part(own_three, down[:HALF], HALF), v_down)
    weight_term = ring_sum(1, plan[0], (weight_term, down[PER], one[PER], up[PER]))
    apart = zero + one[:PER] + three
    apart_two = permute(apart[8:12], u_far)
    apart_far = permute(
        jnp.concatenate([apart[4:8], apart[12:16], weight_term[None]], axis=0), y_far
    )
    last, apart_far = tie(apart[:4] + apart_two, apart_far)
    last = permute(last, y_far)
    weight_term = weight_term + apart_far[8]
    total = own + own_one + own_three
    two = permute(with_tile(total[8:12], weight_term), u_far)
    one = permute(with_tile(total[4:8] + apart_far[:4], weight_term), u_up)
    three = permute(with_tile(total[12:16] + apart_far[4:8], weight_term), u_down)
    weight_term = ring_sum(0, plan[0], (weight_term, three[4], two[4], one[4]))
    return total[:4] + last + one[:4] + two[:4] + three[:4], weight_term


def per_device(features, weight, cotangent, tiles, tile_rows, tile_cols, counts):
    nrow = features.shape[1] // TILE
    loop = lax.axis_index(LOOP)
    wide = lax.axis_index(WIDE)
    tile_collection = tiles.reshape(SLOTS, TILE, TILE)
    count = counts.reshape(1)
    plan = make_plan(tile_rows.reshape(SLOTS), tile_cols.reshape(SLOTS), count, loop, wide)
    across = weight.T

    own, one, two, three, partner = gather_own(features, loop)
    first = jnp.concatenate([own, one], axis=0)
    second = jnp.concatenate([two, three], axis=0)
    plan, across, first, second, partner = tie(plan, across, first, second, partner)
    one_first, three_second = permute(first, v_down), permute(second, v_up)
    second_far = permute(second, y_far)
    one_second, three_first = permute(second, v_down), permute(first, v_up)
    count, one_first, partner = tie(count, one_first, partner)
    partner_one = permute(partner, u_down)
    pairs = pair_tiles(count, tile_collection)
    near = [first, second, one_first, one_second, three_first, three_second]
    far = [permute(one_first, v_down), permute(three_second, v_up)]
    first, second = jnp.concatenate([partner, partner_one], axis=0), second_far
    one_first, three_second = permute(first, v_down), permute(second, v_up)
    first, second, *far = tie(first, second, *far)
    one_second, three_first = permute(second, v_down), permute(first, v_up)
    partial = forward_part(0, plan[:4], pairs, near + far, None, nrow)
    one_first, three_second, partial = tie(one_first, three_second, partial[0])
    apart = [first, second, one_first, one_second, three_first, three_second]
    far = [permute(one_first, v_down), permute(three_second, v_up)]
    partial = forward_part(1, plan[:4], pairs, apart, partial, nrow)
    *kept, given_first, given_second = forward_part(2, plan[:4], pairs, far, partial[0], nrow)

    bounds = plan[0]
    kept = [kept[0] + permute(given_first, core_swap), kept[1] + permute(given_second, core_swap)]
    kept = [value + permute(value, y_pair) for value in kept]
    early = middle_part(
        0, bounds, across, weight, cotangent, kept[0], permute(kept[0], core_swap), pairs
    )
    activated, spread, weight_term = middle_part(
        1, bounds, across, weight, cotangent, kept[1], permute(kept[1], core_swap), pairs, early
    )
    total, weight_term = scatter_terms(plan, pairs, spread, weight_term)
    far_total = permute(total, y_pair)
    own_other = permute(with_tile(total, weight_term), core_swap)
    parts = [total, own_other, far_total, permute(far_total, core_swap), weight_term]
    return (activated, *assemble(bounds, parts))


def solution(mesh):
    split = jax.sharding.Mesh(mesh.devices.reshape(2, 2, 2, SIDE, SIDE), AXES)
    return jax.shard_map(
        per_device,
        mesh=split,
        in_specs=(
            P(None, WIDE),
            P(),
            P(None, WIDE),
            P(LOOP, WIDE, None, None, None),
            P(LOOP, WIDE, None),
            P(LOOP, WIDE, None),
            P(LOOP, WIDE),
        ),
        out_specs=(P(None, WIDE), P(None, WIDE), P()),
        check_vma=False,
    )
```

```python
import functools

import jax
import jax.numpy as jnp
from jax import lax
from jax.experimental import pallas as pl
from jax.experimental.pallas import tpu as pltpu
from jax.sharding import PartitionSpec as P

HI = lax.Precision.HIGHEST
GELU_SCALE = 0.7978845608028654
GELU_CUBE = 0.044715
AXES = ("y_lo", "core", "y_hi", "x", "z")
LOOP = ("y_lo", "core")
WIDE = ("y_hi", "x", "z")
SIDE = 4
TILE = 128
SLOTS = 256
GROUP = 16
CHUNK = 32
STAGES = 4
PAIR_BYTES = 30 * 1024 * 1024
PER = 16
HALF = 8
FORWARD = (
    (1, 3, 48, (HALF,) * 8),
    (0, 1, 0, (HALF,) * 6),
    (3, 4, 112, (HALF,) * 2),
)
BACKWARD = (
    (2, 4, 96, (PER, PER), (1, 1)),
    (0, 2, 0, (PER,) * 6, (0, 1, 0, 0, 0, 0)),
)
CORE = 5
LOW = 6
FIRST = 7
VMEM_BYTES = 8 * 1024 * 1024


def device_index(y, core, x, z):
    y, x, z = y % SIDE, x % SIDE, z % SIDE
    return (((y & 1) * 2 + core) * 2 + (y >> 1)) * 16 + x * SIDE + z


def permute(value, move):
    pairs = []
    for y in range(SIDE):
        for core in range(2):
            for x in range(SIDE):
                for z in range(SIDE):
                    pairs.append((device_index(y, core, x, z), device_index(*move(y, core, x, z))))
    return lax.ppermute(value, AXES, pairs)


def along(first, step):
    def move(y, core, x, z):
        if (core == 0) == first:
            return (y, core, x + step, z)
        return (y, core, x, z + step)

    return move


u_up, u_down, u_far = along(True, 1), along(True, -1), along(True, 2)
v_up, v_down = along(False, 1), along(False, -1)


def y_partner(y, core, x, z):
    return (3 - y, core, x, z)


def y_pair(y, core, x, z):
    return (y ^ 1, core, x, z)


def y_far(y, core, x, z):
    return (y + 2, core, x, z)


def core_swap(y, core, x, z):
    return (y, 1 - core, x, z)


def tie(*values):
    return lax.optimization_barrier(values)


def split_high_low(value):
    high = value.astype(jnp.bfloat16)
    low = (value - high.astype(jnp.float32)).astype(jnp.bfloat16)
    return high, low


def pair_kernel(count_ref, tiles_ref, out_ref, held, sems):
    count = count_ref[0]

    def copy(chunk):
        source = tiles_ref.at[pl.ds(chunk * CHUNK, CHUNK)]
        return pltpu.make_async_copy(source, held.at[chunk % STAGES], sems.at[chunk % STAGES])

    def when_live(chunk):
        return pl.when(chunk * CHUNK < count)

    for chunk in range(STAGES):
        when_live(chunk)(copy(chunk).start)
    for chunk in range(SLOTS // CHUNK):

        @when_live(chunk)
        def _():
            copy(chunk).wait()

            @pl.loop(0, CHUNK, unroll=8)
            def _(j):
                high, low = split_high_low(held[chunk % STAGES, j])
                out_ref[chunk * CHUNK + j, :, :TILE] = high
                out_ref[chunk * CHUNK + j, :, TILE:] = low

            if chunk + STAGES < SLOTS // CHUNK:
                when_live(chunk + STAGES)(copy(chunk + STAGES).start)


def pair_tiles(count, tiles):
    return pl.pallas_call(
        pair_kernel,
        name="pair_tiles",
        out_shape=pltpu.VMEM((SLOTS, TILE, 2 * TILE), jnp.bfloat16),
        in_specs=[smem(), anywhere()],
        out_specs=vmem(),
        scratch_shapes=[
            pltpu.VMEM((STAGES, CHUNK, TILE, TILE), jnp.float32),
            pltpu.SemaphoreType.DMA((STAGES,)),
        ],
        cost_estimate=cost(8),
        compiler_params=pltpu.CompilerParams(vmem_limit_bytes=PAIR_BYTES),
    )(count, tiles)


def class_range(bounds_ref, first, last):
    begin, end = bounds_ref[first], bounds_ref[last]
    return begin, end, (end - begin + GROUP - 1) // GROUP


def forward_kernel(which, bounds_ref, order_ref, rows_ref, slots_ref, tiles_ref, *rest):
    first, last, base, sizes = FORWARD[which]
    buffers = rest[: len(sizes)]
    rest = rest[len(sizes) :]
    prior_ref = rest[0] if which else None
    pairs, total = rest[-2:]
    nrow = total.shape[0] - 1
    begin, end, groups = class_range(bounds_ref, first, last)
    if which:
        total[0:nrow] = prior_ref[...]
    else:
        total[0:nrow] = jnp.zeros((nrow, TILE, TILE), jnp.float32)
    for index, size in enumerate(sizes):
        start = sum(sizes[:index])

        @pl.loop(0, size, unroll=4)
        def _(j):
            high, low = split_high_low(buffers[index][j])
            pairs[start + j, :, :TILE] = high
            pairs[start + j, :, TILE:] = low

    @pl.loop(0, groups)
    def _(group):
        for j in range(GROUP):
            spot = group * GROUP + j
            place = jnp.minimum(begin + spot, SLOTS - 1)
            live = begin + spot < end
            row = jnp.where(live, rows_ref[place], nrow)
            slot = jnp.where(live, slots_ref[place] - base, 0)
            right = pairs[slot]
            product = jnp.dot(
                tiles_ref[order_ref[place]],
                jnp.concatenate([right, right], axis=0),
                preferred_element_type=jnp.float32,
            )
            total[row] += product[:, :TILE] + product[:, TILE:]

    if which == len(FORWARD) - 1:
        core = bounds_ref[CORE]
        part = nrow // 4
        for index, out_ref in enumerate(rest[-6:-2]):
            side = core if index < 2 else 1 - core
            out_ref[...] = total[pl.ds((side * 2 + index % 2) * part, part)]
    else:
        rest[-3][...] = total[0:nrow]


def backward_kernel(which, bounds_ref, order_ref, rows_ref, slots_ref, tiles_ref, slope_ref, *rest):
    first, last, base, sizes, extra = BACKWARD[which]
    if which == 0:
        weight_term_ref, *rest = rest
    buffers = rest[: len(sizes)]
    total, out_sems, *rest = rest[len(sizes) :]
    if which == 0:
        (term_sems,) = rest
        term_copies = [
            pltpu.make_async_copy(weight_term_ref, buffer.at[PER], term_sems.at[index])
            for index, buffer in enumerate(buffers)
        ]
        for copy in term_copies:
            copy.start()
    begin, end, groups = class_range(bounds_ref, first, last)
    @pl.loop(0, sum(sizes), unroll=4)
    def _(slot):
        total[slot] = jnp.zeros((TILE, TILE), jnp.float32)

    @pl.loop(0, groups)
    def _(group):
        for j in range(GROUP):
            spot = group * GROUP + j
            place = jnp.minimum(begin + spot, SLOTS - 1)
            live = begin + spot < end
            slot = jnp.where(live, slots_ref[place] - base, sum(sizes))
            right = tiles_ref[order_ref[place]]
            product = jnp.dot(
                slope_ref[rows_ref[place]],
                jnp.concatenate([right, right], axis=0),
                preferred_element_type=jnp.float32,
            )
            total[slot] += product[:, :TILE] + product[:, TILE:]

    copies = []
    for index, size in enumerate(sizes):
        copy = pltpu.make_async_copy(
            total.at[pl.ds(sum(sizes[:index]), size)],
            buffers[index].at[pl.ds(0, size)],
            out_sems.at[index],
        )
        copy.start()
        copies.append(copy)
    if which == 0:
        copies += term_copies
    for copy in copies:
        copy.wait()


def smem():
    return pl.BlockSpec(memory_space=pltpu.SMEM)


def vmem():
    return pl.BlockSpec(memory_space=pltpu.VMEM)


def anywhere():
    return pl.BlockSpec(memory_space=pl.ANY)


def cost(microseconds):
    return pl.CostEstimate(
        flops=int(microseconds * 1.1e9), bytes_accessed=1 << 20, transcendentals=0
    )


def forward_part(which, plan, tiles, buffers, prior, nrow):
    extra = [prior] if which else []
    sizes = FORWARD[which][-1]
    out_shape = [jax.ShapeDtypeStruct((nrow, TILE, TILE), jnp.float32)]
    if which == len(FORWARD) - 1:
        out_shape = [jax.ShapeDtypeStruct((nrow // 4, TILE, TILE), jnp.float32)] * 4
    return pl.pallas_call(
        functools.partial(forward_kernel, which),
        name="forward_tiles_%d" % which,
        out_shape=out_shape,
        in_specs=[smem()] * 4 + [vmem()] * (1 + len(sizes) + len(extra)),
        out_specs=[vmem()] * len(out_shape),
        scratch_shapes=[
            pltpu.VMEM((sum(sizes), TILE, 2 * TILE), jnp.bfloat16),
            pltpu.VMEM((nrow + 1, TILE, TILE), jnp.float32),
        ],
        cost_estimate=cost((6, 5, 2)[which]),
        compiler_params=pltpu.CompilerParams(vmem_limit_bytes=VMEM_BYTES),
    )(*plan, tiles, *buffers, *extra)


def backward_part(which, plan, tiles, slope, weight_term=()):
    sizes, extra = BACKWARD[which][-2:]
    return pl.pallas_call(
        functools.partial(backward_kernel, which),
        name="backward_tiles_%d" % which,
        out_shape=[
            jax.ShapeDtypeStruct((size + more, TILE, TILE), jnp.float32)
            for size, more in zip(sizes, extra)
        ],
        in_specs=[smem()] * 4 + [vmem()] * (2 + len(weight_term)),
        out_specs=[anywhere()] * len(sizes),
        scratch_shapes=[
            pltpu.VMEM((sum(sizes) + 1, TILE, TILE), jnp.float32),
            pltpu.SemaphoreType.DMA((len(sizes),)),
        ]
        + [pltpu.SemaphoreType.DMA((2,))] * len(weight_term),
        cost_estimate=cost((3, 8)[which]),
        compiler_params=pltpu.CompilerParams(vmem_limit_bytes=VMEM_BYTES),
    )(*plan, tiles, slope, *weight_term)


def triple_left(value):
    high, low = split_high_low(value)
    return jnp.concatenate([high, low, high], axis=1)


def triple_right(value, axis):
    high, low = split_high_low(value)
    return jnp.concatenate([high, high, low], axis=axis)


def middle_kernel(which, bounds_ref, across_ref, weight_ref, cotangent_ref, *rest):
    kept_ref, other_ref = rest[0:2]
    core = bounds_ref[CORE]
    part = kept_ref.shape[0]
    across = triple_left(across_ref[...])
    weight = triple_left(weight_ref[...])
    if which == 0:
        activated_ref, spread_ref, weight_term_ref = rest[-3:]
        weight_term = jnp.zeros((TILE, TILE), jnp.float32)
    else:
        early_activated_ref, early_spread_ref, early_term_ref = rest[3:6]
        activated_ref, spread_ref, weight_term_ref = rest[-3:]
        weight_term = early_term_ref[...]
    for index, source in enumerate((kept_ref, other_ref)):
        side = core if index == 0 else 1 - core
        row = (side * 2 + which) * part
        columns = pl.ds(pl.multiple_of(row * TILE, part * TILE), part * TILE)
        block = source[...].reshape(part * TILE, TILE)
        value = lax.dot_general(
            across,
            triple_right(block, 1),
            (((1,), (1,)), ((), ())),
            preferred_element_type=jnp.float32,
        )
        square = value * value
        bend = jnp.tanh(GELU_SCALE * (value + GELU_CUBE * (square * value)))
        activated = 0.5 * value * (1.0 + bend)
        rate = 0.5 * (1.0 + bend) + 0.5 * value * (1.0 - bend * bend) * (
            GELU_SCALE * (1.0 + 3.0 * GELU_CUBE * square)
        )
        slope = cotangent_ref[:, columns] * rate
        weight_term += jnp.dot(
            triple_left(slope), triple_right(block, 0), preferred_element_type=jnp.float32
        )
        spread = jnp.dot(weight, triple_right(slope, 0), preferred_element_type=jnp.float32)
        high, low = split_high_low(spread)
        place = index * part if which == 0 else row
        for j in range(part):
            spread_ref[place + j, :, :TILE] = high[:, j * TILE : (j + 1) * TILE]
            spread_ref[place + j, :, TILE:] = low[:, j * TILE : (j + 1) * TILE]
        if which == 0:
            activated_ref[index] = activated
        else:
            activated_ref[:, columns] = activated
            early = side * 2 * part
            early_columns = pl.ds(pl.multiple_of(early * TILE, part * TILE), part * TILE)
            activated_ref[:, early_columns] = early_activated_ref[index]
            spread_ref[pl.ds(early, part)] = early_spread_ref[index * part : (index + 1) * part]
    weight_term_ref[...] = jnp.transpose(weight_term) if which else weight_term


def middle_part(which, bounds, across, weight, cotangent, kept, other, pairs, early=()):
    part = kept.shape[0]
    rows = 4 * part if which else 2 * part
    activated = cotangent.shape if which else (2, TILE, part * TILE)
    return pl.pallas_call(
        functools.partial(middle_kernel, which),
        name="middle_%d" % which,
        out_shape=[
            jax.ShapeDtypeStruct(activated, jnp.float32),
            jax.ShapeDtypeStruct((rows, TILE, 2 * TILE), jnp.bfloat16),
            jax.ShapeDtypeStruct(weight.shape, jnp.float32),
        ],
        in_specs=[smem()] + [vmem()] * (6 + len(early)),
        out_specs=[vmem()] * 3,
        cost_estimate=cost(2),
        compiler_params=pltpu.CompilerParams(vmem_limit_bytes=VMEM_BYTES),
    )(bounds, across, weight, cotangent, kept, other, pairs, *early)


def ring_sum_kernel(which, bounds_ref, own_ref, one_ref, two_ref, three_ref, out_ref):
    refs = (own_ref, one_ref, two_ref, three_ref)
    for place in range(SIDE):

        @pl.when(bounds_ref[FIRST + which] == place)
        def _():
            parts = [refs[(index - place) % SIDE] for index in range(SIDE)]
            out_ref[...] = (parts[0][...] + parts[1][...]) + (parts[2][...] + parts[3][...])


def ring_sum(which, bounds, parts):
    return pl.pallas_call(
        functools.partial(ring_sum_kernel, which),
        name="ring_sum_%d" % which,
        out_shape=jax.ShapeDtypeStruct((TILE, TILE), jnp.float32),
        in_specs=[smem()] + [vmem()] * SIDE,
        out_specs=vmem(),
        compiler_params=pltpu.CompilerParams(vmem_limit_bytes=VMEM_BYTES),
    )(bounds, *parts)


def assemble_kernel(
    bounds_ref, own_ref, own_other_ref, across_ref, across_other_ref, term_ref, out_ref, sum_ref
):
    core, low = bounds_ref[CORE], bounds_ref[LOW]
    for source, chip, side in (
        (own_ref, low, core),
        (own_other_ref, low, 1 - core),
        (across_ref, 1 - low, core),
        (across_other_ref, 1 - low, 1 - core),
    ):
        for j in range(4):
            place = (chip * 2 + side) * 4 + j
            out_ref[:, pl.ds(pl.multiple_of(place * TILE, TILE), TILE)] = source[j]

    @pl.when(core == 0)
    def _():
        sum_ref[...] = term_ref[...]

    @pl.when(core == 1)
    def _():
        sum_ref[...] = own_other_ref[4]


def assemble(bounds, parts):
    return pl.pallas_call(
        assemble_kernel,
        name="assemble",
        out_shape=[
            jax.ShapeDtypeStruct((TILE, 16 * TILE), jnp.float32),
            jax.ShapeDtypeStruct((TILE, TILE), jnp.float32),
        ],
        in_specs=[smem()] + [vmem()] * 5,
        out_specs=[vmem()] * 2,
        compiler_params=pltpu.CompilerParams(vmem_limit_bytes=VMEM_BYTES),
    )(bounds, *parts)


def make_plan(rows, cols, count, loop, wide):
    core = loop % 2
    node_block = cols // 4
    across = (node_block // 16) ^ (wide // 16)
    dx = (node_block // 4 - wide // 4) % 4
    dz = (node_block - wide) % 4
    du = jnp.where(core == 0, dx, dz)
    dv = jnp.where(core == 0, dz, dx)
    place = jnp.where(dv == 2, 3, jnp.where(dv == 3, 2, dv))
    start = jnp.where(
        place < 3, (1 - across) * 48 + place * PER, 96 + across * PER
    )
    slots = start + du * 4 + cols % 4
    spots = jnp.arange(SLOTS, dtype=jnp.int32)
    kind = jnp.where(place < 3, 1 - across, 2 + across)
    kind = jnp.where(spots < count[0], kind, 4)
    ahead = (kind[None, :] < kind[:, None]) | (
        (kind[None, :] == kind[:, None]) & (spots[None, :] < spots[:, None])
    )
    rank = jnp.sum(ahead.astype(jnp.int32), axis=1)
    here = rank[None, :] == spots[:, None]

    def sort(values):
        return jnp.sum(jnp.where(here, values[None, :], 0), axis=1)

    inner = du * 4 + cols % 4
    back_slots = jnp.where(
        place < 3, slots, 96 + (inner // HALF) * PER + across * HALF + inner % HALF
    )
    steps = jnp.arange(9, dtype=jnp.int32)
    bounds = jnp.sum((kind[None, :] < steps[:, None]).astype(jnp.int32), axis=1)
    bounds = jnp.where(steps == CORE, loop % 2, jnp.where(steps == LOW, loop // 2, bounds))
    ring = jnp.where(core == 0, wide // 4 % 4, wide % 4)
    other_ring = jnp.where(core == 0, wide % 4, wide // 4 % 4)
    bounds = jnp.where(steps == FIRST, ring, jnp.where(steps == FIRST + 1, other_ring, bounds))
    return bounds, sort(spots), sort(rows), sort(slots), sort(back_slots)


def quarter_tiles(features, index):
    feats = features.shape[0]
    split = features.reshape(feats, 4, 4, TILE)
    piece = lax.dynamic_index_in_dim(split, index, 1, keepdims=False)
    return jnp.transpose(piece, (1, 2, 0))


def gather_own(features, loop):
    own = quarter_tiles(features, loop)
    one, three, two = permute(own, u_down), permute(own, u_up), permute(own, u_far)
    partner = permute(quarter_tiles(features, loop ^ 2), y_partner)
    return own, one, two, three, partner


def with_tile(value, tile):
    return jnp.concatenate([value, tile[None]], axis=0)


def add_part(value, part, start):
    size = part.shape[0]
    return lax.dynamic_update_slice_in_dim(value, value[start : start + size] + part, start, 0)


def scatter_terms(plan, pairs, spread, weight_term):
    back_plan = plan[:3] + plan[4:]
    up, down, spread = tie(*backward_part(0, back_plan, pairs, spread, (weight_term,)), spread)
    up, down = permute(up, v_up), permute(down, v_down)
    zero, one, three, own, own_one, own_three = backward_part(1, back_plan, pairs, spread)
    one = lax.dynamic_update_slice_in_dim(add_part(one, up[HALF:PER], 0), up[PER:], PER, 0)
    three = add_part(three, down[HALF:PER], HALF)
    one, three = permute(one, v_up), permute(three, v_down)
    own_one = permute(add_part(own_one, up[:HALF], 0), v_up)
    own_three = permute(add_part(own_three, down[:HALF], HALF), v_down)
    weight_term = ring_sum(1, plan[0], (weight_term, down[PER], one[PER], up[PER]))
    apart = zero + one[:PER] + three
    apart_two = permute(apart[8:12], u_far)
    far_one = permute(with_tile(apart[4:8], weight_term), y_far)
    far_three = permute(apart[12:16], y_far)
    last, far_three = tie(apart[:4] + apart_two, far_three)
    last = permute(last, y_far)
    weight_term = weight_term + far_one[4]
    total = own + own_one + own_three
    two = permute(with_tile(total[8:12], weight_term), u_far)
    one = permute(with_tile(total[4:8] + far_one[:4], weight_term), u_up)
    three = permute(with_tile(total[12:16] + far_three, weight_term), u_down)
    weight_term = ring_sum(0, plan[0], (weight_term, three[4], two[4], one[4]))
    return total[:4] + last + one[:4] + two[:4] + three[:4], weight_term


def per_device(features, weight, cotangent, tiles, tile_rows, tile_cols, counts):
    nrow = features.shape[1] // TILE
    loop = lax.axis_index(LOOP)
    wide = lax.axis_index(WIDE)
    tile_collection = tiles.reshape(SLOTS, TILE, TILE)
    count = counts.reshape(1)
    plan = make_plan(tile_rows.reshape(SLOTS), tile_cols.reshape(SLOTS), count, loop, wide)
    across = weight.T

    own, one, two, three, partner = gather_own(features, loop)
    first = jnp.concatenate([own, one], axis=0)
    second = jnp.concatenate([two, three], axis=0)
    plan, across, first, second, partner = tie(plan, across, first, second, partner)
    one_first, three_second = permute(first, v_down), permute(second, v_up)
    second_far = permute(second, y_far)
    one_second, three_first = permute(second, v_down), permute(first, v_up)
    count, one_first, partner = tie(count, one_first, partner)
    partner_one = permute(partner, u_down)
    pairs = pair_tiles(count, tile_collection)
    near = [first, second, one_first, one_second, three_first, three_second]
    far = [permute(one_first, v_down), permute(three_second, v_up)]
    first, second = jnp.concatenate([partner, partner_one], axis=0), second_far
    one_first, three_second = permute(first, v_down), permute(second, v_up)
    first, second, *far = tie(first, second, *far)
    one_second, three_first = permute(second, v_down), permute(first, v_up)
    partial = forward_part(0, plan[:4], pairs, near + far, None, nrow)
    one_first, three_second, partial = tie(one_first, three_second, partial[0])
    apart = [first, second, one_first, one_second, three_first, three_second]
    far = [permute(one_first, v_down), permute(three_second, v_up)]
    partial = forward_part(1, plan[:4], pairs, apart, partial, nrow)
    *kept, given_first, given_second = forward_part(2, plan[:4], pairs, far, partial[0], nrow)

    bounds = plan[0]
    kept = [kept[0] + permute(given_first, core_swap), kept[1] + permute(given_second, core_swap)]
    kept = [value + permute(value, y_pair) for value in kept]
    early = middle_part(
        0, bounds, across, weight, cotangent, kept[0], permute(kept[0], core_swap), pairs
    )
    activated, spread, weight_term = middle_part(
        1, bounds, across, weight, cotangent, kept[1], permute(kept[1], core_swap), pairs, early
    )
    total, weight_term = scatter_terms(plan, pairs, spread, weight_term)
    far_total = permute(total, y_pair)
    own_other = permute(with_tile(total, weight_term), core_swap)
    parts = [total, own_other, far_total, permute(far_total, core_swap), weight_term]
    return (activated, *assemble(bounds, parts))


def solution(mesh):
    split = jax.sharding.Mesh(mesh.devices.reshape(2, 2, 2, SIDE, SIDE), AXES)
    return jax.shard_map(
        per_device,
        mesh=split,
        in_specs=(
            P(None, WIDE),
            P(),
            P(None, WIDE),
            P(LOOP, WIDE, None, None, None),
            P(LOOP, WIDE, None),
            P(LOOP, WIDE, None),
            P(LOOP, WIDE),
        ),
        out_specs=(P(None, WIDE), P(None, WIDE), P()),
        check_vma=False,
    )
```

```python
import functools

import jax
import jax.numpy as jnp
from jax import lax
from jax.experimental import pallas as pl
from jax.experimental.pallas import tpu as pltpu
from jax.sharding import PartitionSpec as P

HI = lax.Precision.HIGHEST
GELU_SCALE = 0.7978845608028654
GELU_CUBE = 0.044715
AXES = ("y_lo", "core", "y_hi", "x", "z")
LOOP = ("y_lo", "core")
WIDE = ("y_hi", "x", "z")
SIDE = 4
TILE = 128
SLOTS = 256
GROUP = 16
CHUNK = 32
STAGES = 4
PAIR_BYTES = 30 * 1024 * 1024
PER = 16
HALF = 8
FORWARD = (
    (1, 3, 48, (HALF,) * 8),
    (0, 1, 0, (HALF,) * 6),
    (3, 4, 112, (HALF,) * 2),
)
BACKWARD = (
    (2, 4, 96, (PER, PER), (1, 1)),
    (0, 2, 0, (PER,) * 6, (0, 1, 0, 0, 0, 0)),
)
CORE = 5
LOW = 6
FIRST = 7
VMEM_BYTES = 8 * 1024 * 1024


def device_index(y, core, x, z):
    y, x, z = y % SIDE, x % SIDE, z % SIDE
    return (((y & 1) * 2 + core) * 2 + (y >> 1)) * 16 + x * SIDE + z


def permute(value, move):
    pairs = []
    for y in range(SIDE):
        for core in range(2):
            for x in range(SIDE):
                for z in range(SIDE):
                    pairs.append((device_index(y, core, x, z), device_index(*move(y, core, x, z))))
    return lax.ppermute(value, AXES, pairs)


def along(first, step):
    def move(y, core, x, z):
        if (core == 0) == first:
            return (y, core, x + step, z)
        return (y, core, x, z + step)

    return move


u_up, u_down, u_far = along(True, 1), along(True, -1), along(True, 2)
v_up, v_down = along(False, 1), along(False, -1)


def y_partner(y, core, x, z):
    return (3 - y, core, x, z)


def y_pair(y, core, x, z):
    return (y ^ 1, core, x, z)


def y_far(y, core, x, z):
    return (y + 2, core, x, z)


def core_swap(y, core, x, z):
    return (y, 1 - core, x, z)


def tie(*values):
    return lax.optimization_barrier(values)


def split_high_low(value):
    high = value.astype(jnp.bfloat16)
    low = (value - high.astype(jnp.float32)).astype(jnp.bfloat16)
    return high, low


def pair_kernel(count_ref, tiles_ref, out_ref, held, sems):
    count = count_ref[0]

    def copy(chunk):
        source = tiles_ref.at[pl.ds(chunk * CHUNK, CHUNK)]
        return pltpu.make_async_copy(source, held.at[chunk % STAGES], sems.at[chunk % STAGES])

    def when_live(chunk):
        return pl.when(chunk * CHUNK < count)

    for chunk in range(STAGES):
        when_live(chunk)(copy(chunk).start)
    for chunk in range(SLOTS // CHUNK):

        @when_live(chunk)
        def _():
            copy(chunk).wait()

            @pl.loop(0, CHUNK, unroll=8)
            def _(j):
                high, low = split_high_low(held[chunk % STAGES, j])
                out_ref[chunk * CHUNK + j, :, :TILE] = high
                out_ref[chunk * CHUNK + j, :, TILE:] = low

            if chunk + STAGES < SLOTS // CHUNK:
                when_live(chunk + STAGES)(copy(chunk + STAGES).start)


def pair_tiles(count, tiles):
    return pl.pallas_call(
        pair_kernel,
        name="pair_tiles",
        out_shape=pltpu.VMEM((SLOTS, TILE, 2 * TILE), jnp.bfloat16),
        in_specs=[smem(), anywhere()],
        out_specs=vmem(),
        scratch_shapes=[
            pltpu.VMEM((STAGES, CHUNK, TILE, TILE), jnp.float32),
            pltpu.SemaphoreType.DMA((STAGES,)),
        ],
        cost_estimate=cost(8),
        compiler_params=pltpu.CompilerParams(vmem_limit_bytes=PAIR_BYTES),
    )(count, tiles)


def class_range(bounds_ref, first, last):
    begin, end = bounds_ref[first], bounds_ref[last]
    return begin, end, (end - begin + GROUP - 1) // GROUP


def forward_kernel(which, bounds_ref, order_ref, rows_ref, slots_ref, tiles_ref, *rest):
    first, last, base, sizes = FORWARD[which]
    buffers = rest[: len(sizes)]
    rest = rest[len(sizes) :]
    prior_ref = rest[0] if which else None
    pairs, total = rest[-2:]
    nrow = total.shape[0] - 1
    begin, end, groups = class_range(bounds_ref, first, last)
    if which:
        total[0:nrow] = prior_ref[...]
    else:
        total[0:nrow] = jnp.zeros((nrow, TILE, TILE), jnp.float32)
    for index, size in enumerate(sizes):
        start = sum(sizes[:index])

        @pl.loop(0, size, unroll=4)
        def _(j):
            high, low = split_high_low(buffers[index][j])
            pairs[start + j, :, :TILE] = high
            pairs[start + j, :, TILE:] = low

    @pl.loop(0, groups)
    def _(group):
        for j in range(GROUP):
            spot = group * GROUP + j
            place = jnp.minimum(begin + spot, SLOTS - 1)
            live = begin + spot < end
            row = jnp.where(live, rows_ref[place], nrow)
            slot = jnp.where(live, slots_ref[place] - base, 0)
            right = pairs[slot]
            product = jnp.dot(
                tiles_ref[order_ref[place]],
                jnp.concatenate([right, right], axis=0),
                preferred_element_type=jnp.float32,
            )
            total[row] += product[:, :TILE] + product[:, TILE:]

    if which == len(FORWARD) - 1:
        core = bounds_ref[CORE]
        part = nrow // 4
        for index, out_ref in enumerate(rest[-6:-2]):
            side = core if index < 2 else 1 - core
            out_ref[...] = total[pl.ds((side * 2 + index % 2) * part, part)]
    else:
        rest[-3][...] = total[0:nrow]


def backward_kernel(which, bounds_ref, order_ref, rows_ref, slots_ref, tiles_ref, slope_ref, *rest):
    first, last, base, sizes, extra = BACKWARD[which]
    if which == 0:
        weight_term_ref, *rest = rest
    buffers = rest[: len(sizes)]
    total, out_sems, *rest = rest[len(sizes) :]
    if which == 0:
        (term_sems,) = rest
        term_copies = [
            pltpu.make_async_copy(weight_term_ref, buffer.at[PER], term_sems.at[index])
            for index, buffer in enumerate(buffers)
        ]
        for copy in term_copies:
            copy.start()
    begin, end, groups = class_range(bounds_ref, first, last)
    @pl.loop(0, sum(sizes), unroll=4)
    def _(slot):
        total[slot] = jnp.zeros((TILE, TILE), jnp.float32)

    @pl.loop(0, groups)
    def _(group):
        for j in range(GROUP):
            spot = group * GROUP + j
            place = jnp.minimum(begin + spot, SLOTS - 1)
            live = begin + spot < end
            slot = jnp.where(live, slots_ref[place] - base, sum(sizes))
            right = tiles_ref[order_ref[place]]
            product = jnp.dot(
                slope_ref[rows_ref[place]],
                jnp.concatenate([right, right], axis=0),
                preferred_element_type=jnp.float32,
            )
            total[slot] += product[:, :TILE] + product[:, TILE:]

    copies = []
    for index, size in enumerate(sizes):
        copy = pltpu.make_async_copy(
            total.at[pl.ds(sum(sizes[:index]), size)],
            buffers[index].at[pl.ds(0, size)],
            out_sems.at[index],
        )
        copy.start()
        copies.append(copy)
    if which == 0:
        copies += term_copies
    for copy in copies:
        copy.wait()


def smem():
    return pl.BlockSpec(memory_space=pltpu.SMEM)


def vmem():
    return pl.BlockSpec(memory_space=pltpu.VMEM)


def anywhere():
    return pl.BlockSpec(memory_space=pl.ANY)


def cost(microseconds):
    return pl.CostEstimate(
        flops=int(microseconds * 1.1e9), bytes_accessed=1 << 20, transcendentals=0
    )


def forward_part(which, plan, tiles, buffers, prior, nrow):
    extra = [prior] if which else []
    sizes = FORWARD[which][-1]
    out_shape = [jax.ShapeDtypeStruct((nrow, TILE, TILE), jnp.float32)]
    if which == len(FORWARD) - 1:
        out_shape = [jax.ShapeDtypeStruct((nrow // 4, TILE, TILE), jnp.float32)] * 4
    return pl.pallas_call(
        functools.partial(forward_kernel, which),
        name="forward_tiles_%d" % which,
        out_shape=out_shape,
        in_specs=[smem()] * 4 + [vmem()] * (1 + len(sizes) + len(extra)),
        out_specs=[vmem()] * len(out_shape),
        scratch_shapes=[
            pltpu.VMEM((sum(sizes), TILE, 2 * TILE), jnp.bfloat16),
            pltpu.VMEM((nrow + 1, TILE, TILE), jnp.float32),
        ],
        cost_estimate=cost((6, 5, 2)[which]),
        compiler_params=pltpu.CompilerParams(vmem_limit_bytes=VMEM_BYTES),
    )(*plan, tiles, *buffers, *extra)


def backward_part(which, plan, tiles, slope, weight_term=()):
    sizes, extra = BACKWARD[which][-2:]
    return pl.pallas_call(
        functools.partial(backward_kernel, which),
        name="backward_tiles_%d" % which,
        out_shape=[
            jax.ShapeDtypeStruct((size + more, TILE, TILE), jnp.float32)
            for size, more in zip(sizes, extra)
        ],
        in_specs=[smem()] * 4 + [vmem()] * (2 + len(weight_term)),
        out_specs=[anywhere()] * len(sizes),
        scratch_shapes=[
            pltpu.VMEM((sum(sizes) + 1, TILE, TILE), jnp.float32),
            pltpu.SemaphoreType.DMA((len(sizes),)),
        ]
        + [pltpu.SemaphoreType.DMA((2,))] * len(weight_term),
        cost_estimate=cost((3, 8)[which]),
        compiler_params=pltpu.CompilerParams(vmem_limit_bytes=VMEM_BYTES),
    )(*plan, tiles, slope, *weight_term)


def triple_left(value):
    high, low = split_high_low(value)
    return jnp.concatenate([high, low, high], axis=1)


def triple_right(value, axis):
    high, low = split_high_low(value)
    return jnp.concatenate([high, high, low], axis=axis)


def middle_kernel(which, bounds_ref, across_ref, weight_ref, cotangent_ref, *rest):
    kept_ref, other_ref = rest[0:2]
    core = bounds_ref[CORE]
    part = kept_ref.shape[0]
    across = triple_left(across_ref[...])
    weight = triple_left(weight_ref[...])
    if which == 0:
        activated_ref, spread_ref, weight_term_ref = rest[-3:]
        weight_term = jnp.zeros((TILE, TILE), jnp.float32)
    else:
        early_activated_ref, early_spread_ref, early_term_ref = rest[3:6]
        activated_ref, spread_ref, weight_term_ref = rest[-3:]
        weight_term = early_term_ref[...]
    for index, source in enumerate((kept_ref, other_ref)):
        side = core if index == 0 else 1 - core
        row = (side * 2 + which) * part
        columns = pl.ds(pl.multiple_of(row * TILE, part * TILE), part * TILE)
        block = source[...].reshape(part * TILE, TILE)
        value = lax.dot_general(
            across,
            triple_right(block, 1),
            (((1,), (1,)), ((), ())),
            preferred_element_type=jnp.float32,
        )
        square = value * value
        bend = jnp.tanh(GELU_SCALE * (value + GELU_CUBE * (square * value)))
        activated = 0.5 * value * (1.0 + bend)
        rate = 0.5 * (1.0 + bend) + 0.5 * value * (1.0 - bend * bend) * (
            GELU_SCALE * (1.0 + 3.0 * GELU_CUBE * square)
        )
        slope = cotangent_ref[:, columns] * rate
        weight_term += jnp.dot(
            triple_left(slope), triple_right(block, 0), preferred_element_type=jnp.float32
        )
        spread = jnp.dot(weight, triple_right(slope, 0), preferred_element_type=jnp.float32)
        high, low = split_high_low(spread)
        place = index * part if which == 0 else row
        for j in range(part):
            spread_ref[place + j, :, :TILE] = high[:, j * TILE : (j + 1) * TILE]
            spread_ref[place + j, :, TILE:] = low[:, j * TILE : (j + 1) * TILE]
        if which == 0:
            activated_ref[index] = activated
        else:
            activated_ref[:, columns] = activated
            early = side * 2 * part
            early_columns = pl.ds(pl.multiple_of(early * TILE, part * TILE), part * TILE)
            activated_ref[:, early_columns] = early_activated_ref[index]
            spread_ref[pl.ds(early, part)] = early_spread_ref[index * part : (index + 1) * part]
    weight_term_ref[...] = jnp.transpose(weight_term) if which else weight_term


def middle_part(which, bounds, across, weight, cotangent, kept, other, pairs, early=()):
    part = kept.shape[0]
    rows = 4 * part if which else 2 * part
    activated = cotangent.shape if which else (2, TILE, part * TILE)
    return pl.pallas_call(
        functools.partial(middle_kernel, which),
        name="middle_%d" % which,
        out_shape=[
            jax.ShapeDtypeStruct(activated, jnp.float32),
            jax.ShapeDtypeStruct((rows, TILE, 2 * TILE), jnp.bfloat16),
            jax.ShapeDtypeStruct(weight.shape, jnp.float32),
        ],
        in_specs=[smem()] + [vmem()] * (6 + len(early)),
        out_specs=[vmem()] * 3,
        cost_estimate=cost(2),
        compiler_params=pltpu.CompilerParams(vmem_limit_bytes=VMEM_BYTES),
    )(bounds, across, weight, cotangent, kept, other, pairs, *early)


def ring_sum_kernel(which, bounds_ref, own_ref, one_ref, two_ref, three_ref, out_ref):
    refs = (own_ref, one_ref, two_ref, three_ref)
    for place in range(SIDE):

        @pl.when(bounds_ref[FIRST + which] == place)
        def _():
            parts = [refs[(index - place) % SIDE] for index in range(SIDE)]
            out_ref[...] = (parts[0][...] + parts[1][...]) + (parts[2][...] + parts[3][...])


def ring_sum(which, bounds, parts):
    return pl.pallas_call(
        functools.partial(ring_sum_kernel, which),
        name="ring_sum_%d" % which,
        out_shape=jax.ShapeDtypeStruct((TILE, TILE), jnp.float32),
        in_specs=[smem()] + [vmem()] * SIDE,
        out_specs=vmem(),
        compiler_params=pltpu.CompilerParams(vmem_limit_bytes=VMEM_BYTES),
    )(bounds, *parts)


def assemble_kernel(
    bounds_ref, own_ref, own_other_ref, across_ref, across_other_ref, term_ref, out_ref, sum_ref
):
    core, low = bounds_ref[CORE], bounds_ref[LOW]
    for source, chip, side in (
        (own_ref, low, core),
        (own_other_ref, low, 1 - core),
        (across_ref, 1 - low, core),
        (across_other_ref, 1 - low, 1 - core),
    ):
        for j in range(4):
            place = (chip * 2 + side) * 4 + j
            out_ref[:, pl.ds(pl.multiple_of(place * TILE, TILE), TILE)] = source[j]

    @pl.when(core == 0)
    def _():
        sum_ref[...] = term_ref[...]

    @pl.when(core == 1)
    def _():
        sum_ref[...] = own_other_ref[4]


def assemble(bounds, parts):
    return pl.pallas_call(
        assemble_kernel,
        name="assemble",
        out_shape=[
            jax.ShapeDtypeStruct((TILE, 16 * TILE), jnp.float32),
            jax.ShapeDtypeStruct((TILE, TILE), jnp.float32),
        ],
        in_specs=[smem()] + [vmem()] * 5,
        out_specs=[vmem()] * 2,
        compiler_params=pltpu.CompilerParams(vmem_limit_bytes=VMEM_BYTES),
    )(bounds, *parts)


def make_plan(rows, cols, count, loop, wide):
    core = loop % 2
    node_block = cols // 4
    across = (node_block // 16) ^ (wide // 16)
    dx = (node_block // 4 - wide // 4) % 4
    dz = (node_block - wide) % 4
    du = jnp.where(core == 0, dx, dz)
    dv = jnp.where(core == 0, dz, dx)
    place = jnp.where(dv == 2, 3, jnp.where(dv == 3, 2, dv))
    start = jnp.where(
        place < 3, (1 - across) * 48 + place * PER, 96 + across * PER
    )
    slots = start + du * 4 + cols % 4
    spots = jnp.arange(SLOTS, dtype=jnp.int32)
    kind = jnp.where(place < 3, 1 - across, 2 + across)
    kind = jnp.where(spots < count[0], kind, 4)
    ahead = (kind[None, :] < kind[:, None]) | (
        (kind[None, :] == kind[:, None]) & (spots[None, :] < spots[:, None])
    )
    rank = jnp.sum(ahead.astype(jnp.int32), axis=1)
    here = rank[None, :] == spots[:, None]

    def sort(values):
        return jnp.sum(jnp.where(here, values[None, :], 0), axis=1)

    inner = du * 4 + cols % 4
    back_slots = jnp.where(
        place < 3, slots, 96 + (inner // HALF) * PER + across * HALF + inner % HALF
    )
    steps = jnp.arange(9, dtype=jnp.int32)
    bounds = jnp.sum((kind[None, :] < steps[:, None]).astype(jnp.int32), axis=1)
    bounds = jnp.where(steps == CORE, loop % 2, jnp.where(steps == LOW, loop // 2, bounds))
    ring = jnp.where(core == 0, wide // 4 % 4, wide % 4)
    other_ring = jnp.where(core == 0, wide % 4, wide // 4 % 4)
    bounds = jnp.where(steps == FIRST, ring, jnp.where(steps == FIRST + 1, other_ring, bounds))
    return bounds, sort(spots), sort(rows), sort(slots), sort(back_slots)


def quarter_tiles(features, index):
    feats = features.shape[0]
    split = features.reshape(feats, 4, 4, TILE)
    piece = lax.dynamic_index_in_dim(split, index, 1, keepdims=False)
    return jnp.transpose(piece, (1, 2, 0))


def gather_own(features, loop):
    own = quarter_tiles(features, loop)
    one, three, two = permute(own, u_down), permute(own, u_up), permute(own, u_far)
    partner = permute(quarter_tiles(features, loop ^ 2), y_partner)
    return own, one, two, three, partner


def with_tile(value, tile):
    return jnp.concatenate([value, tile[None]], axis=0)


def add_part(value, part, start):
    size = part.shape[0]
    return lax.dynamic_update_slice_in_dim(value, value[start : start + size] + part, start, 0)


def scatter_terms(plan, pairs, spread, weight_term):
    back_plan = plan[:3] + plan[4:]
    up, down, spread = tie(*backward_part(0, back_plan, pairs, spread, (weight_term,)), spread)
    up, down = permute(up, v_up), permute(down, v_down)
    zero, one, three, own, own_one, own_three = backward_part(1, back_plan, pairs, spread)
    one = lax.dynamic_update_slice_in_dim(add_part(one, up[HALF:PER], 0), up[PER:], PER, 0)
    three = add_part(three, down[HALF:PER], HALF)
    one, three = permute(one, v_up), permute(three, v_down)
    own_one = permute(add_part(own_one, up[:HALF], 0), v_up)
    own_three = permute(add_part(own_three, down[:HALF], HALF), v_down)
    weight_term = ring_sum(1, plan[0], (weight_term, down[PER], one[PER], up[PER]))
    apart = zero + one[:PER] + three
    apart_two = permute(apart[8:12], u_far)
    far_one = permute(with_tile(apart[4:8], weight_term), y_far)
    far_three = permute(apart[12:16], y_far)
    last, far_three = tie(apart[:4] + apart_two, far_three)
    last = permute(last, y_far)
    weight_term = weight_term + far_one[4]
    total = own + own_one + own_three
    two = permute(with_tile(total[8:12], weight_term), u_far)
    one = permute(with_tile(total[4:8] + far_one[:4], weight_term), u_up)
    three = permute(with_tile(total[12:16] + far_three, weight_term), u_down)
    base, one = tie(total[:4] + last, one)
    weight_term = ring_sum(0, plan[0], (weight_term, three[4], two[4], one[4]))
    return base + one[:4] + two[:4] + three[:4], weight_term


def per_device(features, weight, cotangent, tiles, tile_rows, tile_cols, counts):
    nrow = features.shape[1] // TILE
    loop = lax.axis_index(LOOP)
    wide = lax.axis_index(WIDE)
    tile_collection = tiles.reshape(SLOTS, TILE, TILE)
    count = counts.reshape(1)
    plan = make_plan(tile_rows.reshape(SLOTS), tile_cols.reshape(SLOTS), count, loop, wide)
    across = weight.T

    own, one, two, three, partner = gather_own(features, loop)
    first = jnp.concatenate([own, one], axis=0)
    second = jnp.concatenate([two, three], axis=0)
    plan, across, first, second, partner = tie(plan, across, first, second, partner)
    one_first, three_second = permute(first, v_down), permute(second, v_up)
    second_far = permute(second, y_far)
    one_second, three_first = permute(second, v_down), permute(first, v_up)
    count, one_first, partner = tie(count, one_first, partner)
    partner_one = permute(partner, u_down)
    pairs = pair_tiles(count, tile_collection)
    near = [first, second, one_first, one_second, three_first, three_second]
    far = [permute(one_first, v_down), permute(three_second, v_up)]
    first, second = jnp.concatenate([partner, partner_one], axis=0), second_far
    one_first, three_second = permute(first, v_down), permute(second, v_up)
    first, second, *far = tie(first, second, *far)
    one_second, three_first = permute(second, v_down), permute(first, v_up)
    partial = forward_part(0, plan[:4], pairs, near + far, None, nrow)
    one_first, three_second, partial = tie(one_first, three_second, partial[0])
    apart = [first, second, one_first, one_second, three_first, three_second]
    far = [permute(one_first, v_down), permute(three_second, v_up)]
    partial = forward_part(1, plan[:4], pairs, apart, partial, nrow)
    *kept, given_first, given_second = forward_part(2, plan[:4], pairs, far, partial[0], nrow)

    bounds = plan[0]
    kept = [kept[0] + permute(given_first, core_swap), kept[1] + permute(given_second, core_swap)]
    kept = [value + permute(value, y_pair) for value in kept]
    early = middle_part(
        0, bounds, across, weight, cotangent, kept[0], permute(kept[0], core_swap), pairs
    )
    activated, spread, weight_term = middle_part(
        1, bounds, across, weight, cotangent, kept[1], permute(kept[1], core_swap), pairs, early
    )
    total, weight_term = scatter_terms(plan, pairs, spread, weight_term)
    far_total = permute(total, y_pair)
    own_other = permute(with_tile(total, weight_term), core_swap)
    parts = [total, own_other, far_total, permute(far_total, core_swap), weight_term]
    return (activated, *assemble(bounds, parts))


def solution(mesh):
    split = jax.sharding.Mesh(mesh.devices.reshape(2, 2, 2, SIDE, SIDE), AXES)
    return jax.shard_map(
        per_device,
        mesh=split,
        in_specs=(
            P(None, WIDE),
            P(),
            P(None, WIDE),
            P(LOOP, WIDE, None, None, None),
            P(LOOP, WIDE, None),
            P(LOOP, WIDE, None),
            P(LOOP, WIDE),
        ),
        out_specs=(P(None, WIDE), P(None, WIDE), P()),
        check_vma=False,
    )
```

```python
import functools

import jax
import jax.numpy as jnp
from jax import lax
from jax.experimental import pallas as pl
from jax.experimental.pallas import tpu as pltpu
from jax.sharding import PartitionSpec as P

HI = lax.Precision.HIGHEST
GELU_SCALE = 0.7978845608028654
GELU_CUBE = 0.044715
AXES = ("y_lo", "core", "y_hi", "x", "z")
LOOP = ("y_lo", "core")
WIDE = ("y_hi", "x", "z")
SIDE = 4
TILE = 128
SLOTS = 256
GROUP = 16
CHUNK = 32
STAGES = 4
PAIR_BYTES = 30 * 1024 * 1024
PER = 16
HALF = 8
FORWARD = (
    (1, 3, 48, (HALF,) * 8),
    (0, 1, 0, (HALF,) * 6),
    (3, 4, 112, (HALF,) * 2),
)
BACKWARD = (
    (2, 4, 96, (PER, PER), (1, 1)),
    (0, 2, 0, (PER,) * 6, (0, 1, 0, 0, 0, 0)),
)
CORE = 5
LOW = 6
FIRST = 7
VMEM_BYTES = 8 * 1024 * 1024


def device_index(y, core, x, z):
    y, x, z = y % SIDE, x % SIDE, z % SIDE
    return (((y & 1) * 2 + core) * 2 + (y >> 1)) * 16 + x * SIDE + z


def permute(value, move):
    pairs = []
    for y in range(SIDE):
        for core in range(2):
            for x in range(SIDE):
                for z in range(SIDE):
                    pairs.append((device_index(y, core, x, z), device_index(*move(y, core, x, z))))
    return lax.ppermute(value, AXES, pairs)


def along(first, step):
    def move(y, core, x, z):
        if (core == 0) == first:
            return (y, core, x + step, z)
        return (y, core, x, z + step)

    return move


u_up, u_down, u_far = along(True, 1), along(True, -1), along(True, 2)
v_up, v_down = along(False, 1), along(False, -1)


def y_partner(y, core, x, z):
    return (3 - y, core, x, z)


def y_pair(y, core, x, z):
    return (y ^ 1, core, x, z)


def y_far(y, core, x, z):
    return (y + 2, core, x, z)


def core_swap(y, core, x, z):
    return (y, 1 - core, x, z)


def tie(*values):
    return lax.optimization_barrier(values)


def split_high_low(value):
    high = value.astype(jnp.bfloat16)
    low = (value - high.astype(jnp.float32)).astype(jnp.bfloat16)
    return high, low


def pair_kernel(count_ref, tiles_ref, out_ref, held, sems):
    count = count_ref[0]

    def copy(chunk):
        source = tiles_ref.at[pl.ds(chunk * CHUNK, CHUNK)]
        return pltpu.make_async_copy(source, held.at[chunk % STAGES], sems.at[chunk % STAGES])

    def when_live(chunk):
        return pl.when(chunk * CHUNK < count)

    for chunk in range(STAGES):
        when_live(chunk)(copy(chunk).start)
    for chunk in range(SLOTS // CHUNK):

        @when_live(chunk)
        def _():
            copy(chunk).wait()

            @pl.loop(0, CHUNK, unroll=8)
            def _(j):
                high, low = split_high_low(held[chunk % STAGES, j])
                out_ref[chunk * CHUNK + j, :, :TILE] = high
                out_ref[chunk * CHUNK + j, :, TILE:] = low

            if chunk + STAGES < SLOTS // CHUNK:
                when_live(chunk + STAGES)(copy(chunk + STAGES).start)


def pair_tiles(count, tiles):
    return pl.pallas_call(
        pair_kernel,
        name="pair_tiles",
        out_shape=pltpu.VMEM((SLOTS, TILE, 2 * TILE), jnp.bfloat16),
        in_specs=[smem(), anywhere()],
        out_specs=vmem(),
        scratch_shapes=[
            pltpu.VMEM((STAGES, CHUNK, TILE, TILE), jnp.float32),
            pltpu.SemaphoreType.DMA((STAGES,)),
        ],
        cost_estimate=cost(8),
        compiler_params=pltpu.CompilerParams(vmem_limit_bytes=PAIR_BYTES),
    )(count, tiles)


def class_range(bounds_ref, first, last):
    begin, end = bounds_ref[first], bounds_ref[last]
    return begin, end, (end - begin + GROUP - 1) // GROUP


def forward_kernel(which, bounds_ref, order_ref, rows_ref, slots_ref, tiles_ref, *rest):
    first, last, base, sizes = FORWARD[which]
    buffers = rest[: len(sizes)]
    rest = rest[len(sizes) :]
    prior_ref = rest[0] if which else None
    pairs, total = rest[-2:]
    nrow = total.shape[0] - 1
    begin, end, groups = class_range(bounds_ref, first, last)
    if which:
        total[0:nrow] = prior_ref[...]
    else:
        total[0:nrow] = jnp.zeros((nrow, TILE, TILE), jnp.float32)
    for index, size in enumerate(sizes):
        start = sum(sizes[:index])

        @pl.loop(0, size, unroll=4)
        def _(j):
            high, low = split_high_low(buffers[index][j])
            pairs[start + j, :, :TILE] = high
            pairs[start + j, :, TILE:] = low

    @pl.loop(0, groups)
    def _(group):
        for j in range(GROUP):
            spot = group * GROUP + j
            place = jnp.minimum(begin + spot, SLOTS - 1)
            live = begin + spot < end
            row = jnp.where(live, rows_ref[place], nrow)
            slot = jnp.where(live, slots_ref[place] - base, 0)
            right = pairs[slot]
            product = jnp.dot(
                tiles_ref[order_ref[place]],
                jnp.concatenate([right, right], axis=0),
                preferred_element_type=jnp.float32,
            )
            total[row] += product[:, :TILE] + product[:, TILE:]

    if which == len(FORWARD) - 1:
        core = bounds_ref[CORE]
        part = nrow // 4
        for index, out_ref in enumerate(rest[-6:-2]):
            side = core if index < 2 else 1 - core
            out_ref[...] = total[pl.ds((side * 2 + index % 2) * part, part)]
    else:
        rest[-3][...] = total[0:nrow]


def backward_kernel(which, bounds_ref, order_ref, rows_ref, slots_ref, tiles_ref, slope_ref, *rest):
    first, last, base, sizes, extra = BACKWARD[which]
    if which == 0:
        weight_term_ref, *rest = rest
    buffers = rest[: len(sizes)]
    total, out_sems, *rest = rest[len(sizes) :]
    if which == 0:
        (term_sems,) = rest
        term_copies = [
            pltpu.make_async_copy(weight_term_ref, buffer.at[PER], term_sems.at[index])
            for index, buffer in enumerate(buffers)
        ]
        for copy in term_copies:
            copy.start()
    begin, end, groups = class_range(bounds_ref, first, last)
    @pl.loop(0, sum(sizes), unroll=4)
    def _(slot):
        total[slot] = jnp.zeros((TILE, TILE), jnp.float32)

    @pl.loop(0, groups)
    def _(group):
        for j in range(GROUP):
            spot = group * GROUP + j
            place = jnp.minimum(begin + spot, SLOTS - 1)
            live = begin + spot < end
            slot = jnp.where(live, slots_ref[place] - base, sum(sizes))
            right = tiles_ref[order_ref[place]]
            product = jnp.dot(
                slope_ref[rows_ref[place]],
                jnp.concatenate([right, right], axis=0),
                preferred_element_type=jnp.float32,
            )
            total[slot] += product[:, :TILE] + product[:, TILE:]

    copies = []
    for index, size in enumerate(sizes):
        copy = pltpu.make_async_copy(
            total.at[pl.ds(sum(sizes[:index]), size)],
            buffers[index].at[pl.ds(0, size)],
            out_sems.at[index],
        )
        copy.start()
        copies.append(copy)
    if which == 0:
        copies += term_copies
    for copy in copies:
        copy.wait()


def smem():
    return pl.BlockSpec(memory_space=pltpu.SMEM)


def vmem():
    return pl.BlockSpec(memory_space=pltpu.VMEM)


def anywhere():
    return pl.BlockSpec(memory_space=pl.ANY)


def cost(microseconds):
    return pl.CostEstimate(
        flops=int(microseconds * 1.1e9), bytes_accessed=1 << 20, transcendentals=0
    )


def forward_part(which, plan, tiles, buffers, prior, nrow):
    extra = [prior] if which else []
    sizes = FORWARD[which][-1]
    out_shape = [jax.ShapeDtypeStruct((nrow, TILE, TILE), jnp.float32)]
    if which == len(FORWARD) - 1:
        out_shape = [jax.ShapeDtypeStruct((nrow // 4, TILE, TILE), jnp.float32)] * 4
    return pl.pallas_call(
        functools.partial(forward_kernel, which),
        name="forward_tiles_%d" % which,
        out_shape=out_shape,
        in_specs=[smem()] * 4 + [vmem()] * (1 + len(sizes) + len(extra)),
        out_specs=[vmem()] * len(out_shape),
        scratch_shapes=[
            pltpu.VMEM((sum(sizes), TILE, 2 * TILE), jnp.bfloat16),
            pltpu.VMEM((nrow + 1, TILE, TILE), jnp.float32),
        ],
        cost_estimate=cost((6, 5, 2)[which]),
        compiler_params=pltpu.CompilerParams(vmem_limit_bytes=VMEM_BYTES),
    )(*plan, tiles, *buffers, *extra)


def backward_part(which, plan, tiles, slope, weight_term=()):
    sizes, extra = BACKWARD[which][-2:]
    return pl.pallas_call(
        functools.partial(backward_kernel, which),
        name="backward_tiles_%d" % which,
        out_shape=[
            jax.ShapeDtypeStruct((size + more, TILE, TILE), jnp.float32)
            for size, more in zip(sizes, extra)
        ],
        in_specs=[smem()] * 4 + [vmem()] * (2 + len(weight_term)),
        out_specs=[anywhere()] * len(sizes),
        scratch_shapes=[
            pltpu.VMEM((sum(sizes) + 1, TILE, TILE), jnp.float32),
            pltpu.SemaphoreType.DMA((len(sizes),)),
        ]
        + [pltpu.SemaphoreType.DMA((2,))] * len(weight_term),
        cost_estimate=cost((3, 8)[which]),
        compiler_params=pltpu.CompilerParams(vmem_limit_bytes=VMEM_BYTES),
    )(*plan, tiles, slope, *weight_term)


def triple_left(value):
    high, low = split_high_low(value)
    return jnp.concatenate([high, low, high], axis=1)


def triple_right(value, axis):
    high, low = split_high_low(value)
    return jnp.concatenate([high, high, low], axis=axis)


def middle_kernel(which, bounds_ref, across_ref, weight_ref, cotangent_ref, *rest):
    kept_ref, other_ref = rest[0:2]
    core = bounds_ref[CORE]
    part = kept_ref.shape[0]
    across = triple_left(across_ref[...])
    weight = triple_left(weight_ref[...])
    if which == 0:
        activated_ref, spread_ref, weight_term_ref = rest[-3:]
        weight_term = jnp.zeros((TILE, TILE), jnp.float32)
    else:
        early_activated_ref, early_spread_ref, early_term_ref = rest[3:6]
        activated_ref, spread_ref, weight_term_ref = rest[-3:]
        weight_term = early_term_ref[...]
    for index, source in enumerate((kept_ref, other_ref)):
        side = core if index == 0 else 1 - core
        row = (side * 2 + which) * part
        columns = pl.ds(pl.multiple_of(row * TILE, part * TILE), part * TILE)
        block = source[...].reshape(part * TILE, TILE)
        value = lax.dot_general(
            across,
            triple_right(block, 1),
            (((1,), (1,)), ((), ())),
            preferred_element_type=jnp.float32,
        )
        square = value * value
        bend = jnp.tanh(GELU_SCALE * (value + GELU_CUBE * (square * value)))
        activated = 0.5 * value * (1.0 + bend)
        rate = 0.5 * (1.0 + bend) + 0.5 * value * (1.0 - bend * bend) * (
            GELU_SCALE * (1.0 + 3.0 * GELU_CUBE * square)
        )
        slope = cotangent_ref[:, columns] * rate
        weight_term += jnp.dot(
            triple_left(slope), triple_right(block, 0), preferred_element_type=jnp.float32
        )
        spread = jnp.dot(weight, triple_right(slope, 0), preferred_element_type=jnp.float32)
        high, low = split_high_low(spread)
        place = index * part if which == 0 else row
        for j in range(part):
            spread_ref[place + j, :, :TILE] = high[:, j * TILE : (j + 1) * TILE]
            spread_ref[place + j, :, TILE:] = low[:, j * TILE : (j + 1) * TILE]
        if which == 0:
            activated_ref[index] = activated
        else:
            activated_ref[:, columns] = activated
            early = side * 2 * part
            early_columns = pl.ds(pl.multiple_of(early * TILE, part * TILE), part * TILE)
            activated_ref[:, early_columns] = early_activated_ref[index]
            spread_ref[pl.ds(early, part)] = early_spread_ref[index * part : (index + 1) * part]
    weight_term_ref[...] = jnp.transpose(weight_term) if which else weight_term


def middle_part(which, bounds, across, weight, cotangent, kept, other, pairs, early=()):
    part = kept.shape[0]
    rows = 4 * part if which else 2 * part
    activated = cotangent.shape if which else (2, TILE, part * TILE)
    return pl.pallas_call(
        functools.partial(middle_kernel, which),
        name="middle_%d" % which,
        out_shape=[
            jax.ShapeDtypeStruct(activated, jnp.float32),
            jax.ShapeDtypeStruct((rows, TILE, 2 * TILE), jnp.bfloat16),
            jax.ShapeDtypeStruct(weight.shape, jnp.float32),
        ],
        in_specs=[smem()] + [vmem()] * (6 + len(early)),
        out_specs=[vmem()] * 3,
        cost_estimate=cost(2),
        compiler_params=pltpu.CompilerParams(vmem_limit_bytes=VMEM_BYTES),
    )(bounds, across, weight, cotangent, kept, other, pairs, *early)


def ring_sum_kernel(which, bounds_ref, own_ref, one_ref, two_ref, three_ref, out_ref):
    refs = (own_ref, one_ref, two_ref, three_ref)
    for place in range(SIDE):

        @pl.when(bounds_ref[FIRST + which] == place)
        def _():
            parts = [refs[(index - place) % SIDE] for index in range(SIDE)]
            out_ref[...] = (parts[0][...] + parts[1][...]) + (parts[2][...] + parts[3][...])


def ring_sum(which, bounds, parts):
    return pl.pallas_call(
        functools.partial(ring_sum_kernel, which),
        name="ring_sum_%d" % which,
        out_shape=jax.ShapeDtypeStruct((TILE, TILE), jnp.float32),
        in_specs=[smem()] + [vmem()] * SIDE,
        out_specs=vmem(),
        compiler_params=pltpu.CompilerParams(vmem_limit_bytes=VMEM_BYTES),
    )(bounds, *parts)


def assemble_kernel(
    bounds_ref, own_ref, own_other_ref, across_ref, across_other_ref, term_ref, out_ref, sum_ref
):
    core, low = bounds_ref[CORE], bounds_ref[LOW]
    for source, chip, side in (
        (own_ref, low, core),
        (own_other_ref, low, 1 - core),
        (across_ref, 1 - low, core),
        (across_other_ref, 1 - low, 1 - core),
    ):
        for j in range(4):
            place = (chip * 2 + side) * 4 + j
            out_ref[:, pl.ds(pl.multiple_of(place * TILE, TILE), TILE)] = source[j]

    @pl.when(core == 0)
    def _():
        sum_ref[...] = term_ref[...]

    @pl.when(core == 1)
    def _():
        sum_ref[...] = own_other_ref[4]


def assemble(bounds, parts):
    return pl.pallas_call(
        assemble_kernel,
        name="assemble",
        out_shape=[
            jax.ShapeDtypeStruct((TILE, 16 * TILE), jnp.float32),
            jax.ShapeDtypeStruct((TILE, TILE), jnp.float32),
        ],
        in_specs=[smem()] + [vmem()] * 5,
        out_specs=[vmem()] * 2,
        compiler_params=pltpu.CompilerParams(vmem_limit_bytes=VMEM_BYTES),
    )(bounds, *parts)


def make_plan(rows, cols, count, loop, wide):
    core = loop % 2
    node_block = cols // 4
    across = (node_block // 16) ^ (wide // 16)
    dx = (node_block // 4 - wide // 4) % 4
    dz = (node_block - wide) % 4
    du = jnp.where(core == 0, dx, dz)
    dv = jnp.where(core == 0, dz, dx)
    place = jnp.where(dv == 2, 3, jnp.where(dv == 3, 2, dv))
    start = jnp.where(
        place < 3, (1 - across) * 48 + place * PER, 96 + across * PER
    )
    slots = start + du * 4 + cols % 4
    spots = jnp.arange(SLOTS, dtype=jnp.int32)
    kind = jnp.where(place < 3, 1 - across, 2 + across)
    kind = jnp.where(spots < count[0], kind, 4)
    ahead = (kind[None, :] < kind[:, None]) | (
        (kind[None, :] == kind[:, None]) & (spots[None, :] < spots[:, None])
    )
    rank = jnp.sum(ahead.astype(jnp.int32), axis=1)
    here = rank[None, :] == spots[:, None]

    def sort(values):
        return jnp.sum(jnp.where(here, values[None, :], 0), axis=1)

    inner = du * 4 + cols % 4
    back_slots = jnp.where(
        place < 3, slots, 96 + (inner // HALF) * PER + across * HALF + inner % HALF
    )
    steps = jnp.arange(9, dtype=jnp.int32)
    bounds = jnp.sum((kind[None, :] < steps[:, None]).astype(jnp.int32), axis=1)
    bounds = jnp.where(steps == CORE, loop % 2, jnp.where(steps == LOW, loop // 2, bounds))
    ring = jnp.where(core == 0, wide // 4 % 4, wide % 4)
    other_ring = jnp.where(core == 0, wide % 4, wide // 4 % 4)
    bounds = jnp.where(steps == FIRST, ring, jnp.where(steps == FIRST + 1, other_ring, bounds))
    return bounds, sort(spots), sort(rows), sort(slots), sort(back_slots)


def quarter_tiles(features, index):
    feats = features.shape[0]
    split = features.reshape(feats, 4, 4, TILE)
    piece = lax.dynamic_index_in_dim(split, index, 1, keepdims=False)
    return jnp.transpose(piece, (1, 2, 0))


def gather_own(features, loop):
    own = quarter_tiles(features, loop)
    one, three, two = permute(own, u_down), permute(own, u_up), permute(own, u_far)
    partner = permute(quarter_tiles(features, loop ^ 2), y_partner)
    return own, one, two, three, partner


def with_tile(value, tile):
    return jnp.concatenate([value, tile[None]], axis=0)


def add_part(value, part, start):
    size = part.shape[0]
    return lax.dynamic_update_slice_in_dim(value, value[start : start + size] + part, start, 0)


def scatter_terms(plan, pairs, spread, weight_term):
    back_plan = plan[:3] + plan[4:]
    up, down, spread = tie(*backward_part(0, back_plan, pairs, spread, (weight_term,)), spread)
    up, down = permute(up, v_up), permute(down, v_down)
    zero, one, three, own, own_one, own_three = backward_part(1, back_plan, pairs, spread)
    one = lax.dynamic_update_slice_in_dim(add_part(one, up[HALF:PER], 0), up[PER:], PER, 0)
    three = add_part(three, down[HALF:PER], HALF)
    one, three = permute(one, v_up), permute(three, v_down)
    own_one = permute(add_part(own_one, up[:HALF], 0), v_up)
    own_three = permute(add_part(own_three, down[:HALF], HALF), v_down)
    weight_term = ring_sum(1, plan[0], (weight_term, down[PER], one[PER], up[PER]))
    apart = zero + one[:PER] + three
    apart_two = permute(apart[8:12], u_far)
    far_one = permute(with_tile(apart[4:8], weight_term), y_far)
    far_three = permute(apart[12:16], y_far)
    last, far_three = tie(apart[:4] + apart_two, far_three)
    filler = apart[:2]
    last = permute(jnp.concatenate([last, filler], axis=0), y_far)[:4]
    weight_term = weight_term + far_one[4]
    total = own + own_one + own_three
    two = permute(with_tile(total[8:12], weight_term), u_far)
    one = permute(with_tile(total[4:8] + far_one[:4], weight_term), u_up)
    three = permute(with_tile(total[12:16] + far_three, weight_term), u_down)
    weight_term = ring_sum(0, plan[0], (weight_term, three[4], two[4], one[4]))
    return total[:4] + last + one[:4] + two[:4] + three[:4], weight_term


def per_device(features, weight, cotangent, tiles, tile_rows, tile_cols, counts):
    nrow = features.shape[1] // TILE
    loop = lax.axis_index(LOOP)
    wide = lax.axis_index(WIDE)
    tile_collection = tiles.reshape(SLOTS, TILE, TILE)
    count = counts.reshape(1)
    plan = make_plan(tile_rows.reshape(SLOTS), tile_cols.reshape(SLOTS), count, loop, wide)
    across = weight.T

    own, one, two, three, partner = gather_own(features, loop)
    first = jnp.concatenate([own, one], axis=0)
    second = jnp.concatenate([two, three], axis=0)
    plan, across, first, second, partner = tie(plan, across, first, second, partner)
    one_first, three_second = permute(first, v_down), permute(second, v_up)
    second_far = permute(second, y_far)
    one_second, three_first = permute(second, v_down), permute(first, v_up)
    count, one_first, partner = tie(count, one_first, partner)
    partner_one = permute(partner, u_down)
    pairs = pair_tiles(count, tile_collection)
    near = [first, second, one_first, one_second, three_first, three_second]
    far = [permute(one_first, v_down), permute(three_second, v_up)]
    first, second = jnp.concatenate([partner, partner_one], axis=0), second_far
    one_first, three_second = permute(first, v_down), permute(second, v_up)
    first, second, *far = tie(first, second, *far)
    one_second, three_first = permute(second, v_down), permute(first, v_up)
    partial = forward_part(0, plan[:4], pairs, near + far, None, nrow)
    one_first, three_second, partial = tie(one_first, three_second, partial[0])
    apart = [first, second, one_first, one_second, three_first, three_second]
    far = [permute(one_first, v_down), permute(three_second, v_up)]
    partial = forward_part(1, plan[:4], pairs, apart, partial, nrow)
    *kept, given_first, given_second = forward_part(2, plan[:4], pairs, far, partial[0], nrow)

    bounds = plan[0]
    kept = [kept[0] + permute(given_first, core_swap), kept[1] + permute(given_second, core_swap)]
    kept = [value + permute(value, y_pair) for value in kept]
    early = middle_part(
        0, bounds, across, weight, cotangent, kept[0], permute(kept[0], core_swap), pairs
    )
    activated, spread, weight_term = middle_part(
        1, bounds, across, weight, cotangent, kept[1], permute(kept[1], core_swap), pairs, early
    )
    total, weight_term = scatter_terms(plan, pairs, spread, weight_term)
    far_total = permute(total, y_pair)
    own_other = permute(with_tile(total, weight_term), core_swap)
    parts = [total, own_other, far_total, permute(far_total, core_swap), weight_term]
    return (activated, *assemble(bounds, parts))


def solution(mesh):
    split = jax.sharding.Mesh(mesh.devices.reshape(2, 2, 2, SIDE, SIDE), AXES)
    return jax.shard_map(
        per_device,
        mesh=split,
        in_specs=(
            P(None, WIDE),
            P(),
            P(None, WIDE),
            P(LOOP, WIDE, None, None, None),
            P(LOOP, WIDE, None),
            P(LOOP, WIDE, None),
            P(LOOP, WIDE),
        ),
        out_specs=(P(None, WIDE), P(None, WIDE), P()),
        check_vma=False,
    )
```

```python
import functools

import jax
import jax.numpy as jnp
from jax import lax
from jax.experimental import pallas as pl
from jax.experimental.pallas import tpu as pltpu
from jax.sharding import PartitionSpec as P

HI = lax.Precision.HIGHEST
GELU_SCALE = 0.7978845608028654
GELU_CUBE = 0.044715
AXES = ("y_lo", "core", "y_hi", "x", "z")
LOOP = ("y_lo", "core")
WIDE = ("y_hi", "x", "z")
SIDE = 4
TILE = 128
SLOTS = 256
GROUP = 16
CHUNK = 32
STAGES = 4
PAIR_BYTES = 30 * 1024 * 1024
PER = 16
HALF = 8
FORWARD = (
    (1, 3, 48, (HALF,) * 8),
    (0, 1, 0, (HALF,) * 6),
    (3, 4, 112, (HALF,) * 2),
)
BACKWARD = (
    (2, 4, 96, (PER, PER), (1, 1)),
    (0, 2, 0, (PER,) * 6, (0, 1, 0, 0, 0, 0)),
)
CORE = 5
LOW = 6
FIRST = 7
VMEM_BYTES = 8 * 1024 * 1024


def device_index(y, core, x, z):
    y, x, z = y % SIDE, x % SIDE, z % SIDE
    return (((y & 1) * 2 + core) * 2 + (y >> 1)) * 16 + x * SIDE + z


def permute(value, move):
    pairs = []
    for y in range(SIDE):
        for core in range(2):
            for x in range(SIDE):
                for z in range(SIDE):
                    pairs.append((device_index(y, core, x, z), device_index(*move(y, core, x, z))))
    return lax.ppermute(value, AXES, pairs)


def along(first, step):
    def move(y, core, x, z):
        if (core == 0) == first:
            return (y, core, x + step, z)
        return (y, core, x, z + step)

    return move


u_up, u_down, u_far = along(True, 1), along(True, -1), along(True, 2)
v_up, v_down = along(False, 1), along(False, -1)


def y_partner(y, core, x, z):
    return (3 - y, core, x, z)


def y_pair(y, core, x, z):
    return (y ^ 1, core, x, z)


def y_far(y, core, x, z):
    return (y + 2, core, x, z)


def core_swap(y, core, x, z):
    return (y, 1 - core, x, z)


def tie(*values):
    return lax.optimization_barrier(values)


def split_high_low(value):
    high = value.astype(jnp.bfloat16)
    low = (value - high.astype(jnp.float32)).astype(jnp.bfloat16)
    return high, low


def pair_kernel(count_ref, tiles_ref, out_ref, held, sems):
    count = count_ref[0]

    def copy(chunk):
        source = tiles_ref.at[pl.ds(chunk * CHUNK, CHUNK)]
        return pltpu.make_async_copy(source, held.at[chunk % STAGES], sems.at[chunk % STAGES])

    def when_live(chunk):
        return pl.when(chunk * CHUNK < count)

    for chunk in range(STAGES):
        when_live(chunk)(copy(chunk).start)
    for chunk in range(SLOTS // CHUNK):

        @when_live(chunk)
        def _():
            copy(chunk).wait()

            @pl.loop(0, CHUNK, unroll=8)
            def _(j):
                high, low = split_high_low(held[chunk % STAGES, j])
                out_ref[chunk * CHUNK + j, :, :TILE] = high
                out_ref[chunk * CHUNK + j, :, TILE:] = low

            if chunk + STAGES < SLOTS // CHUNK:
                when_live(chunk + STAGES)(copy(chunk + STAGES).start)


def pair_tiles(count, tiles):
    return pl.pallas_call(
        pair_kernel,
        name="pair_tiles",
        out_shape=pltpu.VMEM((SLOTS, TILE, 2 * TILE), jnp.bfloat16),
        in_specs=[smem(), anywhere()],
        out_specs=vmem(),
        scratch_shapes=[
            pltpu.VMEM((STAGES, CHUNK, TILE, TILE), jnp.float32),
            pltpu.SemaphoreType.DMA((STAGES,)),
        ],
        cost_estimate=cost(8),
        compiler_params=pltpu.CompilerParams(vmem_limit_bytes=PAIR_BYTES),
    )(count, tiles)


def class_range(bounds_ref, first, last):
    begin, end = bounds_ref[first], bounds_ref[last]
    return begin, end, (end - begin + GROUP - 1) // GROUP


def forward_kernel(which, bounds_ref, order_ref, rows_ref, slots_ref, tiles_ref, *rest):
    first, last, base, sizes = FORWARD[which]
    buffers = rest[: len(sizes)]
    rest = rest[len(sizes) :]
    prior_ref = rest[0] if which else None
    pairs, total = rest[-2:]
    nrow = total.shape[0] - 1
    begin, end, groups = class_range(bounds_ref, first, last)
    if which:
        total[0:nrow] = prior_ref[...]
    else:
        total[0:nrow] = jnp.zeros((nrow, TILE, TILE), jnp.float32)
    for index, size in enumerate(sizes):
        start = sum(sizes[:index])

        @pl.loop(0, size, unroll=4)
        def _(j):
            high, low = split_high_low(buffers[index][j])
            pairs[start + j, :, :TILE] = high
            pairs[start + j, :, TILE:] = low

    @pl.loop(0, groups)
    def _(group):
        for j in range(GROUP):
            spot = group * GROUP + j
            place = jnp.minimum(begin + spot, SLOTS - 1)
            live = begin + spot < end
            row = jnp.where(live, rows_ref[place], nrow)
            slot = jnp.where(live, slots_ref[place] - base, 0)
            right = pairs[slot]
            product = jnp.dot(
                tiles_ref[order_ref[place]],
                jnp.concatenate([right, right], axis=0),
                preferred_element_type=jnp.float32,
            )
            total[row] += product[:, :TILE] + product[:, TILE:]

    if which == len(FORWARD) - 1:
        core = bounds_ref[CORE]
        part = nrow // 4
        for index, out_ref in enumerate(rest[-6:-2]):
            side = core if index < 2 else 1 - core
            out_ref[...] = total[pl.ds((side * 2 + index % 2) * part, part)]
    else:
        rest[-3][...] = total[0:nrow]


def backward_kernel(which, bounds_ref, order_ref, rows_ref, slots_ref, tiles_ref, slope_ref, *rest):
    first, last, base, sizes, extra = BACKWARD[which]
    if which == 0:
        weight_term_ref, *rest = rest
    buffers = rest[: len(sizes)]
    total, out_sems, *rest = rest[len(sizes) :]
    if which == 0:
        (term_sems,) = rest
        term_copies = [
            pltpu.make_async_copy(weight_term_ref, buffer.at[PER], term_sems.at[index])
            for index, buffer in enumerate(buffers)
        ]
        for copy in term_copies:
            copy.start()
    begin, end, groups = class_range(bounds_ref, first, last)
    @pl.loop(0, sum(sizes), unroll=4)
    def _(slot):
        total[slot] = jnp.zeros((TILE, TILE), jnp.float32)

    @pl.loop(0, groups)
    def _(group):
        for j in range(GROUP):
            spot = group * GROUP + j
            place = jnp.minimum(begin + spot, SLOTS - 1)
            live = begin + spot < end
            slot = jnp.where(live, slots_ref[place] - base, sum(sizes))
            right = tiles_ref[order_ref[place]]
            product = jnp.dot(
                slope_ref[rows_ref[place]],
                jnp.concatenate([right, right], axis=0),
                preferred_element_type=jnp.float32,
            )
            total[slot] += product[:, :TILE] + product[:, TILE:]

    copies = []
    for index, size in enumerate(sizes):
        copy = pltpu.make_async_copy(
            total.at[pl.ds(sum(sizes[:index]), size)],
            buffers[index].at[pl.ds(0, size)],
            out_sems.at[index],
        )
        copy.start()
        copies.append(copy)
    if which == 0:
        copies += term_copies
    for copy in copies:
        copy.wait()


def smem():
    return pl.BlockSpec(memory_space=pltpu.SMEM)


def vmem():
    return pl.BlockSpec(memory_space=pltpu.VMEM)


def anywhere():
    return pl.BlockSpec(memory_space=pl.ANY)


def cost(microseconds):
    return pl.CostEstimate(
        flops=int(microseconds * 1.1e9), bytes_accessed=1 << 20, transcendentals=0
    )


def forward_part(which, plan, tiles, buffers, prior, nrow):
    extra = [prior] if which else []
    sizes = FORWARD[which][-1]
    out_shape = [jax.ShapeDtypeStruct((nrow, TILE, TILE), jnp.float32)]
    if which == len(FORWARD) - 1:
        out_shape = [jax.ShapeDtypeStruct((nrow // 4, TILE, TILE), jnp.float32)] * 4
    return pl.pallas_call(
        functools.partial(forward_kernel, which),
        name="forward_tiles_%d" % which,
        out_shape=out_shape,
        in_specs=[smem()] * 4 + [vmem()] * (1 + len(sizes) + len(extra)),
        out_specs=[vmem()] * len(out_shape),
        scratch_shapes=[
            pltpu.VMEM((sum(sizes), TILE, 2 * TILE), jnp.bfloat16),
            pltpu.VMEM((nrow + 1, TILE, TILE), jnp.float32),
        ],
        cost_estimate=cost((6, 5, 2)[which]),
        compiler_params=pltpu.CompilerParams(vmem_limit_bytes=VMEM_BYTES),
    )(*plan, tiles, *buffers, *extra)


def backward_part(which, plan, tiles, slope, weight_term=()):
    sizes, extra = BACKWARD[which][-2:]
    return pl.pallas_call(
        functools.partial(backward_kernel, which),
        name="backward_tiles_%d" % which,
        out_shape=[
            jax.ShapeDtypeStruct((size + more, TILE, TILE), jnp.float32)
            for size, more in zip(sizes, extra)
        ],
        in_specs=[smem()] * 4 + [vmem()] * (2 + len(weight_term)),
        out_specs=[anywhere()] * len(sizes),
        scratch_shapes=[
            pltpu.VMEM((sum(sizes) + 1, TILE, TILE), jnp.float32),
            pltpu.SemaphoreType.DMA((len(sizes),)),
        ]
        + [pltpu.SemaphoreType.DMA((2,))] * len(weight_term),
        cost_estimate=cost((3, 8)[which]),
        compiler_params=pltpu.CompilerParams(vmem_limit_bytes=VMEM_BYTES),
    )(*plan, tiles, slope, *weight_term)


def triple_left(value):
    high, low = split_high_low(value)
    return jnp.concatenate([high, low, high], axis=1)


def triple_right(value, axis):
    high, low = split_high_low(value)
    return jnp.concatenate([high, high, low], axis=axis)


def middle_kernel(which, bounds_ref, across_ref, weight_ref, cotangent_ref, *rest):
    kept_ref, other_ref = rest[0:2]
    core = bounds_ref[CORE]
    part = kept_ref.shape[0]
    across = triple_left(across_ref[...])
    weight = triple_left(weight_ref[...])
    if which == 0:
        activated_ref, spread_ref, weight_term_ref = rest[-3:]
        weight_term = jnp.zeros((TILE, TILE), jnp.float32)
    else:
        early_activated_ref, early_spread_ref, early_term_ref = rest[3:6]
        activated_ref, spread_ref, weight_term_ref = rest[-3:]
        weight_term = early_term_ref[...]
    for index, source in enumerate((kept_ref, other_ref)):
        side = core if index == 0 else 1 - core
        row = (side * 2 + which) * part
        columns = pl.ds(pl.multiple_of(row * TILE, part * TILE), part * TILE)
        block = source[...].reshape(part * TILE, TILE)
        value = lax.dot_general(
            across,
            triple_right(block, 1),
            (((1,), (1,)), ((), ())),
            preferred_element_type=jnp.float32,
        )
        square = value * value
        bend = jnp.tanh(GELU_SCALE * (value + GELU_CUBE * (square * value)))
        activated = 0.5 * value * (1.0 + bend)
        rate = 0.5 * (1.0 + bend) + 0.5 * value * (1.0 - bend * bend) * (
            GELU_SCALE * (1.0 + 3.0 * GELU_CUBE * square)
        )
        slope = cotangent_ref[:, columns] * rate
        weight_term += jnp.dot(
            triple_left(slope), triple_right(block, 0), preferred_element_type=jnp.float32
        )
        spread = jnp.dot(weight, triple_right(slope, 0), preferred_element_type=jnp.float32)
        high, low = split_high_low(spread)
        place = index * part if which == 0 else row
        for j in range(part):
            spread_ref[place + j, :, :TILE] = high[:, j * TILE : (j + 1) * TILE]
            spread_ref[place + j, :, TILE:] = low[:, j * TILE : (j + 1) * TILE]
        if which == 0:
            activated_ref[index] = activated
        else:
            activated_ref[:, columns] = activated
            early = side * 2 * part
            early_columns = pl.ds(pl.multiple_of(early * TILE, part * TILE), part * TILE)
            activated_ref[:, early_columns] = early_activated_ref[index]
            spread_ref[pl.ds(early, part)] = early_spread_ref[index * part : (index + 1) * part]
    weight_term_ref[...] = jnp.transpose(weight_term) if which else weight_term


def middle_part(which, bounds, across, weight, cotangent, kept, other, pairs, early=()):
    part = kept.shape[0]
    rows = 4 * part if which else 2 * part
    activated = cotangent.shape if which else (2, TILE, part * TILE)
    return pl.pallas_call(
        functools.partial(middle_kernel, which),
        name="middle_%d" % which,
        out_shape=[
            jax.ShapeDtypeStruct(activated, jnp.float32),
            jax.ShapeDtypeStruct((rows, TILE, 2 * TILE), jnp.bfloat16),
            jax.ShapeDtypeStruct(weight.shape, jnp.float32),
        ],
        in_specs=[smem()] + [vmem()] * (6 + len(early)),
        out_specs=[vmem()] * 3,
        cost_estimate=cost(2),
        compiler_params=pltpu.CompilerParams(vmem_limit_bytes=VMEM_BYTES),
    )(bounds, across, weight, cotangent, kept, other, pairs, *early)


def ring_sum_kernel(which, bounds_ref, own_ref, one_ref, two_ref, three_ref, out_ref):
    refs = (own_ref, one_ref, two_ref, three_ref)
    for place in range(SIDE):

        @pl.when(bounds_ref[FIRST + which] == place)
        def _():
            parts = [refs[(index - place) % SIDE] for index in range(SIDE)]
            out_ref[...] = (parts[0][...] + parts[1][...]) + (parts[2][...] + parts[3][...])


def ring_sum(which, bounds, parts):
    return pl.pallas_call(
        functools.partial(ring_sum_kernel, which),
        name="ring_sum_%d" % which,
        out_shape=jax.ShapeDtypeStruct((TILE, TILE), jnp.float32),
        in_specs=[smem()] + [vmem()] * SIDE,
        out_specs=vmem(),
        compiler_params=pltpu.CompilerParams(vmem_limit_bytes=VMEM_BYTES),
    )(bounds, *parts)


def assemble_kernel(
    bounds_ref, own_ref, own_other_ref, across_ref, across_other_ref, term_ref, out_ref, sum_ref
):
    core, low = bounds_ref[CORE], bounds_ref[LOW]
    for source, chip, side in (
        (own_ref, low, core),
        (own_other_ref, low, 1 - core),
        (across_ref, 1 - low, core),
        (across_other_ref, 1 - low, 1 - core),
    ):
        for j in range(4):
            place = (chip * 2 + side) * 4 + j
            out_ref[:, pl.ds(pl.multiple_of(place * TILE, TILE), TILE)] = source[j]

    @pl.when(core == 0)
    def _():
        sum_ref[...] = term_ref[...]

    @pl.when(core == 1)
    def _():
        sum_ref[...] = own_other_ref[4]


def assemble(bounds, parts):
    return pl.pallas_call(
        assemble_kernel,
        name="assemble",
        out_shape=[
            jax.ShapeDtypeStruct((TILE, 16 * TILE), jnp.float32),
            jax.ShapeDtypeStruct((TILE, TILE), jnp.float32),
        ],
        in_specs=[smem()] + [vmem()] * 5,
        out_specs=[vmem()] * 2,
        compiler_params=pltpu.CompilerParams(vmem_limit_bytes=VMEM_BYTES),
    )(bounds, *parts)


def make_plan(rows, cols, count, loop, wide):
    core = loop % 2
    node_block = cols // 4
    across = (node_block // 16) ^ (wide // 16)
    dx = (node_block // 4 - wide // 4) % 4
    dz = (node_block - wide) % 4
    du = jnp.where(core == 0, dx, dz)
    dv = jnp.where(core == 0, dz, dx)
    place = jnp.where(dv == 2, 3, jnp.where(dv == 3, 2, dv))
    start = jnp.where(
        place < 3, (1 - across) * 48 + place * PER, 96 + across * PER
    )
    slots = start + du * 4 + cols % 4
    spots = jnp.arange(SLOTS, dtype=jnp.int32)
    kind = jnp.where(place < 3, 1 - across, 2 + across)
    kind = jnp.where(spots < count[0], kind, 4)
    ahead = (kind[None, :] < kind[:, None]) | (
        (kind[None, :] == kind[:, None]) & (spots[None, :] < spots[:, None])
    )
    rank = jnp.sum(ahead.astype(jnp.int32), axis=1)
    here = rank[None, :] == spots[:, None]

    def sort(values):
        return jnp.sum(jnp.where(here, values[None, :], 0), axis=1)

    inner = du * 4 + cols % 4
    back_slots = jnp.where(
        place < 3, slots, 96 + (inner // HALF) * PER + across * HALF + inner % HALF
    )
    steps = jnp.arange(9, dtype=jnp.int32)
    bounds = jnp.sum((kind[None, :] < steps[:, None]).astype(jnp.int32), axis=1)
    bounds = jnp.where(steps == CORE, loop % 2, jnp.where(steps == LOW, loop // 2, bounds))
    ring = jnp.where(core == 0, wide // 4 % 4, wide % 4)
    other_ring = jnp.where(core == 0, wide % 4, wide // 4 % 4)
    bounds = jnp.where(steps == FIRST, ring, jnp.where(steps == FIRST + 1, other_ring, bounds))
    return bounds, sort(spots), sort(rows), sort(slots), sort(back_slots)


def quarter_tiles(features, index):
    feats = features.shape[0]
    split = features.reshape(feats, 4, 4, TILE)
    piece = lax.dynamic_index_in_dim(split, index, 1, keepdims=False)
    return jnp.transpose(piece, (1, 2, 0))


def gather_own(features, loop):
    own = quarter_tiles(features, loop)
    one, three, two = permute(own, u_down), permute(own, u_up), permute(own, u_far)
    partner = permute(quarter_tiles(features, loop ^ 2), y_partner)
    return own, one, two, three, partner


def with_tile(value, tile):
    return jnp.concatenate([value, tile[None]], axis=0)


def add_part(value, part, start):
    size = part.shape[0]
    return lax.dynamic_update_slice_in_dim(value, value[start : start + size] + part, start, 0)


def scatter_terms(plan, pairs, spread, weight_term):
    back_plan = plan[:3] + plan[4:]
    up, down, spread = tie(*backward_part(0, back_plan, pairs, spread, (weight_term,)), spread)
    up, down = permute(up, v_up), permute(down, v_down)
    zero, one, three, own, own_one, own_three = backward_part(1, back_plan, pairs, spread)
    one = lax.dynamic_update_slice_in_dim(add_part(one, up[HALF:PER], 0), up[PER:], PER, 0)
    three = add_part(three, down[HALF:PER], HALF)
    one, three = permute(one, v_up), permute(three, v_down)
    own_one = permute(add_part(own_one, up[:HALF], 0), v_up)
    own_three = permute(add_part(own_three, down[:HALF], HALF), v_down)
    weight_term = ring_sum(1, plan[0], (weight_term, down[PER], one[PER], up[PER]))
    apart = zero + one[:PER] + three
    apart_two = permute(apart[8:12], u_far)
    apart_far = permute(
        jnp.concatenate([apart[4:8], apart[12:16], weight_term[None]], axis=0), y_far
    )
    last, apart_far = tie(apart[:4] + apart_two, apart_far)
    last = permute(last, y_far)
    weight_term = weight_term + apart_far[8]
    total = own + own_one + own_three
    two = permute(with_tile(total[8:12], weight_term), u_far)
    one = permute(with_tile(total[4:8] + apart_far[:4], weight_term), u_up)
    three = permute(with_tile(total[12:16] + apart_far[4:8], weight_term), u_down)
    weight_term = ring_sum(0, plan[0], (weight_term, three[4], two[4], one[4]))
    return total[:4] + last + one[:4] + two[:4] + three[:4], weight_term


def per_device(features, weight, cotangent, tiles, tile_rows, tile_cols, counts):
    nrow = features.shape[1] // TILE
    loop = lax.axis_index(LOOP)
    wide = lax.axis_index(WIDE)
    tile_collection = tiles.reshape(SLOTS, TILE, TILE)
    count = counts.reshape(1)
    plan = make_plan(tile_rows.reshape(SLOTS), tile_cols.reshape(SLOTS), count, loop, wide)
    across = weight.T

    own, one, two, three, partner = gather_own(features, loop)
    first = jnp.concatenate([own, one], axis=0)
    second = jnp.concatenate([two, three], axis=0)
    plan, across, first, second, partner = tie(plan, across, first, second, partner)
    one_first, three_second = permute(first, v_down), permute(second, v_up)
    second_far = permute(second, y_far)
    one_second, three_first = permute(second, v_down), permute(first, v_up)
    partner_one = permute(partner, u_down)
    count, one_first, partner_one = tie(count, one_first, partner_one)
    pairs = pair_tiles(count, tile_collection)
    near = [first, second, one_first, one_second, three_first, three_second]
    far = [permute(one_first, v_down), permute(three_second, v_up)]
    first, second = jnp.concatenate([partner, partner_one], axis=0), second_far
    one_first, three_second = permute(first, v_down), permute(second, v_up)
    first, second, *far = tie(first, second, *far)
    one_second, three_first = permute(second, v_down), permute(first, v_up)
    partial = forward_part(0, plan[:4], pairs, near + far, None, nrow)
    one_first, three_second, partial = tie(one_first, three_second, partial[0])
    apart = [first, second, one_first, one_second, three_first, three_second]
    far = [permute(one_first, v_down), permute(three_second, v_up)]
    partial = forward_part(1, plan[:4], pairs, apart, partial, nrow)
    *kept, given_first, given_second = forward_part(2, plan[:4], pairs, far, partial[0], nrow)

    bounds = plan[0]
    kept = [kept[0] + permute(given_first, core_swap), kept[1] + permute(given_second, core_swap)]
    kept = [value + permute(value, y_pair) for value in kept]
    early = middle_part(
        0, bounds, across, weight, cotangent, kept[0], permute(kept[0], core_swap), pairs
    )
    activated, spread, weight_term = middle_part(
        1, bounds, across, weight, cotangent, kept[1], permute(kept[1], core_swap), pairs, early
    )
    total, weight_term = scatter_terms(plan, pairs, spread, weight_term)
    far_total = permute(total, y_pair)
    own_other = permute(with_tile(total, weight_term), core_swap)
    parts = [total, own_other, far_total, permute(far_total, core_swap), weight_term]
    return (activated, *assemble(bounds, parts))


def solution(mesh):
    split = jax.sharding.Mesh(mesh.devices.reshape(2, 2, 2, SIDE, SIDE), AXES)
    return jax.shard_map(
        per_device,
        mesh=split,
        in_specs=(
            P(None, WIDE),
            P(),
            P(None, WIDE),
            P(LOOP, WIDE, None, None, None),
            P(LOOP, WIDE, None),
            P(LOOP, WIDE, None),
            P(LOOP, WIDE),
        ),
        out_specs=(P(None, WIDE), P(None, WIDE), P()),
        check_vma=False,
    )
```
